32 devices in a mesh: dp: 4 (over y, x), expert: 8 (over z, core).
Axes of the slice: x: 2, y: 2, z: 4, core: 2. Of those that a mesh axis runs over, the one named last changes fastest.
Arguments:
- tokens: bfloat16 [32768, 768], P(('dp', 'expert')), may hold values from -6 to 6
- expert_ids: int32 [32768, 1], P(('dp', 'expert')), may hold values from 0 to 15
- bucket_ids: int32 [512, 512], replicated, may hold values from 0 to 31
- attn_gain: float32 [768], replicated, may hold values from 0.5 to 1.5
- ffn_gain: float32 [768], replicated, may hold values from 0.5 to 1.5
- query_weight: bfloat16 [768, 768], replicated, may hold values from -0.21875 to 0.21875
- key_weight: bfloat16 [768, 768], replicated, may hold values from -0.21875 to 0.21875
- value_weight: bfloat16 [768, 768], replicated, may hold values from -0.21875 to 0.21875
- output_weight: bfloat16 [768, 768], replicated, may hold values from -1.75 to 1.75
- router_weight: bfloat16 [768, 16], replicated, may hold values from -0.25 to 0.25
- bucket_bias: float32 [32, 12], replicated, may hold values from -6 to 6
- expert_in: bfloat16 [16, 768, 3072], P('expert'), may hold values from -0.21875 to 0.21875
- expert_out: bfloat16 [16, 3072, 768], P('expert'), may hold values from -6 to 6
- grad_output: bfloat16 [32768, 768], P(('dp', 'expert')), may hold values from -6 to 6
Outputs:
- mixed: bfloat16 [32768, 768], P(('dp', 'expert'))
- grad_tokens: float32 [32768, 768], P(('dp', 'expert'))
- grad_attn_gain: float32 [768], replicated
- grad_ffn_gain: float32 [768], replicated
- grad_query_weight: float32 [768, 768], replicated
- grad_key_weight: float32 [768, 768], replicated
- grad_value_weight: float32 [768, 768], replicated
- grad_output_weight: float32 [768, 768], replicated
- grad_router_weight: float32 [768, 16], replicated
- grad_bucket_bias: float32 [32, 12], replicated
- grad_expert_in: float32 [16, 768, 3072], P('expert', None, 'dp')
- grad_expert_out: float32 [16, 3072, 768], P('expert', 'dp')
The draws below stay inside these ranges and needn't reach their ends.
All inputs are finite; a program needn't handle non-finite values.
Results may differ from the reference program's by a relative error of at most 0.015.
Values may be sent and summed in bfloat16 or wider, within the bound.
A program may use at most 256 MiB of HBM per device.

```python
import jax
import jax.numpy as jnp
from jax import lax

D = 768
HEADS = 12
HEAD_DIM = 64
FF = 3072
BUCKETS = 32
SEQ_LEN = 512
SEQS = 2
EXPERTS = 16
TOK_DEV = 1024
TOKENS = 32768
CAP = 80
N_DP = 4
N_EXPERT = 8


def place_ends(entries, rng, least, top_value):
    longest = entries.shape.index(max(entries.shape))
    spots = []
    for shift in (0, 1):
        where = [jax.random.randint(jax.random.fold_in(rng, axis), (), 0, length) for axis, length in enumerate(entries.shape)]
        where[longest] = (where[longest] + shift) % entries.shape[longest]
        spots.append(tuple(where))
    return entries.at[spots[0]].set(least).at[spots[1]].set(top_value)


def steps_of(own_key, shape, split, low, high):
    gain, own = 1.0, jax.random.fold_in(own_key, 6)
    for axis_at, parts in split:
        draws = jnp.exp(jax.random.uniform(jax.random.fold_in(own, axis_at), (parts,), jnp.float32, low / len(split), high / len(split)))
        gain = gain * jnp.repeat(draws, shape[axis_at] // parts).reshape([-1 if axis == axis_at else 1 for axis in range(len(shape))])
    return gain


def choose_distinct(rng, rows, count, top, lift):
    ranking = jax.random.permutation(jax.random.fold_in(rng, 1), count)
    favour = ranking
    for power in range(3):
        favour = favour * favour // count
    favour = favour * lift // count
    chance = jax.random.randint(jax.random.fold_in(rng, 2), (rows, count), 0, 4096) + favour
    fixed_rows = jax.random.permutation(jax.random.fold_in(rng, 3), rows)[jnp.arange(count) % rows]
    chance = jnp.where(jnp.arange(rows)[:, None] == fixed_rows[None, :], 1 << 14, chance)
    priority = chance * count + jnp.arange(count)
    return lax.top_k(priority.astype(jnp.int32), top)[1].astype(jnp.int32)


def gaussian(key, shape, scale, most, pieces=(), kind=jnp.bfloat16):
    entries = scale * jax.random.normal(key, shape, jnp.float32)
    if pieces:
        entries = entries * steps_of(key, shape, pieces, -0.22, 0.18)
    return jnp.clip(entries, -most, most).astype(kind)


def setup_inputs(seed: int = 0) -> dict:
    splits = jax.random.split(jax.random.key(seed), 15)
    return {
        "tokens": gaussian(splits[0], (TOKENS, D), 1.0, 6.0, ((0, 32),)),
        "expert_ids": choose_distinct(splits[1], TOKENS, EXPERTS, 1, 1024),
        "bucket_ids": place_ends(jax.random.randint(splits[2], (SEQ_LEN, SEQ_LEN), 0, BUCKETS), jax.random.fold_in(splits[2], 1), 0, BUCKETS - 1).astype(jnp.int32),
        "attn_gain": jnp.clip(1.0 + 0.1 * jax.random.normal(splits[3], (D,), jnp.float32), 0.5, 1.5),
        "ffn_gain": jnp.clip(1.0 + 0.1 * jax.random.normal(splits[4], (D,), jnp.float32), 0.5, 1.5),
        "query_weight": gaussian(splits[5], (D, D), D ** -0.5, 0.21875),
        "key_weight": gaussian(splits[6], (D, D), D ** -0.5, 0.21875),
        "value_weight": gaussian(splits[7], (D, D), D ** -0.5, 0.21875),
        "output_weight": gaussian(splits[8], (D, D), (D // 64) ** -0.5, 1.75),
        "router_weight": gaussian(splits[9], (D, EXPERTS), (0.5 * D ** -0.5), 0.25),
        "bucket_bias": gaussian(splits[10], (BUCKETS, HEADS), 1.0, 6.0, (), jnp.float32),
        "expert_in": gaussian(splits[11], (EXPERTS, D, FF), D ** -0.5, 0.21875, ((0, 8),)),
        "expert_out": gaussian(splits[12], (EXPERTS, FF, D), (2.0 * EXPERTS * FF ** -0.5), 6.0, ((0, 8),)),
        "grad_output": gaussian(splits[13], (TOKENS, D), 1.0, 6.0, ((0, 32),)),
    }


@jax.custom_vjp
def low(v):
    return lax.optimization_barrier(v.astype(jnp.bfloat16)).astype(jnp.float32)

@jax.custom_vjp
def low_back(v):
    return v

def low_keep(v):
    return (low(v), None)

def low_pass(kept, grad):
    return (grad,)

def back_keep(v):
    return (v, None)

def back_low(kept, grad):
    return (low(grad),)
low.defvjp(low_keep, low_pass)
low_back.defvjp(back_keep, back_low)
HIGHEST = lax.Precision.HIGHEST
EPSILON = 1e-06

def matmul(left, right):
    return jnp.dot(left, right, precision=HIGHEST, preferred_element_type=jnp.float32)

def round_both(values):
    return low_back(low(values))

def rms_norm(values, gain_row):
    return values * lax.rsqrt(lax.optimization_barrier(jnp.mean(values * values, axis=-1, keepdims=True)) + EPSILON) * gain_row

def slot_tokens(expert_of):
    device_count = N_DP * N_EXPERT
    grouped = expert_of.reshape(device_count, TOK_DEV)
    offsets = jnp.arange(device_count, dtype=jnp.int32) * TOK_DEV
    numbers = jnp.arange(EXPERTS, dtype=jnp.int32)

    def one_device(inputs):
        own_ids, offset_row = inputs
        one_hot = (own_ids[:, None] == numbers[None, :]).astype(jnp.int32)
        position = lax.optimization_barrier(jnp.sum(jnp.cumsum(one_hot, axis=0) * one_hot, axis=1)) - 1
        slot_of = jnp.where(position < CAP, own_ids * CAP + position, EXPERTS * CAP)
        row_ids = offset_row + jnp.arange(TOK_DEV, dtype=jnp.int32)
        return jnp.full((EXPERTS * CAP,), TOKENS, jnp.int32).at[slot_of].set(row_ids, mode='drop')
    tables = lax.map(one_device, (grouped, offsets))
    tables = tables.reshape(device_count, EXPERTS, CAP).transpose(1, 0, 2)
    return tables.reshape(EXPERTS, device_count * CAP)

def layer_forward(token_rows, attn_gain, ffn_gain, query_weight, key_weight, value_weight, output_weight, router_weight, bucket_bias, expert_in, expert_out, slot_token, one_hot, bucket_ids):
    device_count = N_DP * N_EXPERT
    normed = low(rms_norm(token_rows, attn_gain))
    query_rows = round_both(matmul(normed, query_weight))
    key_rows = round_both(matmul(normed, key_weight))
    value_rows = round_both(matmul(normed, value_weight))
    position_bias = jnp.transpose(bucket_bias[bucket_ids], (2, 0, 1))
    shape_four = (SEQS, SEQ_LEN, HEADS, HEAD_DIM)

    def attend(group):
        query_dev, key_dev, value_dev = group
        raw_scores = jnp.einsum('sqhd,skhd->shqk', query_dev.reshape(shape_four), key_dev.reshape(shape_four), precision=HIGHEST)
        scores = low_back(raw_scores * 0.125 + position_bias[None])
        weights = low(jax.nn.softmax(scores, axis=-1))
        heads_out = jnp.einsum('shqk,skhd->sqhd', weights, value_dev.reshape(shape_four), precision=HIGHEST)
        return heads_out.reshape(TOK_DEV, D)

    def by_device(values):
        return values.reshape(device_count, TOK_DEV, D)
    attended = lax.map(jax.checkpoint(attend), (by_device(query_rows), by_device(key_rows), by_device(value_rows)))
    attended = round_both(attended.reshape(TOKENS, D))
    residual = token_rows + low_back(matmul(attended, output_weight))
    normed_ffn = low(rms_norm(residual, ffn_gain))
    logits = low_back(matmul(normed_ffn, router_weight))
    router_probs = jax.nn.softmax(logits, axis=-1)
    gate_prob = lax.optimization_barrier(jnp.sum(router_probs * one_hot, axis=1))
    padded = jnp.concatenate([normed_ffn, jnp.zeros((1, D), jnp.float32)], axis=0)
    dispatched = low_back(padded[slot_token])

    def expert(inputs):
        rows_in, weight_in, weight_out = inputs
        pre_act = low_back(matmul(rows_in, weight_in))
        hidden = low(jax.nn.gelu(pre_act))
        return round_both(matmul(hidden, weight_out))
    returned = lax.map(jax.checkpoint(expert), (dispatched, expert_in, expert_out))
    combined = jnp.zeros((TOKENS + 1, D), jnp.float32).at[slot_token.reshape(-1)].add(returned.reshape(-1, D))
    return residual + gate_prob[:, None] * combined[:TOKENS]

def reference(tokens, expert_ids, bucket_ids, attn_gain, ffn_gain, query_weight, key_weight, value_weight, output_weight, router_weight, bucket_bias, expert_in, expert_out, grad_output):
    expert_of = expert_ids[:, 0]
    slot_token = slot_tokens(expert_of)
    one_hot = (expert_of[:, None] == jnp.arange(EXPERTS, dtype=jnp.int32)[None, :]).astype(jnp.float32)

    def forward(token_rows, gain_one, gain_two, weight_query, weight_key, weight_value, weight_output, weight_router, bias_table, weight_in, weight_out):
        return layer_forward(token_rows, gain_one, gain_two, weight_query, weight_key, weight_value, weight_output, weight_router, bias_table, weight_in, weight_out, slot_token, one_hot, bucket_ids)
    params = (tokens.astype(jnp.float32), attn_gain, ffn_gain, query_weight.astype(jnp.float32), key_weight.astype(jnp.float32), value_weight.astype(jnp.float32), output_weight.astype(jnp.float32), router_weight.astype(jnp.float32), bucket_bias, expert_in.astype(jnp.float32), expert_out.astype(jnp.float32))
    mixed, pull_back = jax.vjp(forward, *params)
    grads = pull_back(grad_output.astype(jnp.float32))
    return (mixed.astype(jnp.bfloat16), grads[0], grads[1], grads[2], grads[3], grads[4], grads[5], grads[6], grads[7], grads[8], grads[9], grads[10])
```

```python
import functools

import jax
import jax.numpy as jnp
from jax import lax
from jax.experimental import pallas as pl
from jax.experimental.pallas import tpu as pltpu
from jax.sharding import PartitionSpec as P

EPSILON = 1e-06
BF = jnp.bfloat16
F32 = jnp.float32
LANES = 128
VMEM_BYTES = 60 * 1024 * 1024


def dot_nn(left, right):
    return lax.dot_general(left, right, (((1,), (0,)), ((), ())), preferred_element_type=F32)


def dot_nt(left, right):
    return lax.dot_general(left, right, (((1,), (1,)), ((), ())), preferred_element_type=F32)


def dot_tn(left, right):
    return lax.dot_general(left, right, (((0,), (0,)), ((), ())), preferred_element_type=F32)


def iota(shape, axis):
    return lax.broadcasted_iota(jnp.int32, shape, axis)


def whole(shape):
    return pl.BlockSpec(shape, lambda *_: (0,) * len(shape))


def params(**more):
    return pltpu.CompilerParams(vmem_limit_bytes=VMEM_BYTES, **more)


def slots_kernel(ranks, local, cap, ids_col, ids_row, grad, slot_col, slot_row, slot_grads):
    rows = grad.shape[0]
    experts = ranks * local
    first = iota((rows, rows), 0)
    second = iota((rows, rows), 1)

    def place_of(ids, hot, counts, axis):
        place = jnp.sum(jnp.where(hot, counts, 0.0), axis=axis, keepdims=True).astype(jnp.int32)
        rank = jnp.floor((ids.astype(F32) + 0.5) * (1.0 / local)).astype(jnp.int32)
        base = ((ids - rank * local) * ranks + rank) * cap
        return jnp.where(place < cap, base + place, -1)

    hot_col = ids_col[...] == iota((rows, experts), 1)
    counts_col = dot_nn((second < first).astype(BF), hot_col.astype(BF))
    slot_col[...] = place_of(ids_col[...], hot_col, counts_col, 1)
    hot_row = ids_row[...] == iota((experts, rows), 0)
    counts_row = dot_nn(hot_row.astype(BF), (first < second).astype(BF))
    slot_row[...] = place_of(ids_row[...], hot_row, counts_row, 0)
    pick = (iota((experts * cap, rows), 0) == slot_row[...]).astype(BF)
    slot_grads[...] = dot_nn(pick, grad[...]).astype(BF)


def make_slots(ranks, local, cap, expert_ids, grad_output):
    rows, width = grad_output.shape
    slots = ranks * local * cap
    return pl.pallas_call(
        functools.partial(slots_kernel, ranks, local, cap),
        out_shape=(
            jax.ShapeDtypeStruct((rows, 1), jnp.int32),
            jax.ShapeDtypeStruct((1, rows), jnp.int32),
            jax.ShapeDtypeStruct((slots, width), BF),
        ),
        compiler_params=params(),
        name="slots",
    )(expert_ids, expert_ids.reshape(1, rows), grad_output)


def forward_kernel(
    head_dim, seq_len,
    tokens, ids, table, gain_one, gain_two, wq, wk, wv, wo, wr, ids_col, slot_row,
    normed_o, q_o, k_o, v_o, att_o, inv_o, soft_o, residual_o, nf_o, gate_o, slots_o,
):
    step = pl.program_id(0)
    rows, width = tokens.shape
    group = wq.shape[1]

    @pl.when(step == 0)
    def _():
        x = tokens[...].astype(F32)
        factor = lax.rsqrt(jnp.mean(x * x, axis=-1, keepdims=True) + EPSILON)
        normed_o[...] = (x * factor * gain_one[...]).astype(BF)
        residual_o[...] = x

    normed = normed_o[...]
    q_o[...] = dot_nn(normed, wq[...]).astype(BF)
    k_o[...] = dot_nn(normed, wk[...]).astype(BF)
    v_o[...] = dot_nn(normed, wv[...]).astype(BF)
    lane = iota((seq_len, LANES), 1)
    per_tile = LANES // head_dim
    for tile in range(group // LANES):
        cols = slice(tile * LANES, (tile + 1) * LANES)
        gathered = [None] * (rows // seq_len)
        scaled = [None] * (rows // seq_len)
        for part in range(per_tile):
            head = tile * per_tile + part
            mine = (lane >= part * head_dim) & (lane < (part + 1) * head_dim)
            row = jnp.broadcast_to(table[0, head:head + 1, :], (seq_len, LANES))
            bias = jnp.concatenate(
                [
                    jnp.take_along_axis(
                        row, ids[:, c:c + LANES], axis=1, mode="promise_in_bounds"
                    )
                    for c in range(0, seq_len, LANES)
                ],
                axis=1,
            )
            for seq in range(rows // seq_len):
                span = slice(seq * seq_len, (seq + 1) * seq_len)
                query = jnp.where(mine, q_o[span, cols] * 0.125, 0).astype(BF)
                scores = dot_nt(query, k_o[span, cols]) + bias
                weights = jnp.exp(scores - jnp.max(scores, axis=-1, keepdims=True))
                inverse = 1.0 / jnp.sum(weights, axis=-1, keepdims=True)
                low = weights.astype(BF)
                soft_o[head, seq] = low
                out = dot_nn(low, v_o[span, cols]) * inverse
                inverse = jnp.broadcast_to(inverse, (seq_len, LANES))
                if part == 0:
                    gathered[seq], scaled[seq] = out, inverse
                else:
                    gathered[seq] = jnp.where(mine, out, gathered[seq])
                    scaled[seq] = jnp.where(mine, inverse, scaled[seq])
        for seq in range(rows // seq_len):
            span = slice(seq * seq_len, (seq + 1) * seq_len)
            att_o[span, cols] = gathered[seq].astype(BF)
            inv_o[span, cols] = scaled[seq]
    residual_o[...] += dot_nn(att_o[...], wo[...])

    @pl.when(step == pl.num_programs(0) - 1)
    def _():
        residual = residual_o[...]
        factor = lax.rsqrt(jnp.mean(residual * residual, axis=-1, keepdims=True) + EPSILON)
        low = (residual * factor * gain_two[...]).astype(BF)
        nf_o[...] = low
        logits = dot_nn(low, wr[...])
        weights = jnp.exp(logits - jnp.max(logits, axis=-1, keepdims=True))
        probs = weights / jnp.sum(weights, axis=-1, keepdims=True)
        hot = ids_col[...] == iota(logits.shape, 1)
        gate_o[...] = jnp.sum(jnp.where(hot, probs, 0.0), axis=1, keepdims=True)
        pick = (iota((slots_o.shape[0], rows), 0) == slot_row[...]).astype(BF)
        slots_o[...] = dot_nn(pick, low).astype(BF)


def forward(tokens, bucket_ids, table, gains, weights, wr, expert_ids, slot_row, slots, head_dim):
    rows, width = tokens.shape
    seq_len = bucket_ids.shape[0]
    groups, per_group, _ = table.shape
    group = width // groups
    heads = groups * per_group
    seqs = rows // seq_len
    cols = lambda shape: pl.BlockSpec(shape, lambda g: (0, g))
    wq, wk, wv, wo = weights
    return pl.pallas_call(
        functools.partial(forward_kernel, head_dim, seq_len),
        grid=(groups,),
        in_specs=[
            whole((rows, width)),
            whole((seq_len, seq_len)),
            pl.BlockSpec((1, per_group, LANES), lambda g: (g, 0, 0)),
            whole((1, width)),
            whole((1, width)),
            cols((width, group)),
            cols((width, group)),
            cols((width, group)),
            pl.BlockSpec((group, width), lambda g: (g, 0)),
            whole(wr.shape),
            whole((rows, 1)),
            whole((1, rows)),
        ],
        out_specs=(
            whole((rows, width)),
            cols((rows, group)),
            cols((rows, group)),
            cols((rows, group)),
            cols((rows, group)),
            cols((rows, group)),
            pl.BlockSpec((per_group, seqs, seq_len, seq_len), lambda g: (g, 0, 0, 0)),
            whole((rows, width)),
            whole((rows, width)),
            whole((rows, 1)),
            whole((slots, width)),
        ),
        out_shape=(
            jax.ShapeDtypeStruct((rows, width), BF),
            jax.ShapeDtypeStruct((rows, width), BF),
            jax.ShapeDtypeStruct((rows, width), BF),
            jax.ShapeDtypeStruct((rows, width), BF),
            jax.ShapeDtypeStruct((rows, width), BF),
            jax.ShapeDtypeStruct((rows, width), F32),
            jax.ShapeDtypeStruct((heads, seqs, seq_len, seq_len), BF),
            jax.ShapeDtypeStruct((rows, width), F32),
            jax.ShapeDtypeStruct((rows, width), BF),
            jax.ShapeDtypeStruct((rows, 1), F32),
            jax.ShapeDtypeStruct((slots, width), BF),
        ),
        compiler_params=params(dimension_semantics=("arbitrary",)),
        cost_estimate=pl.CostEstimate(
            flops=2 * rows * width * (4 * width + 2 * seq_len * 4),
            bytes_accessed=40 << 20,
            transcendentals=heads * rows * seq_len,
        ),
        name="forward",
    )(tokens, bucket_ids, table, *gains, wq, wk, wv, wo, wr, expert_ids, slot_row)


def expert_kernel(
    order, which, rows_in, grads_in, weight_in, weight_out, wr,
    returned_o, back_o, router_o, grad_in_o, grad_out_o,
    scaled, probs_s, back_sum, result_sum,
):
    step = pl.program_id(0)

    @pl.when(step == 0)
    def _():
        logits = dot_nn(rows_in[...], wr[...])
        weights = jnp.exp(logits - jnp.max(logits, axis=-1, keepdims=True))
        probs = weights / jnp.sum(weights, axis=-1, keepdims=True)
        probs_s[...] = probs
        hot = iota(logits.shape, 1) == which[0]
        gate = jnp.sum(jnp.where(hot, probs, 0.0), axis=1, keepdims=True)
        scaled[...] = (gate * grads_in[...].astype(F32)).astype(BF)
        back_sum[...] = jnp.zeros_like(back_sum)
        result_sum[...] = jnp.zeros_like(result_sum)

    rows = rows_in[...]
    grads = scaled[...]
    pre = dot_nn(rows, weight_in[0])
    grad_hidden = dot_nt(grads, weight_out[0])
    scale = 0.7978845608028654
    square = pre * pre
    bent = jnp.tanh(scale * (pre + 0.044715 * (pre * square)))
    half = 0.5 * (1.0 + bent)
    hidden = (pre * half).astype(BF)
    slope = half + (0.5 * scale) * pre * (1.0 - bent * bent) * (1.0 + 0.134145 * square)
    grad_pre = (grad_hidden * slope).astype(BF)
    grad_in_o[0] = dot_tn(rows, grad_pre).astype(BF)
    grad_out_o[0] = dot_tn(hidden, grads).astype(BF)
    result_sum[...] += dot_nn(hidden, weight_out[0])
    back_sum[...] += dot_nt(grad_pre, weight_in[0])

    @pl.when(step == pl.num_programs(0) - 1)
    def _():
        returned = result_sum[...].astype(BF)
        returned_o[...] = returned
        probs = probs_s[...]
        hot = iota(probs.shape, 1) == which[0]
        gate = jnp.sum(jnp.where(hot, probs, 0.0), axis=1, keepdims=True)
        grad_gate = jnp.sum(
            grads_in[...].astype(F32) * returned.astype(F32), axis=1, keepdims=True
        )
        grad_logits = (probs * (jnp.where(hot, 1.0, 0.0) - gate) * grad_gate).astype(BF)
        router_o[...] = dot_tn(rows_in[...], grad_logits)
        back_o[...] = (back_sum[...] + dot_nt(grad_logits, wr[...])).astype(BF)


def expert_step(order, which, local, rows_in, grads_in, weight_in, weight_out, wr):
    rows, width = rows_in.shape
    hidden = weight_in.shape[2]
    steps = order.shape[0]
    chunk = hidden // steps
    experts = wr.shape[1]
    return pl.pallas_call(
        expert_kernel,
        grid_spec=pltpu.PrefetchScalarGridSpec(
            num_scalar_prefetch=2,
            grid=(steps,),
            in_specs=[
                whole((rows, width)),
                whole((rows, width)),
                pl.BlockSpec((1, width, chunk), lambda s, order, which: (local, 0, order[s])),
                pl.BlockSpec((1, chunk, width), lambda s, order, which: (local, order[s], 0)),
                whole(wr.shape),
            ],
            out_specs=(
                whole((rows, width)),
                whole((rows, width)),
                whole((width, experts)),
                pl.BlockSpec((1, width, chunk), lambda s, order, which: (s, 0, 0)),
                pl.BlockSpec((1, chunk, width), lambda s, order, which: (s, 0, 0)),
            ),
            scratch_shapes=[
                pltpu.VMEM((rows, width), BF),
                pltpu.VMEM((rows, experts), F32),
                pltpu.VMEM((rows, width), F32),
                pltpu.VMEM((rows, width), F32),
            ],
        ),
        out_shape=(
            jax.ShapeDtypeStruct((rows, width), BF),
            jax.ShapeDtypeStruct((rows, width), BF),
            jax.ShapeDtypeStruct((width, experts), F32),
            jax.ShapeDtypeStruct((steps, width, chunk), BF),
            jax.ShapeDtypeStruct((steps, chunk, width), BF),
        ),
        compiler_params=params(dimension_semantics=("arbitrary",)),
        cost_estimate=pl.CostEstimate(
            flops=12 * rows * width * hidden,
            bytes_accessed=8 * width * hidden,
            transcendentals=rows * hidden,
        ),
        name="expert",
    )(order, which, rows_in, grads_in, weight_in, weight_out, wr)


def middle_kernel(
    slots, slot_col, residual, grad, gain_two, att, wo,
    grad_residual_o, grad_att_o, grad_gain_o, grad_wo_o,
):
    rows, width = residual.shape
    pick = (slot_col[...] == iota((rows, slots.shape[0]), 1)).astype(BF)
    upstream = dot_nn(pick, slots[...])
    values = residual[...]
    factor = lax.rsqrt(jnp.mean(values * values, axis=-1, keepdims=True) + EPSILON)
    weighted = upstream * gain_two[...]
    inner = jnp.mean(weighted * values, axis=-1, keepdims=True)
    grad_gain_o[...] = jnp.sum(upstream * values * factor, axis=0, keepdims=True)
    grad_residual = (
        grad[...].astype(F32)
        + factor * weighted
        - values * (factor * factor * factor) * inner
    )
    grad_residual_o[...] = grad_residual
    low = grad_residual.astype(BF)
    grad_wo_o[...] = dot_tn(att[...], low).astype(BF)
    grad_att_o[...] = dot_nt(low, wo[...]).astype(BF)


def middle(slots, slot_col, residual, grad, gain_two, att, wo):
    rows, width = residual.shape
    return pl.pallas_call(
        middle_kernel,
        out_shape=(
            jax.ShapeDtypeStruct((rows, width), F32),
            jax.ShapeDtypeStruct((rows, width), BF),
            jax.ShapeDtypeStruct((1, width), F32),
            jax.ShapeDtypeStruct((width, width), BF),
        ),
        compiler_params=params(),
        cost_estimate=pl.CostEstimate(
            flops=2 * rows * width * (slots.shape[0] + 2 * width),
            bytes_accessed=20 << 20,
            transcendentals=0,
        ),
        name="middle",
    )(slots, slot_col, residual, grad, gain_two, att, wo)


def backward_kernel(
    head_dim, seq_len, buckets,
    tokens, gain_one, normed, ids, grad_residual, q, k, v, att, inv, soft, grad_att, wq, wk, wv,
    grad_tokens_o, grad_gain_o, grad_wq_o, grad_wk_o, grad_wv_o, grad_bucket_o,
    score_sums, normed_sum,
):
    step = pl.program_id(0)
    rows, width = tokens.shape
    group = wq.shape[1]
    per_tile = LANES // head_dim
    per_group = group // head_dim
    seqs = rows // seq_len
    lane = iota((seq_len, LANES), 1)
    outs = [[[None] * seqs for _ in range(group // LANES)] for _ in range(3)]
    for tile in range(group // LANES):
        cols = slice(tile * LANES, (tile + 1) * LANES)
        for seq in range(seqs):
            span = slice(seq * seq_len, (seq + 1) * seq_len)
            heads_grad = (grad_att[span, cols].astype(F32) * inv[span, cols])
            low_grad = heads_grad.astype(BF)
            inner = low_grad.astype(F32) * att[span, cols].astype(F32)
            grad_t = low_grad.T
            query_t = q[span, cols].T
            query_sum = None
            key_rows, value_rows = [], []
            for part in range(per_tile):
                head = tile * per_tile + part
                mine = (lane >= part * head_dim) & (lane < (part + 1) * head_dim)
                heads = slice(part * head_dim, (part + 1) * head_dim)
                grad_probs = dot_nt(jnp.where(mine, low_grad, 0).astype(BF), v[span, cols])
                row_inner = jnp.sum(jnp.where(mine, inner, 0.0), axis=-1, keepdims=True)
                low_soft = soft[head, seq]
                scores = (low_soft.astype(F32) * (grad_probs - row_inner)).astype(BF)
                if seq == 0:
                    score_sums[step * per_group + head] = scores
                else:
                    score_sums[step * per_group + head] = (
                        score_sums[step * per_group + head].astype(F32) + scores.astype(F32)
                    ).astype(BF)
                value_rows.append(dot_nn(grad_t[heads, :], low_soft))
                key_rows.append(dot_nn(query_t[heads, :], scores))
                grad_query = dot_nn(scores, k[span, cols])
                query_sum = grad_query if part == 0 else jnp.where(mine, grad_query, query_sum)
            outs[0][tile][seq] = (query_sum * 0.125).astype(BF)
            outs[1][tile][seq] = (jnp.concatenate(key_rows, axis=0).T * 0.125).astype(BF)
            outs[2][tile][seq] = jnp.concatenate(value_rows, axis=0).T.astype(BF)

    def assemble(parts):
        return jnp.concatenate([jnp.concatenate(tile, axis=0) for tile in parts], axis=1)

    grad_q, grad_k, grad_v = [assemble(parts) for parts in outs]
    low_normed = normed[...]
    grad_wq_o[...] = dot_tn(low_normed, grad_q).astype(BF)
    grad_wk_o[...] = dot_tn(low_normed, grad_k).astype(BF)
    grad_wv_o[...] = dot_tn(low_normed, grad_v).astype(BF)
    part = dot_nt(grad_q, wq[...]) + dot_nt(grad_k, wk[...]) + dot_nt(grad_v, wv[...])

    @pl.when(step == 0)
    def _():
        normed_sum[...] = part

    @pl.when(step > 0)
    def _():
        normed_sum[...] += part

    @pl.when(step == pl.num_programs(0) - 1)
    def _():
        upstream = normed_sum[...]
        values = tokens[...].astype(F32)
        factor = lax.rsqrt(jnp.mean(values * values, axis=-1, keepdims=True) + EPSILON)
        weighted = upstream * gain_one[...]
        inner = jnp.mean(weighted * values, axis=-1, keepdims=True)
        grad_gain_o[...] = jnp.sum(upstream * values * factor, axis=0, keepdims=True)
        grad_tokens_o[...] = (
            grad_residual[...]
            + factor * weighted
            - values * (factor * factor * factor) * inner
        )
        heads = score_sums.shape[0]
        rows_at = 16
        sums = jnp.zeros((rows_at * buckets, heads * rows_at), F32)

        def add(block, sums):
            at = pl.multiple_of(block * rows_at, rows_at)
            own = ids[pl.ds(at, rows_at), :]
            hot = own[:, None, :] == iota((rows_at, buckets, seq_len), 1)
            hot = hot.astype(BF).reshape(rows_at * buckets, seq_len)
            scores = score_sums[:, pl.ds(at, rows_at), :].reshape(heads * rows_at, seq_len)
            return sums + dot_nt(hot, scores)

        sums = lax.fori_loop(0, seq_len // rows_at, add, sums)
        sums = sums.reshape(rows_at, buckets, heads * rows_at)
        keep = iota(sums.shape, 0) == iota(sums.shape, 2) % rows_at
        grad_bucket_o[...] = jnp.sum(jnp.where(keep, sums, 0.0), axis=0)


def backward(
    tokens, gain_one, normed, bucket_ids, grad_residual, q, k, v, att, inv, soft, grad_att, weights,
    groups, head_dim, buckets,
):
    rows, width = tokens.shape
    seq_len = bucket_ids.shape[0]
    heads, seqs = soft.shape[:2]
    group = width // groups
    per_group = heads // groups
    cols = lambda shape: pl.BlockSpec(shape, lambda g: (0, g))
    once = lambda shape: pl.BlockSpec(
        shape, lambda g: (0,) * len(shape), pipeline_mode=pl.Buffered(1)
    )
    grads = pl.pallas_call(
        functools.partial(backward_kernel, head_dim, seq_len, buckets),
        grid=(groups,),
        in_specs=[
            once((rows, width)),
            whole((1, width)),
            once((rows, width)),
            once((seq_len, seq_len)),
            once((rows, width)),
            cols((rows, group)),
            cols((rows, group)),
            cols((rows, group)),
            cols((rows, group)),
            cols((rows, group)),
            pl.BlockSpec((per_group, seqs, seq_len, seq_len), lambda g: (g, 0, 0, 0)),
            cols((rows, group)),
            cols((width, group)),
            cols((width, group)),
            cols((width, group)),
        ],
        out_specs=(
            whole((rows, width)),
            whole((1, width)),
            cols((width, group)),
            cols((width, group)),
            cols((width, group)),
            whole((buckets, heads * 16)),
        ),
        scratch_shapes=[
            pltpu.VMEM((heads, seq_len, seq_len), BF),
            pltpu.VMEM((rows, width), F32),
        ],
        out_shape=(
            jax.ShapeDtypeStruct((rows, width), F32),
            jax.ShapeDtypeStruct((1, width), F32),
            jax.ShapeDtypeStruct((width, width), BF),
            jax.ShapeDtypeStruct((width, width), BF),
            jax.ShapeDtypeStruct((width, width), BF),
            jax.ShapeDtypeStruct((buckets, heads * 16), F32),
        ),
        compiler_params=params(dimension_semantics=("arbitrary",)),
        cost_estimate=pl.CostEstimate(
            flops=2 * rows * width * (6 * width + 5 * seq_len * 4),
            bytes_accessed=50 << 20,
            transcendentals=0,
        ),
        name="backward",
    )(
        tokens, gain_one, normed, bucket_ids, grad_residual, q, k, v, att, inv, soft, grad_att,
        *weights,
    )
    return grads[:-1] + (grads[-1].reshape(buckets, heads, 16).sum(axis=2),)


def combine_kernel(slots, slot_col, residual, gate, mixed_o):
    pick = (slot_col[...] == iota((residual.shape[0], slots.shape[0]), 1)).astype(BF)
    mixed_o[...] = (residual[...] + gate[...] * dot_nn(pick, slots[...])).astype(BF)


def combine(slots, slot_col, residual, gate):
    rows, width = residual.shape
    return pl.pallas_call(
        combine_kernel,
        out_shape=jax.ShapeDtypeStruct((rows, width), BF),
        compiler_params=params(),
        cost_estimate=pl.CostEstimate(
            flops=2 * rows * width * slots.shape[0], bytes_accessed=8 << 20, transcendentals=0
        ),
        name="combine",
    )(slots, slot_col, residual, gate)


def swap(values, axis, bit):
    size = lax.axis_size(axis)
    return lax.ppermute(values, axis, [(i, i ^ bit) for i in range(size)])


def bits_of(size):
    return [1 << i for i in range(size.bit_length() - 1)]


def scatter_sum(blocks, axis, bits):
    count = blocks.shape[0]
    held = {j: blocks[count - 1 - j] for j in range(count)}
    for bit in bits:
        sent = [j for j in held if j & bit]
        arrived = swap(jnp.stack([held[j] for j in sent]), axis, bit)
        for at, j in enumerate(sent):
            total = held[j ^ bit].astype(F32) + arrived[at].astype(F32)
            held[j ^ bit] = total if len(held) == 2 else total.astype(BF)
            del held[j]
    return held[0]


def all_sum(values, steps):
    rows = values.shape[0]
    width = values.shape[1]
    trail = []
    held = values
    for axis, bit in steps:
        high = (lax.axis_index(axis) & bit) != 0
        half = held.shape[0] // 2
        low_part, high_part = held[:half], held[half:]
        arrived = swap(jnp.where(high, low_part, high_part), axis, bit)
        own = jnp.where(high, high_part, low_part)
        held = (own.astype(F32) + arrived.astype(F32)).astype(values.dtype)
    for axis, bit in reversed(steps):
        high = (lax.axis_index(axis) & bit) != 0
        arrived = swap(held, axis, bit)
        held = jnp.concatenate(
            [jnp.where(high, arrived, held), jnp.where(high, held, arrived)], axis=0
        )
    return held


def per_device(
    tokens,
    expert_ids,
    bucket_ids,
    attn_gain,
    ffn_gain,
    query_weight,
    key_weight,
    value_weight,
    output_weight,
    router_weight,
    bucket_bias,
    expert_in,
    expert_out,
    grad_output,
):
    tok_rows, width = tokens.shape
    buckets, heads = bucket_bias.shape
    head_dim = width // heads
    local = expert_in.shape[0]
    ranks = lax.axis_size("expert")
    copies = lax.axis_size("dp")
    experts = local * ranks
    cap = (5 * tok_rows + 4 * experts - 1) // (4 * experts)
    slots = experts * cap
    half = slots // local
    per_group = 4
    groups = heads // per_group
    my_rank = lax.axis_index("expert")
    my_copy = lax.axis_index("dp")
    table = jnp.pad(bucket_bias.T, ((0, 0), (0, LANES - buckets)))
    table = table.reshape(groups, per_group, LANES)
    gains = (attn_gain.reshape(1, width), ffn_gain.reshape(1, width))

    slot_col, slot_row, grad_slots = make_slots(ranks, local, cap, expert_ids, grad_output)

    def exchange(rows):
        blocks = rows.reshape(ranks, cap, width)
        got = lax.all_to_all(blocks, "expert", split_axis=0, concat_axis=0, tiled=True)
        return got.reshape(half, width)

    (
        normed, q, k, v, att, inv, soft, residual, nf, gate, row_slots
    ) = forward(
        tokens, bucket_ids, table, gains,
        (query_weight, key_weight, value_weight, output_weight),
        router_weight, expert_ids, slot_row, slots, head_dim,
    )
    order = my_copy ^ (copies - 1 - jnp.arange(copies, dtype=jnp.int32))
    grads_at = [exchange(grad_slots[e * half:(e + 1) * half]) for e in range(local)]
    rows_at = [exchange(row_slots[e * half:(e + 1) * half]) for e in range(local)]
    returned, back, router, shares_in, shares_out = [], [], [], [], []
    for e in range(local):
        which = (my_rank * local + e).reshape(1).astype(jnp.int32)
        one = expert_step(
            order, which, e, rows_at[e], grads_at[e], expert_in, expert_out, router_weight
        )
        returned.append(exchange(one[0]))
        back.append(exchange(one[1]))
        router.append(one[2])
        shares_in.append(one[3])
        shares_out.append(one[4])
    bits = bits_of(copies)
    grad_expert_in = jnp.stack([scatter_sum(s, "dp", bits) for s in shares_in])
    grad_expert_out = jnp.stack([scatter_sum(s, "dp", bits[::-1]) for s in shares_out])
    grad_residual, grad_att, grad_ffn_gain, grad_wo = middle(
        jnp.concatenate(back), slot_col, residual, grad_output, gains[1], att, output_weight
    )
    grad_tokens, grad_attn_gain, grad_wq, grad_wk, grad_wv, grad_bucket = backward(
        tokens, gains[0], normed, bucket_ids, grad_residual, q, k, v, att, inv, soft, grad_att,
        (query_weight, key_weight, value_weight), groups, head_dim, buckets,
    )
    mixed = combine(jnp.concatenate(returned), slot_col, residual, gate)
    first = [("expert", 1)]
    plane = [("dp", bit) for bit in bits]
    line = [("expert", bit) for bit in bits_of(ranks)[1:]]
    grad_wo = all_sum(grad_wo, first + line + plane)
    grad_wq = all_sum(grad_wq, first + line + plane)
    grad_wk = all_sum(grad_wk, first + plane + line)
    grad_wv = all_sum(grad_wv, first + plane[::-1] + line)
    small = [grad_attn_gain, grad_ffn_gain, sum(router), grad_bucket]
    sizes = [part.size for part in small]
    flat = jnp.concatenate([part.reshape(-1) for part in small])
    flat = lax.psum(flat, ("dp", "expert"))
    out = []
    at = 0
    for part, size in zip(small, sizes):
        out.append(flat[at:at + size].reshape(part.shape))
        at += size
    return (
        mixed,
        grad_tokens,
        out[0].reshape(width),
        out[1].reshape(width),
        grad_wq.astype(F32),
        grad_wk.astype(F32),
        grad_wv.astype(F32),
        grad_wo.astype(F32),
        out[2],
        out[3],
        grad_expert_in,
        grad_expert_out,
    )


def solution(mesh):
    shared = P()
    rows = P(("dp", "expert"), None)
    expert = P("expert", None, None)
    return jax.shard_map(
        per_device,
        mesh=mesh,
        in_specs=(rows, rows) + (shared,) * 9 + (expert, expert, rows),
        out_specs=(rows, rows) + (shared,) * 8 + (P("expert", None, "dp"), P("expert", "dp", None)),
        check_vma=False,
    )
```

```python
import functools

import jax
import jax.numpy as jnp
from jax import lax
from jax.experimental import pallas as pl
from jax.experimental.pallas import tpu as pltpu
from jax.sharding import PartitionSpec as P

EPSILON = 1e-06
BF = jnp.bfloat16
F32 = jnp.float32
LANES = 128
VMEM_BYTES = 62 * 1024 * 1024


def dot_nn(left, right):
    return lax.dot_general(left, right, (((1,), (0,)), ((), ())), preferred_element_type=F32)


def dot_nt(left, right):
    return lax.dot_general(left, right, (((1,), (1,)), ((), ())), preferred_element_type=F32)


def dot_tn(left, right):
    return lax.dot_general(left, right, (((0,), (0,)), ((), ())), preferred_element_type=F32)


def iota(shape, axis):
    return lax.broadcasted_iota(jnp.int32, shape, axis)


def whole(shape):
    return pl.BlockSpec(shape, lambda *_: (0,) * len(shape))


def params(**more):
    return pltpu.CompilerParams(vmem_limit_bytes=VMEM_BYTES, **more)


def slots_kernel(ranks, local, cap, room, ids_col, ids_row, grad, slot_col, slot_row, first_grads, other_grads):
    rows = grad.shape[0]
    experts = ranks * local
    first = iota((rows, rows), 0)
    second = iota((rows, rows), 1)

    def place_of(ids, hot, counts, axis):
        place = jnp.sum(jnp.where(hot, counts, 0.0), axis=axis, keepdims=True).astype(jnp.int32)
        rank = jnp.floor((ids.astype(F32) + 0.5) * (1.0 / local)).astype(jnp.int32)
        base = ((ids - rank * local) * ranks + rank) * room
        return jnp.where(place < cap, base + place, -1)

    hot_col = ids_col[...] == iota((rows, experts), 1)
    counts_col = dot_nn((second < first).astype(BF), hot_col.astype(BF))
    slot_col[...] = place_of(ids_col[...], hot_col, counts_col, 1)
    hot_row = ids_row[...] == iota((experts, rows), 0)
    counts_row = dot_nn(hot_row.astype(BF), (first < second).astype(BF))
    slot_row[...] = place_of(ids_row[...], hot_row, counts_row, 0)
    pick = (iota((experts * room, rows), 0) == slot_row[...]).astype(BF)
    picked = dot_nn(pick, grad[...]).astype(BF)
    first_grads[...] = picked[:ranks * room]
    other_grads[...] = picked[ranks * room:]


def make_slots(ranks, local, cap, room, expert_ids, grad_output):
    rows, width = grad_output.shape
    slots = ranks * local * room
    return pl.pallas_call(
        functools.partial(slots_kernel, ranks, local, cap, room),
        out_shape=(
            jax.ShapeDtypeStruct((rows, 1), jnp.int32),
            jax.ShapeDtypeStruct((1, rows), jnp.int32),
            jax.ShapeDtypeStruct((ranks * room, width), BF),
            jax.ShapeDtypeStruct((slots - ranks * room, width), BF),
        ),
        compiler_params=params(),
        name="slots",
    )(expert_ids, expert_ids.reshape(1, rows), grad_output)


def forward_kernel(
    head_dim, seq_len,
    tokens, ids, table, gain_one, gain_two, wq, wk, wv, wo, wr, ids_col, slot_row,
    normed_o, q_o, k_o, v_o, att_o, inv_o, soft_o, residual_o, nf_o, gate_o, slots_o,
):
    step = pl.program_id(0)
    rows, width = tokens.shape
    group = wq.shape[1]

    @pl.when(step == 0)
    def _():
        x = tokens[...].astype(F32)
        factor = lax.rsqrt(jnp.mean(x * x, axis=-1, keepdims=True) + EPSILON)
        normed_o[...] = (x * factor * gain_one[...]).astype(BF)
        residual_o[...] = x

    normed = normed_o[...]
    q_o[...] = dot_nn(normed, wq[...]).astype(BF)
    k_o[...] = dot_nn(normed, wk[...]).astype(BF)
    v_o[...] = dot_nn(normed, wv[...]).astype(BF)
    lane = iota((seq_len, LANES), 1)
    per_tile = LANES // head_dim
    for tile in range(group // LANES):
        cols = slice(tile * LANES, (tile + 1) * LANES)
        gathered = [None] * (rows // seq_len)
        scaled = [None] * (rows // seq_len)
        for part in range(per_tile):
            head = tile * per_tile + part
            mine = (lane >= part * head_dim) & (lane < (part + 1) * head_dim)
            row = jnp.broadcast_to(table[0, head:head + 1, :], (seq_len, LANES))
            bias = jnp.concatenate(
                [
                    jnp.take_along_axis(
                        row, ids[:, c:c + LANES], axis=1, mode="promise_in_bounds"
                    )
                    for c in range(0, seq_len, LANES)
                ],
                axis=1,
            )
            for seq in range(rows // seq_len):
                span = slice(seq * seq_len, (seq + 1) * seq_len)
                query = jnp.where(mine, q_o[span, cols] * 0.125, 0).astype(BF)
                scores = dot_nt(query, k_o[span, cols]) + bias
                weights = jnp.exp(scores - jnp.max(scores, axis=-1, keepdims=True))
                inverse = 1.0 / jnp.sum(weights, axis=-1, keepdims=True)
                low = weights.astype(BF)
                soft_o[head, seq] = low
                out = dot_nn(low, v_o[span, cols]) * inverse
                inverse = jnp.broadcast_to(inverse, (seq_len, LANES))
                if part == 0:
                    gathered[seq], scaled[seq] = out, inverse
                else:
                    gathered[seq] = jnp.where(mine, out, gathered[seq])
                    scaled[seq] = jnp.where(mine, inverse, scaled[seq])
        for seq in range(rows // seq_len):
            span = slice(seq * seq_len, (seq + 1) * seq_len)
            att_o[span, cols] = gathered[seq].astype(BF)
            inv_o[span, cols] = scaled[seq]
    residual_o[...] += dot_nn(att_o[...], wo[...])

    @pl.when(step == pl.num_programs(0) - 1)
    def _():
        residual = residual_o[...]
        factor = lax.rsqrt(jnp.mean(residual * residual, axis=-1, keepdims=True) + EPSILON)
        low = (residual * factor * gain_two[...]).astype(BF)
        nf_o[...] = low
        logits = dot_nn(low, wr[...])
        weights = jnp.exp(logits - jnp.max(logits, axis=-1, keepdims=True))
        probs = weights / jnp.sum(weights, axis=-1, keepdims=True)
        hot = ids_col[...] == iota(logits.shape, 1)
        gate_o[...] = jnp.sum(jnp.where(hot, probs, 0.0), axis=1, keepdims=True)
        pick = (iota((slots_o.shape[0], rows), 0) == slot_row[...]).astype(BF)
        slots_o[...] = dot_nn(pick, low).astype(BF)


def forward(tokens, bucket_ids, table, gains, weights, wr, expert_ids, slot_row, slots, head_dim):
    rows, width = tokens.shape
    seq_len = bucket_ids.shape[0]
    groups, per_group, _ = table.shape
    group = width // groups
    heads = groups * per_group
    seqs = rows // seq_len
    cols = lambda shape: pl.BlockSpec(shape, lambda g: (0, g))
    wq, wk, wv, wo = weights
    return pl.pallas_call(
        functools.partial(forward_kernel, head_dim, seq_len),
        grid=(groups,),
        in_specs=[
            whole((rows, width)),
            whole((seq_len, seq_len)),
            pl.BlockSpec((1, per_group, LANES), lambda g: (g, 0, 0)),
            whole((1, width)),
            whole((1, width)),
            cols((width, group)),
            cols((width, group)),
            cols((width, group)),
            pl.BlockSpec((group, width), lambda g: (g, 0)),
            whole(wr.shape),
            whole((rows, 1)),
            whole((1, rows)),
        ],
        out_specs=(
            whole((rows, width)),
            cols((rows, group)),
            cols((rows, group)),
            cols((rows, group)),
            cols((rows, group)),
            cols((rows, group)),
            pl.BlockSpec((per_group, seqs, seq_len, seq_len), lambda g: (g, 0, 0, 0)),
            whole((rows, width)),
            whole((rows, width)),
            whole((rows, 1)),
            whole((slots, width)),
        ),
        out_shape=(
            jax.ShapeDtypeStruct((rows, width), BF),
            jax.ShapeDtypeStruct((rows, width), BF),
            jax.ShapeDtypeStruct((rows, width), BF),
            jax.ShapeDtypeStruct((rows, width), BF),
            jax.ShapeDtypeStruct((rows, width), BF),
            jax.ShapeDtypeStruct((rows, width), F32),
            jax.ShapeDtypeStruct((heads, seqs, seq_len, seq_len), BF),
            jax.ShapeDtypeStruct((rows, width), F32),
            jax.ShapeDtypeStruct((rows, width), BF),
            jax.ShapeDtypeStruct((rows, 1), F32),
            jax.ShapeDtypeStruct((slots, width), BF),
        ),
        compiler_params=params(dimension_semantics=("arbitrary",)),
        cost_estimate=pl.CostEstimate(
            flops=2 * rows * width * (4 * width + 2 * seq_len * 4),
            bytes_accessed=40 << 20,
            transcendentals=heads * rows * seq_len,
        ),
        name="forward",
    )(tokens, bucket_ids, table, *gains, wq, wk, wv, wo, wr, expert_ids, slot_row)


def bits_of(size):
    return [1 << i for i in range(size.bit_length() - 1)]


def flip(index, bit):
    return index + bit * (1 - 2 * ((index // bit) % 2))


def flip_all(index, mask, bits):
    for bit in bits:
        index = jnp.where((mask // bit) % 2 == 1, flip(index, bit), index)
    return index


def experts_kernel(
    ranks, copies,
    x_send, g_first, g_send, weight_in, weight_out, wr,
    returned_o, back_o, router_o, sum_in_o, sum_out_o, shares_in_o, shares_out_o,
    x_recv, g_recv, back_send, win, wout, grads_in, grads_out, got_in, got_out,
    last_in, last_out, scaled, probs_s, back_sum, result_sum, result,
    x_ss, x_rs, g_ss, g_rs, b_ss, b_rs, w_sem, share_sem, first_ss, first_rs, next_ss, next_rs,
    result_sem, sum_sem,
):
    local = x_send.shape[0]
    cap, width = x_send.shape[2:]
    rows = ranks * cap
    chunk = win.shape[2]
    steps = copies
    bits = bits_of(copies)
    orders = (bits, bits[::-1])
    me = lax.axis_index("expert")
    copy = lax.axis_index("dp")
    mesh_id = pl.DeviceIdType.MESH

    barrier = pltpu.get_barrier_semaphore()

    def greet(d, carry):
        pl.semaphore_signal(
            barrier, inc=1, device_id={"expert": (me + d) % ranks}, device_id_type=mesh_id
        )
        return carry

    lax.fori_loop(1, ranks, greet, 0)
    for bit in bits:
        pl.semaphore_signal(
            barrier, inc=1, device_id={"dp": flip(copy, bit)}, device_id_type=mesh_id
        )

    def load(s):
        e, j = s // steps, steps - 1 - s % steps
        at = pl.multiple_of(flip_all(copy, j, bits) * chunk, chunk)
        return (
            pltpu.make_async_copy(
                weight_in.at[e, :, pl.ds(at, chunk)], win.at[s % 2], w_sem.at[0, s % 2]
            ),
            pltpu.make_async_copy(
                weight_out.at[e, pl.ds(at, chunk), :], wout.at[s % 2], w_sem.at[1, s % 2]
            ),
        )

    for one in load(0):
        one.start()
    pl.semaphore_wait(barrier, ranks - 1 + len(bits))

    def row_copy(source, target, sends, recvs, e, at, peer):
        return pltpu.make_async_remote_copy(
            src_ref=source.at[e, peer],
            dst_ref=target.at[e, at],
            send_sem=sends.at[e, peer],
            recv_sem=recvs.at[e, at],
            device_id={"expert": peer},
            device_id_type=mesh_id,
        )

    def stay(source, target, recvs, e):
        return pltpu.make_async_copy(source.at[e, me], target.at[e, me], recvs.at[e, me])

    def send(source, target, sends, recvs, e):
        def one(d, carry):
            row_copy(source, target, sends, recvs, e, me, (me + d) % ranks).start()
            return carry

        lax.fori_loop(1, ranks, one, 0)
        stay(source, target, recvs, e).start()

    def arrive(source, target, sends, recvs, e):
        def one(d, carry):
            peer = (me + ranks - d) % ranks
            row_copy(source, target, sends, recvs, e, peer, peer).wait_recv()
            return carry

        lax.fori_loop(1, ranks, one, 0)
        stay(source, target, recvs, e).wait()

    def leave(source, target, sends, recvs, e):
        def one(d, carry):
            row_copy(source, target, sends, recvs, e, me, (me + d) % ranks).wait_send()
            return carry

        lax.fori_loop(1, ranks, one, 0)

    moves = (
        (grads_in, got_in, last_in, 0),
        (grads_out, got_out, last_out, 1),
    )

    def share_copy(which, stage, j):
        grads, got, last, k = moves[which]
        bit = orders[which][stage]
        done = sum(orders[which][:stage])
        kept = [p for p in range(copies) if p & (done + bit) == 0]
        at = kept.index(j ^ bit)
        target, sends, recvs = (got, first_ss, first_rs) if stage == 0 else (last, next_ss, next_rs)
        return pltpu.make_async_remote_copy(
            src_ref=grads.at[j],
            dst_ref=target.at[at],
            send_sem=sends.at[k, at],
            recv_sem=recvs.at[k, at],
            device_id={"dp": flip(copy, bit)},
            device_id_type=mesh_id,
        )

    def keep_sum(which):
        return pltpu.make_async_copy(
            moves[which][0].at[0], (sum_in_o, sum_out_o)[which], sum_sem.at[which]
        )

    def sent_at(which, stage):
        bit = orders[which][stage]
        done = sum(orders[which][:stage])
        return [j for j in range(copies) if j & bit and not j & done]

    def keep_result(e):
        return pltpu.make_async_copy(result, returned_o.at[e], result_sem)

    def store(e, t, k):
        source, target = ((grads_in, shares_in_o), (grads_out, shares_out_o))[k]
        return pltpu.make_async_copy(
            source.at[steps + t % 2], target.at[e - 1, t], share_sem.at[k, t % 2]
        )

    send(x_send, x_recv, x_ss, x_rs, 0)
    router_o[...] = jnp.zeros_like(router_o)

    def body(s, carry):
        e, t = s // steps, s % steps
        j = steps - 1 - t

        @pl.when(s + 1 < local * steps)
        def _():
            for one in load(s + 1):
                one.start()

        @pl.when(t == 0)
        def _():
            arrive(x_send, x_recv, x_ss, x_rs, e)

            @pl.when(e > 0)
            def _():
                arrive(g_send, g_recv, g_ss, g_rs, e - 1)

            @pl.when(e + 1 < local)
            def _():
                send(g_send, g_recv, g_ss, g_rs, e)
                send(x_send, x_recv, x_ss, x_rs, e + 1)

            logits = dot_nn(x_recv[e].reshape(rows, width), wr[...])
            weights = jnp.exp(logits - jnp.max(logits, axis=-1, keepdims=True))
            probs = weights / jnp.sum(weights, axis=-1, keepdims=True)
            probs_s[...] = probs
            hot = iota(logits.shape, 1) == me * local + e
            gate = jnp.sum(jnp.where(hot, probs, 0.0), axis=1, keepdims=True)

            @pl.when(e == 0)
            def _():
                scaled[...] = (gate * g_first[...].astype(F32)).astype(BF)

            @pl.when(e > 0)
            def _():
                raw = g_recv[jnp.maximum(e - 1, 0)].reshape(rows, width)
                scaled[...] = (gate * raw.astype(F32)).astype(BF)

            back_sum[...] = jnp.zeros_like(back_sum)
            result_sum[...] = jnp.zeros_like(result_sum)

        for one in load(s):
            one.wait()

        @pl.when((e > 0) & ((t > 1) | (e > 1)))
        def _():
            for k in range(2):
                store(e, t, k).wait()

        slot = jnp.where(e == 0, j, steps + t % 2)
        own_in, own_out = win[s % 2], wout[s % 2]
        taken = x_recv[e].reshape(rows, width)
        grads = scaled[...]
        pre = dot_nn(taken, own_in)
        grad_hidden = dot_nt(grads, own_out)
        scale = 0.7978845608028654
        square = pre * pre
        bent = jnp.tanh(scale * (pre + 0.044715 * (pre * square)))
        half = 0.5 * (1.0 + bent)
        hidden = (pre * half).astype(BF)
        slope = half + (0.5 * scale) * pre * (1.0 - bent * bent) * (1.0 + 0.134145 * square)
        grad_pre = (grad_hidden * slope).astype(BF)
        grads_in[slot] = dot_tn(taken, grad_pre).astype(BF)
        grads_out[slot] = dot_tn(hidden, grads).astype(BF)

        for at in range(copies):
            @pl.when((e == 0) & (j == at))
            def _():
                for which in range(2):
                    if at in sent_at(which, 0):
                        share_copy(which, 0, at).start()

        @pl.when(e > 0)
        def _():
            for k in range(2):
                store(e, t, k).start()

        result_sum[...] += dot_nn(hidden, own_out)
        back_sum[...] += dot_nt(grad_pre, own_in)

        @pl.when(t == steps - 1)
        def _():
            returned = result_sum[...].astype(BF)

            @pl.when(e > 0)
            def _():
                keep_result(e - 1).wait()

            result[...] = returned
            keep_result(e).start()
            probs = probs_s[...]
            hot = iota(probs.shape, 1) == me * local + e
            gate = jnp.sum(jnp.where(hot, probs, 0.0), axis=1, keepdims=True)

            def finish(raw):
                grad_gate = jnp.sum(
                    raw.astype(F32) * returned.astype(F32), axis=1, keepdims=True
                )
                slope = jnp.where(hot, 1.0, 0.0) - gate
                grad_logits = (probs * slope * grad_gate).astype(BF)
                router_o[...] += dot_tn(grad_logits, x_recv[e].reshape(rows, width))
                back = (back_sum[...] + dot_nt(grad_logits, wr[...])).astype(BF)
                back_send[e] = back.reshape(ranks, cap, width)

            @pl.when(e == 0)
            def _():
                finish(g_first[...])

            @pl.when(e > 0)
            def _():
                finish(g_recv[jnp.maximum(e - 1, 0)].reshape(rows, width))

            send(back_send, back_o, b_ss, b_rs, e)

        return carry

    lax.fori_loop(0, local * steps, body, 0)

    for stage in range(len(bits)):
        for which in range(2):
            grads, got, last, _ = moves[which]
            gone = sent_at(which, stage)
            for at, j in enumerate(gone):
                share_copy(which, stage, j).wait_recv()
                keep = j ^ orders[which][stage]
                held = grads[keep].astype(F32) + (got if stage == 0 else last)[at].astype(F32)
                grads[keep] = held.astype(BF)
                if stage + 1 == len(bits):
                    keep_sum(which).start()
            if stage + 1 < len(bits):
                for j in sent_at(which, stage + 1):
                    share_copy(which, stage + 1, j).start()
        if stage == 0:
            for e in range(local):
                arrive(back_send, back_o, b_ss, b_rs, e)
    for stage in range(len(bits)):
        for which in range(2):
            for j in sent_at(which, stage):
                share_copy(which, stage, j).wait_send()
    for which in range(2):
        keep_sum(which).wait()
    keep_result(local - 1).wait()
    for e in range(local):
        leave(x_send, x_recv, x_ss, x_rs, e)
        leave(back_send, back_o, b_ss, b_rs, e)
        if e:
            leave(g_send, g_recv, g_ss, g_rs, e - 1)
    if local > 1:
        for t in range(max(0, steps - 2), steps):
            for k in range(2):
                store(local - 1, t, k).wait()


def run_experts(x_send, g_first, g_send, weight_in, weight_out, wr, copies):
    local, ranks, cap, width = x_send.shape
    rows = ranks * cap
    hidden = weight_in.shape[2]
    chunk = hidden // copies
    experts = wr.shape[1]
    bits = len(bits_of(copies))
    half = copies // 2
    vmem = pl.BlockSpec(memory_space=pltpu.VMEM)
    hbm = pl.BlockSpec(memory_space=pl.ANY)
    block = (ranks, cap, width)
    dma = pltpu.SemaphoreType.DMA
    return pl.pallas_call(
        functools.partial(experts_kernel, ranks, copies),
        in_specs=[hbm, vmem, hbm, hbm, hbm, vmem],
        out_specs=(hbm, hbm, vmem, hbm, hbm, hbm, hbm),
        out_shape=(
            jax.ShapeDtypeStruct((local, rows, width), BF),
            jax.ShapeDtypeStruct((local,) + block, BF),
            jax.ShapeDtypeStruct((experts, width), F32),
            jax.ShapeDtypeStruct((width, chunk), BF),
            jax.ShapeDtypeStruct((chunk, width), BF),
            jax.ShapeDtypeStruct((local - 1, copies, width, chunk), BF),
            jax.ShapeDtypeStruct((local - 1, copies, chunk, width), BF),
        ),
        scratch_shapes=[
            pltpu.VMEM((local,) + block, BF),
            pltpu.VMEM((local - 1,) + block, BF),
            pltpu.VMEM((local,) + block, BF),
            pltpu.VMEM((2, width, chunk), BF),
            pltpu.VMEM((2, chunk, width), BF),
            pltpu.VMEM((copies + 2, width, chunk), BF),
            pltpu.VMEM((copies + 2, chunk, width), BF),
            pltpu.VMEM((half, width, chunk), BF),
            pltpu.VMEM((half, chunk, width), BF),
            pltpu.VMEM((max(half // 2, 1), width, chunk), BF),
            pltpu.VMEM((max(half // 2, 1), chunk, width), BF),
            pltpu.VMEM((rows, width), BF),
            pltpu.VMEM((rows, experts), F32),
            pltpu.VMEM((rows, width), F32),
            pltpu.VMEM((rows, width), F32),
            pltpu.VMEM((rows, width), BF),
            dma((local, ranks)),
            dma((local, ranks)),
            dma((local - 1, ranks)),
            dma((local - 1, ranks)),
            dma((local, ranks)),
            dma((local, ranks)),
            dma((2, 2)),
            dma((2, 2)),
            dma((2, half)),
            dma((2, half)),
            dma((2, max(half // 2, 1))),
            dma((2, max(half // 2, 1))),
            dma,
            dma((2,)),
        ],
        compiler_params=params(collective_id=0, has_side_effects=True),
        cost_estimate=pl.CostEstimate(
            flops=12 * local * rows * width * hidden,
            bytes_accessed=8 * local * width * hidden,
            transcendentals=local * rows * hidden,
        ),
        name="experts",
    )(x_send, g_first, g_send, weight_in, weight_out, wr)


def middle_kernel(
    slots, slot_col, residual, grad, gain_two, att, wo,
    grad_residual_o, grad_att_o, grad_gain_o, grad_wo_o,
):
    rows, width = residual.shape
    pick = (slot_col[...] == iota((rows, slots.shape[0]), 1)).astype(BF)
    upstream = dot_nn(pick, slots[...])
    values = residual[...]
    factor = lax.rsqrt(jnp.mean(values * values, axis=-1, keepdims=True) + EPSILON)
    weighted = upstream * gain_two[...]
    inner = jnp.mean(weighted * values, axis=-1, keepdims=True)
    grad_gain_o[...] = jnp.sum(upstream * values * factor, axis=0, keepdims=True)
    grad_residual = (
        grad[...].astype(F32)
        + factor * weighted
        - values * (factor * factor * factor) * inner
    )
    grad_residual_o[...] = grad_residual
    low = grad_residual.astype(BF)
    grad_wo = dot_tn(att[...], low).astype(BF)
    for part in range(2):
        grad_wo_o[part] = grad_wo[:, part * (width // 2):(part + 1) * (width // 2)]
    grad_att_o[...] = dot_nt(low, wo[...]).astype(BF)


def middle(slots, slot_col, residual, grad, gain_two, att, wo):
    rows, width = residual.shape
    return pl.pallas_call(
        middle_kernel,
        out_shape=(
            jax.ShapeDtypeStruct((rows, width), F32),
            jax.ShapeDtypeStruct((rows, width), BF),
            jax.ShapeDtypeStruct((1, width), F32),
            jax.ShapeDtypeStruct((2, width, width // 2), BF),
        ),
        compiler_params=params(),
        cost_estimate=pl.CostEstimate(
            flops=2 * rows * width * (slots.shape[0] + 2 * width),
            bytes_accessed=20 << 20,
            transcendentals=0,
        ),
        name="middle",
    )(slots, slot_col, residual, grad, gain_two, att, wo)


PIECES = 4


def sums_inside(width, copies, ranks):
    return ranks == 2 * copies and width % (16 * copies * copies) == 0


def backward_kernel(
    head_dim, seq_len, buckets, copies, ranks,
    tokens, gain_one, normed, ids, grad_residual, q, k, v, att, inv, soft, grad_att, wq, wk, wv,
    grad_wo, grad_gain_two, router, returned, shares_in, shares_out,
    grad_tokens_o, pieces_o, small_o, got_o, sum_in_o, sum_out_o,
    score_sums, normed_sum, parts, part_got, level_got, level_sum, last_got, last_sum,
    keep_in, keep_out, share_in, share_out, next_in, next_out,
    small_s, small_all, small_core, small_line, small_plane, small_half,
    r_ss, r_rs, c_ss, c_rs, l1_ss, l1_rs, l2_ss, l2_rs, g2_ss, g2_rs, g1_ss, g1_rs, h_ss, h_rs,
    own_sem, s_ss, s_rs, n_ss, n_rs, keep_sem, sum_sem, m_ss, m_rs,
):
    step = pl.program_id(0)
    steps = pl.num_programs(0)
    rows, width = tokens.shape
    group = wq.shape[1]
    seqs = rows // seq_len
    local = returned.shape[0]
    bits = bits_of(copies)
    orders = (bits, bits[::-1])
    me = lax.axis_index("expert")
    copy = lax.axis_index("dp")
    core = me % 2
    line = me // 2
    mesh_id = pl.DeviceIdType.MESH
    inside = sums_inside(width, copies, ranks)
    count = copies

    def remote(source, target, sends, recvs, device):
        return pltpu.make_async_remote_copy(
            src_ref=source, dst_ref=target, send_sem=sends, recv_sem=recvs,
            device_id=device, device_id_type=mesh_id,
        )


    def result_copy(e, at, peer):
        return remote(
            returned.at[e, peer], got_o.at[e, at], r_ss.at[e, peer], r_rs.at[e, at],
            {"expert": peer},
        )

    def result_stay(e):
        return pltpu.make_async_copy(returned.at[e, me], got_o.at[e, me], r_rs.at[e, me])

    def results_start(e):
        def one(d, carry):
            result_copy(e, me, (me + d) % ranks).start()
            return carry

        lax.fori_loop(1, ranks, one, 0)
        result_stay(e).start()

    def results_wait(e):
        def one(d, carry):
            peer = (me + ranks - d) % ranks
            result_copy(e, peer, peer).wait_recv()
            result_copy(e, me, (me + d) % ranks).wait_send()
            return carry

        lax.fori_loop(1, ranks, one, 0)
        result_stay(e).wait()


    moves = (
        (shares_in, keep_in, share_in, next_in, sum_in_o),
        (shares_out, keep_out, share_out, next_out, sum_out_o),
    )

    def sent_at(which, stage):
        bit = orders[which][stage]
        done = sum(orders[which][:stage])
        return [j for j in range(copies) if j & bit and not j & done]

    def kept_at(which, stage):
        done = sum(orders[which][:stage + 1])
        return [j for j in range(copies) if not j & done]

    def share_copy(which, stage, j):
        shares, keep, first, last, _ = moves[which]
        bit = orders[which][stage]
        at = kept_at(which, stage).index(j ^ bit)
        if stage == 0:
            source, target, sends, recvs = shares.at[0, copies - 1 - j], first, s_ss, s_rs
        else:
            source, target, sends, recvs = keep.at[kept_at(which, 0).index(j)], last, n_ss, n_rs
        return remote(
            source, target.at[at], sends.at[which, at], recvs.at[which, at],
            {"dp": flip(copy, bit)},
        )

    def keep_copy(which, at, j):
        shares, keep = moves[which][:2]
        return pltpu.make_async_copy(
            shares.at[0, copies - 1 - j], keep.at[at], keep_sem.at[which, at]
        )

    def shares_start():
        for which in range(2):
            for j in sent_at(which, 0):
                share_copy(which, 0, j).start()
        for which in range(2):
            for at, j in enumerate(kept_at(which, 0)):
                keep_copy(which, at, j).start()

    def shares_turn():
        for which in range(2):
            keep, first = moves[which][1:3]
            for at, j in enumerate(kept_at(which, 0)):
                keep_copy(which, at, j).wait()
                share_copy(which, 0, j ^ orders[which][0]).wait_recv()
                keep[at] = (keep[at].astype(F32) + first[at].astype(F32)).astype(BF)
            for j in sent_at(which, 1):
                share_copy(which, 1, j).start()

    def sum_copy(which):
        return pltpu.make_async_copy(moves[which][1].at[0], moves[which][4], sum_sem.at[which])

    def shares_end():
        for which in range(2):
            keep, _, last = moves[which][1:4]
            share_copy(which, 1, orders[which][1]).wait_recv()
            keep[0] = (keep[0].astype(F32) + last[0].astype(F32)).astype(BF)
            sum_copy(which).start()
        for which in range(2):
            for stage in range(2):
                for j in sent_at(which, stage):
                    share_copy(which, stage, j).wait_send()
            sum_copy(which).wait()


    def levels(p):
        along = (line, lambda i: {"expert": 2 * i + core})
        across = (copy, lambda i: {"dp": i})
        return (along, across) if p in ALONG_FIRST else (across, along)

    def core_copy(p):
        return remote(
            parts.at[p, 1 - core], part_got.at[p], c_ss.at[p], c_rs.at[p], {"expert": me + 1 - 2 * core}
        )

    def first_copy(p, peer, at):
        (_, device), _ = levels(p)
        return remote(
            parts.at[p, core, pl.ds(peer * count, count)], level_got.at[p, at],
            l1_ss.at[p, peer], l1_rs.at[p, at], device(peer),
        )

    def second_copy(p, peer, at):
        _, (_, device) = levels(p)
        return remote(
            level_sum.at[p, peer], last_got.at[p, at], l2_ss.at[p, peer], l2_rs.at[p, at],
            device(peer),
        )

    def give_second(p, peer, at):
        (mine, _), (_, device) = levels(p)
        return remote(
            last_sum.at[p], pieces_o.at[p, core, mine * count + at],
            g2_ss.at[p, peer], g2_rs.at[p, at], device(peer),
        )

    def give_own(p):
        (mine, _), (own, _) = levels(p)
        return pltpu.make_async_copy(
            last_sum.at[p], pieces_o.at[p, core, mine * count + own], own_sem.at[p]
        )

    def give_first(p, peer, at):
        (_, device), _ = levels(p)
        block = pieces_o.at[p, core, pl.ds(at * count, count)]
        return remote(block, block, g1_ss.at[p, peer], g1_rs.at[p, at], device(peer))

    def give_core(p, half):
        block = pieces_o.at[p, half]
        return remote(block, block, h_ss.at[p], h_rs.at[p], {"expert": me + 1 - 2 * core})

    def others(own):
        return [(own + d) % count for d in range(1, count)]

    def piece_0(p):
        core_copy(p).start()

    def piece_1(p):
        (own, _), _ = levels(p)
        core_copy(p).wait_recv()
        parts[p, core] = (parts[p, core].astype(F32) + part_got[p].astype(F32)).astype(BF)
        for peer in others(own):
            first_copy(p, peer, own).start()

    def piece_2(p):
        (first, _), (own, _) = levels(p)
        total = parts[p, core, pl.ds(first * count, count)].astype(F32)
        for peer in others(first):
            first_copy(p, peer, peer).wait_recv()
            total += level_got[p, peer].astype(F32)
        level_sum[p] = total.astype(BF)
        for peer in others(own):
            second_copy(p, peer, own).start()

    def piece_3(p):
        _, (own, _) = levels(p)
        total = level_sum[p, own].astype(F32)
        for peer in others(own):
            second_copy(p, peer, peer).wait_recv()
            total += last_got[p, peer].astype(F32)
        last_sum[p] = total.astype(BF)
        for peer in others(own):
            give_second(p, peer, own).start()
        give_own(p).start()

    def piece_4(p):
        (first, _), (own, _) = levels(p)
        for peer in others(own):
            give_second(p, peer, peer).wait_recv()
        give_own(p).wait()
        for peer in others(first):
            give_first(p, peer, first).start()

    def piece_5(p):
        (first, _), _ = levels(p)
        for peer in others(first):
            give_first(p, peer, peer).wait_recv()
        give_core(p, core).start()

    def piece_6(p):
        (first, _), (own, _) = levels(p)
        give_core(p, 1 - core).wait_recv()
        core_copy(p).wait_send()
        give_core(p, core).wait_send()
        for peer in others(first):
            first_copy(p, peer, first).wait_send()
            give_first(p, peer, first).wait_send()
        for peer in others(own):
            second_copy(p, peer, own).wait_send()
            give_second(p, peer, own).wait_send()

    stages = (piece_0, piece_1, piece_2, piece_3, piece_4, piece_5, piece_6)


    half = small_half.shape[0]

    def small_copy(stage, peer, at):
        if stage == 0:
            source, target, device = small_s, small_core, {"expert": me + 1 - 2 * core}
        elif stage == 1:
            source, target, device = small_half, small_line.at[at], {"expert": 2 * peer + core}
        elif stage == 2:
            source, target, device = small_half, small_plane.at[at], {"dp": peer}
        else:
            source = small_all.at[pl.ds(pl.multiple_of(core * half, 8), half)]
            target, device = source, {"expert": me + 1 - 2 * core}
        return remote(source, target, m_ss.at[stage, peer], m_rs.at[stage, at], device)

    def small_0():
        small_copy(0, 0, 0).start()

    def small_1():
        small_copy(0, 0, 0).wait()
        span = pl.ds(pl.multiple_of(core * half, 8), half)
        small_half[...] = small_s[span] + small_core[span]
        for peer in others(line):
            small_copy(1, peer, line).start()

    def small_2():
        total = small_half[...]
        for peer in others(line):
            small_copy(1, peer, peer).wait_recv()
            total += small_line[peer]
        for peer in others(line):
            small_copy(1, peer, line).wait_send()
        small_half[...] = total
        for peer in others(copy):
            small_copy(2, peer, copy).start()

    def small_3():
        total = small_half[...]
        for peer in others(copy):
            small_copy(2, peer, peer).wait_recv()
            total += small_plane[peer]
        small_all[pl.ds(pl.multiple_of(core * half, 8), half)] = total
        small_copy(3, 0, 0).start()

    def small_4():
        for peer in others(copy):
            small_copy(2, peer, copy).wait_send()
        small_copy(3, 0, 0).wait()

    @pl.when(step == 0)
    def _():
        barrier = pltpu.get_barrier_semaphore()

        def greet(axis, own, size):
            def one(d, carry):
                pl.semaphore_signal(
                    barrier, inc=1, device_id={axis: (own + d) % size}, device_id_type=mesh_id
                )
                return carry

            lax.fori_loop(1, size, one, 0)

        greet("expert", me, ranks)
        greet("dp", copy, copies)
        pl.semaphore_wait(barrier, ranks + copies - 2)
        parts[PIECES - 1] = grad_wo[...].reshape(parts.shape[1:])
        if inside:
            piece_0(PIECES - 1)
        shares_start()
        results_start(0)


    per_step = group // head_dim
    lane = iota((seq_len, group), 1)
    grads = [[None] * seqs for _ in range(3)]
    for seq in range(seqs):
        span = slice(seq * seq_len, (seq + 1) * seq_len)
        low_grad = (grad_att[span, :].astype(F32) * inv[span, :]).astype(BF)
        inner = low_grad.astype(F32) * att[span, :].astype(F32)
        grad_t = low_grad.T
        query_t = q[span, :].T
        query_sum = None
        key_rows, value_rows = [], []
        for head in range(per_step):
            mine = (lane >= head * head_dim) & (lane < (head + 1) * head_dim)
            own = slice(head * head_dim, (head + 1) * head_dim)
            grad_probs = dot_nt(jnp.where(mine, low_grad, 0).astype(BF), v[span, :])
            row_inner = jnp.sum(jnp.where(mine, inner, 0.0), axis=-1, keepdims=True)
            low_soft = soft[head, seq]
            scores = (low_soft.astype(F32) * (grad_probs - row_inner)).astype(BF)
            at = step * per_step + head
            if seq == 0:
                score_sums[at] = scores
            else:
                score_sums[at] = (score_sums[at].astype(F32) + scores.astype(F32)).astype(BF)
            value_rows.append(dot_nn(grad_t[own, :], low_soft))
            key_rows.append(dot_nn(query_t[own, :], scores))
            grad_query = dot_nn(scores, k[span, :])
            query_sum = grad_query if head == 0 else jnp.where(mine, grad_query, query_sum)
        grads[0][seq] = (query_sum * 0.125).astype(BF)
        grads[1][seq] = (jnp.concatenate(key_rows, axis=0).T * 0.125).astype(BF)
        grads[2][seq] = jnp.concatenate(value_rows, axis=0).T.astype(BF)
    grads = jnp.concatenate([jnp.concatenate(one, axis=0) for one in grads], axis=1)
    weights = jnp.concatenate([wq[...], wk[...], wv[...]], axis=1)
    parts[step // 2, step % 2] = dot_tn(normed[...], grads).astype(BF).reshape(parts.shape[2:])
    part = dot_nt(grads, weights)

    @pl.when(step == 0)
    def _():
        normed_sum[...] = part

    @pl.when(step > 0)
    def _():
        normed_sum[...] += part

    for after, todo in PIECE_PLAN.items():
        @pl.when(step == after)
        def _():
            for p, stage in todo:
                if inside:
                    stages[stage](p)

    @pl.when(step == 2)
    def _():
        for e in range(1, local):
            results_start(e)

    @pl.when(step == steps - 1)
    def _():
        upstream = normed_sum[...]
        values = tokens[...].astype(F32)
        factor = lax.rsqrt(jnp.mean(values * values, axis=-1, keepdims=True) + EPSILON)
        weighted = upstream * gain_one[...]
        mean = jnp.mean(weighted * values, axis=-1, keepdims=True)
        gain = jnp.sum(upstream * values * factor, axis=0, keepdims=True)
        grad_tokens_o[...] = (
            grad_residual[...]
            + factor * weighted
            - values * (factor * factor * factor) * mean
        )
        heads = score_sums.shape[0]
        rows_at = 16

        def add(block, sums):
            at = pl.multiple_of(block * rows_at, rows_at)
            own = ids[pl.ds(at, rows_at), :]
            hot = own[:, None, :] == iota((rows_at, buckets, seq_len), 1)
            hot = hot.astype(BF).reshape(rows_at * buckets, seq_len)
            scores = score_sums[:, pl.ds(at, rows_at), :].reshape(heads * rows_at, seq_len)
            return sums + dot_nt(hot, scores)

        sums = jnp.zeros((rows_at * buckets, heads * rows_at), F32)
        sums = lax.fori_loop(0, seq_len // rows_at, add, sums)
        sums = sums.reshape(rows_at, buckets, heads * rows_at)
        across = iota(sums.shape, 2)
        keep = iota(sums.shape, 0) == across % rows_at
        sums = jnp.sum(jnp.where(keep, sums, 0.0), axis=0)
        into = iota((heads * rows_at, LANES), 0) // rows_at == iota((heads * rows_at, LANES), 1)
        bucket = lax.dot_general(
            sums, into.astype(F32), (((1,), (0,)), ((), ())),
            precision=lax.Precision.HIGHEST, preferred_element_type=F32,
        )
        small_s[...] = jnp.zeros_like(small_s)
        tiles = width // LANES
        experts = router.shape[0]
        for tile in range(tiles):
            cols = slice(tile * LANES, (tile + 1) * LANES)
            small_s[tile:tile + 1, :] = gain[:, cols]
            small_s[8 + tile:9 + tile, :] = grad_gain_two[:, cols]
            at = 16 + buckets + tile * experts
            small_s[at:at + experts, :] = router[:, cols]
        small_s[16:16 + buckets, :] = bucket
        if inside:
            small_0()
            piece_1(2)
            shares_turn()
            small_1()
            piece_4(0)
            piece_3(1)
            small_2()
            piece_5(3)
            piece_2(2)
            small_3()
            piece_5(0)
            piece_4(1)
            piece_3(2)
            small_4()
            piece_5(1)
            piece_4(2)
        else:
            shares_turn()
        small_o[...] = small_all[...] if inside else small_s[...]
        for e in range(local):
            results_wait(e)
        shares_end()
        if inside:
            piece_5(2)
            for p in (3, 0, 1, 2):
                piece_6(p)
        else:
            for p in range(PIECES):
                out = pltpu.make_async_copy(parts.at[p], pieces_o.at[p], own_sem.at[p])
                out.start()
                out.wait()


ALONG_FIRST = (3, 0, 1)
PIECE_PLAN = {
    0: ((3, 1),),
    1: ((0, 0),),
    2: ((0, 1), (3, 2)),
    3: ((1, 0), (3, 3)),
    4: ((1, 1), (0, 2), (3, 4)),
    5: ((2, 0), (0, 3), (1, 2)),
}


def backward(
    tokens, gain_one, normed, bucket_ids, grad_residual, q, k, v, att, inv, soft, grad_att, weights,
    grad_wo, grad_gain_two, router, returned, shares_in, shares_out, head_dim, buckets, copies, ranks,
):
    rows, width = tokens.shape
    seq_len = bucket_ids.shape[0]
    heads, seqs = soft.shape[:2]
    local = returned.shape[0]
    experts = router.shape[0]
    chunk = shares_in.shape[3]
    group = LANES
    steps = width // group
    per_step = heads // steps
    inside = sums_inside(width, copies, ranks)
    chips = copies * copies if inside else 1
    block = (width // chips, width // 2)
    small_rows = -(-(16 + buckets + width // LANES * experts) // 16) * 16
    cols = lambda shape: pl.BlockSpec(shape, lambda g: (0, g))
    once = lambda shape: pl.BlockSpec(
        shape, lambda g: (0,) * len(shape), pipeline_mode=pl.Buffered(1)
    )
    hbm = pl.BlockSpec(memory_space=pl.ANY)
    dma = pltpu.SemaphoreType.DMA
    each = dma((PIECES, copies))
    return pl.pallas_call(
        functools.partial(backward_kernel, head_dim, seq_len, buckets, copies, ranks),
        grid=(steps,),
        in_specs=[
            once((rows, width)),
            once((1, width)),
            once((rows, width)),
            once((seq_len, seq_len)),
            once((rows, width)),
            cols((rows, group)),
            cols((rows, group)),
            cols((rows, group)),
            cols((rows, group)),
            cols((rows, group)),
            pl.BlockSpec((per_step, seqs, seq_len, seq_len), lambda g: (g, 0, 0, 0)),
            cols((rows, group)),
            cols((width, group)),
            cols((width, group)),
            cols((width, group)),
            once((2, width, width // 2)),
            once((1, width)),
            once((experts, width)),
            hbm,
            hbm,
            hbm,
        ],
        out_specs=(
            once((rows, width)),
            hbm,
            once((small_rows, LANES)),
            hbm,
            hbm,
            hbm,
        ),
        scratch_shapes=[
            pltpu.VMEM((heads, seq_len, seq_len), BF),
            pltpu.VMEM((rows, width), F32),
            pltpu.VMEM((PIECES, 2, chips) + block, BF),
            pltpu.VMEM((PIECES, chips) + block, BF),
            pltpu.VMEM((PIECES, copies, copies) + block if inside else (8, LANES), BF),
            pltpu.VMEM((PIECES, copies) + block if inside else (8, LANES), BF),
            pltpu.VMEM((PIECES, copies) + block if inside else (8, LANES), BF),
            pltpu.VMEM((PIECES,) + block, BF),
            pltpu.VMEM((copies // 2, width, chunk), BF),
            pltpu.VMEM((copies // 2, chunk, width), BF),
            pltpu.VMEM((copies // 2, width, chunk), BF),
            pltpu.VMEM((copies // 2, chunk, width), BF),
            pltpu.VMEM((copies // 4, width, chunk), BF),
            pltpu.VMEM((copies // 4, chunk, width), BF),
            pltpu.VMEM((small_rows, LANES), F32),
            pltpu.VMEM((small_rows, LANES), F32),
            pltpu.VMEM((small_rows, LANES), F32),
            pltpu.VMEM((copies, small_rows // 2, LANES), F32),
            pltpu.VMEM((copies, small_rows // 2, LANES), F32),
            pltpu.VMEM((small_rows // 2, LANES), F32),
            dma((local, ranks)),
            dma((local, ranks)),
            dma((PIECES,)),
            dma((PIECES,)),
            each, each, each, each, each, each, each, each,
            dma((PIECES,)),
            dma((PIECES,)),
            dma((PIECES,)),
            dma((2, copies // 2)),
            dma((2, copies // 2)),
            dma((2, max(copies // 4, 1))),
            dma((2, max(copies // 4, 1))),
            dma((2, copies // 2)),
            dma((2,)),
            dma((4, copies)),
            dma((4, copies)),
        ],
        out_shape=(
            jax.ShapeDtypeStruct((rows, width), F32),
            jax.ShapeDtypeStruct((PIECES, 2, chips) + block, BF),
            jax.ShapeDtypeStruct((small_rows, LANES), F32),
            jax.ShapeDtypeStruct(returned.shape, BF),
            jax.ShapeDtypeStruct((width, chunk), BF),
            jax.ShapeDtypeStruct((chunk, width), BF),
        ),
        compiler_params=params(
            dimension_semantics=("arbitrary",), collective_id=1, has_side_effects=True
        ),
        cost_estimate=pl.CostEstimate(
            flops=2 * rows * width * (6 * width + 5 * seq_len * 4),
            bytes_accessed=50 << 20,
            transcendentals=0,
        ),
        name="backward",
    )(
        tokens, gain_one, normed, bucket_ids, grad_residual, q, k, v, att, inv, soft, grad_att,
        *weights, grad_wo, grad_gain_two, router, returned, shares_in, shares_out,
    )


def finish_kernel(
    slots, slot_col, residual, gate, pieces, in_0, out_0, in_1, out_1,
    mixed_o, wq_o, wk_o, wv_o, wo_o, grad_in_o, grad_out_o,
):
    width = residual.shape[1]
    pick = (slot_col[...] == iota((residual.shape[0], slots.shape[0]), 1)).astype(BF)
    mixed_o[...] = (residual[...] + gate[...] * dot_nn(pick, slots[...])).astype(BF)
    half = width // 2
    part = half // 3
    for step in range(width // part):
        block = pieces[step // 2, step % 2].astype(F32)
        for at, out in enumerate((wq_o, wk_o, wv_o)):
            out[:, step * part:(step + 1) * part] = block[:, at * part:(at + 1) * part]
    for side in range(2):
        wo_o[:, side * half:(side + 1) * half] = pieces[PIECES - 1, side].astype(F32)
    grad_in_o[0] = in_0[...].astype(F32)
    grad_in_o[1] = in_1[...].astype(F32)
    grad_out_o[0] = out_0[...].astype(F32)
    grad_out_o[1] = out_1[...].astype(F32)


def finish(slots, slot_col, residual, gate, pieces, in_0, out_0, in_1, out_1):
    rows, width = residual.shape
    count = 8
    pieces = pieces.reshape(PIECES, 2, width, width // 2)
    chunk = in_0.shape[1]
    by_rows = lambda height, across: pl.BlockSpec((height, across), lambda i: (i, 0))
    part = width // count
    return pl.pallas_call(
        finish_kernel,
        grid=(count,),
        in_specs=[
            whole(slots.shape),
            by_rows(rows // count, 1),
            by_rows(rows // count, width),
            by_rows(rows // count, 1),
            pl.BlockSpec((PIECES, 2, part, width // 2), lambda i: (0, 0, i, 0)),
            by_rows(part, chunk),
            by_rows(chunk // count, width),
            by_rows(part, chunk),
            by_rows(chunk // count, width),
        ],
        out_specs=(
            by_rows(rows // count, width),
            by_rows(part, width),
            by_rows(part, width),
            by_rows(part, width),
            by_rows(part, width),
            pl.BlockSpec((2, part, chunk), lambda i: (0, i, 0)),
            pl.BlockSpec((2, chunk // count, width), lambda i: (0, i, 0)),
        ),
        out_shape=(
            jax.ShapeDtypeStruct((rows, width), BF),
            jax.ShapeDtypeStruct((width, width), F32),
            jax.ShapeDtypeStruct((width, width), F32),
            jax.ShapeDtypeStruct((width, width), F32),
            jax.ShapeDtypeStruct((width, width), F32),
            jax.ShapeDtypeStruct((2, width, chunk), F32),
            jax.ShapeDtypeStruct((2, chunk, width), F32),
        ),
        compiler_params=params(dimension_semantics=("arbitrary",)),
        cost_estimate=pl.CostEstimate(
            flops=2 * rows * width * slots.shape[0], bytes_accessed=40 << 20, transcendentals=0
        ),
        name="finish",
    )(slots, slot_col, residual, gate, pieces, in_0, out_0, in_1, out_1)


def per_device(
    tokens,
    expert_ids,
    bucket_ids,
    attn_gain,
    ffn_gain,
    query_weight,
    key_weight,
    value_weight,
    output_weight,
    router_weight,
    bucket_bias,
    expert_in,
    expert_out,
    grad_output,
):
    tok_rows, width = tokens.shape
    buckets, heads = bucket_bias.shape
    head_dim = width // heads
    local = expert_in.shape[0]
    ranks = lax.axis_size("expert")
    copies = lax.axis_size("dp")
    experts = local * ranks
    cap = (5 * tok_rows + 4 * experts - 1) // (4 * experts)
    room = -(-cap // 16) * 16
    slots = experts * room
    half = slots // local
    per_group = 4
    groups = heads // per_group
    table = jnp.pad(bucket_bias.T, ((0, 0), (0, LANES - buckets)))
    table = table.reshape(groups, per_group, LANES)
    gains = (attn_gain.reshape(1, width), ffn_gain.reshape(1, width))

    slot_col, slot_row, first_grads, other_grads = make_slots(
        ranks, local, cap, room, expert_ids, grad_output
    )
    blocks = (local, ranks, room, width)
    first_grads = lax.all_to_all(
        first_grads.reshape(blocks[1:]), "expert", split_axis=0, concat_axis=0, tiled=True
    )
    (
        normed, q, k, v, att, inv, soft, residual, nf, gate, row_slots
    ) = forward(
        tokens, bucket_ids, table, gains,
        (query_weight, key_weight, value_weight, output_weight),
        router_weight, expert_ids, slot_row, slots, head_dim,
    )
    returned, back, router, sum_in, sum_out, shares_in, shares_out = run_experts(
        row_slots.reshape(blocks), first_grads.reshape(half, width),
        other_grads.reshape((local - 1,) + blocks[1:]), expert_in, expert_out, router_weight, copies,
    )
    grad_residual, grad_att, grad_ffn_gain, grad_wo = middle(
        back.reshape(slots, width), slot_col, residual, grad_output, gains[1], att, output_weight
    )
    grad_tokens, pieces, small, got, next_in, next_out = backward(
        tokens, gains[0], normed, bucket_ids, grad_residual, q, k, v, att, inv, soft, grad_att,
        (query_weight, key_weight, value_weight), grad_wo, grad_ffn_gain, router,
        returned.reshape(blocks), shares_in, shares_out, head_dim, buckets, copies, ranks,
    )
    if not sums_inside(width, copies, ranks):
        pieces = lax.psum(pieces.astype(F32), ("dp", "expert"))
        small = lax.psum(small, ("dp", "expert"))
    mixed, grad_wq, grad_wk, grad_wv, grad_wo, grad_expert_in, grad_expert_out = finish(
        got.reshape(slots, width), slot_col, residual, gate, pieces, sum_in, sum_out, next_in, next_out
    )
    tiles = width // LANES
    grad_attn_gain = small[:tiles].reshape(width)
    grad_ffn_gain = small[8:8 + tiles].reshape(width)
    grad_bucket = small[16:16 + buckets, :heads]
    at = 16 + buckets
    grad_router = small[at:at + experts * tiles].reshape(tiles, experts, LANES)
    grad_router = grad_router.transpose(0, 2, 1).reshape(width, experts)
    return (
        mixed,
        grad_tokens,
        grad_attn_gain,
        grad_ffn_gain,
        grad_wq,
        grad_wk,
        grad_wv,
        grad_wo,
        grad_router,
        grad_bucket,
        grad_expert_in,
        grad_expert_out,
    )


def solution(mesh):
    shared = P()
    rows = P(("dp", "expert"), None)
    expert = P("expert", None, None)
    return jax.shard_map(
        per_device,
        mesh=mesh,
        in_specs=(rows, rows) + (shared,) * 9 + (expert, expert, rows),
        out_specs=(rows, rows) + (shared,) * 8 + (P("expert", None, "dp"), P("expert", "dp", None)),
        check_vma=False,
    )
```

```python
import functools

import jax
import jax.numpy as jnp
from jax import lax
from jax.experimental import pallas as pl
from jax.experimental.pallas import tpu as pltpu
from jax.sharding import PartitionSpec as P

EPSILON = 1e-06
BF = jnp.bfloat16
F32 = jnp.float32
LANES = 128
VMEM_BYTES = 62 * 1024 * 1024


def dot_nn(left, right):
    return lax.dot_general(left, right, (((1,), (0,)), ((), ())), preferred_element_type=F32)


def dot_nt(left, right):
    return lax.dot_general(left, right, (((1,), (1,)), ((), ())), preferred_element_type=F32)


def dot_tn(left, right):
    return lax.dot_general(left, right, (((0,), (0,)), ((), ())), preferred_element_type=F32)


def iota(shape, axis):
    return lax.broadcasted_iota(jnp.int32, shape, axis)


def whole(shape):
    return pl.BlockSpec(shape, lambda *_: (0,) * len(shape))


def params(**more):
    return pltpu.CompilerParams(vmem_limit_bytes=VMEM_BYTES, **more)


def slots_kernel(ranks, local, cap, room, ids_col, ids_row, grad, slot_col, slot_row, slot_grads):
    rows = grad.shape[0]
    experts = ranks * local
    first = iota((rows, rows), 0)
    second = iota((rows, rows), 1)

    def place_of(ids, hot, counts, axis):
        place = jnp.sum(jnp.where(hot, counts, 0.0), axis=axis, keepdims=True).astype(jnp.int32)
        return jnp.where(place < cap, ids * room + place, -1)

    hot_col = ids_col[...] == iota((rows, experts), 1)
    counts_col = dot_nn((second < first).astype(BF), hot_col.astype(BF))
    slot_col[...] = place_of(ids_col[...], hot_col, counts_col, 1)
    hot_row = ids_row[...] == iota((experts, rows), 0)
    counts_row = dot_nn(hot_row.astype(BF), (first < second).astype(BF))
    slot_row[...] = place_of(ids_row[...], hot_row, counts_row, 0)
    pick = (iota((experts * room, rows), 0) == slot_row[...]).astype(BF)
    slot_grads[...] = dot_nn(pick, grad[...]).astype(BF)


def make_slots(ranks, local, cap, room, expert_ids, grad_output):
    rows, width = grad_output.shape
    slots = ranks * local * room
    return pl.pallas_call(
        functools.partial(slots_kernel, ranks, local, cap, room),
        out_shape=(
            jax.ShapeDtypeStruct((rows, 1), jnp.int32),
            jax.ShapeDtypeStruct((1, rows), jnp.int32),
            jax.ShapeDtypeStruct((slots, width), BF),
        ),
        compiler_params=params(),
        name="slots",
    )(expert_ids, expert_ids.reshape(1, rows), grad_output)


def forward_kernel(
    head_dim, seq_len,
    tokens, ids, table, gain_one, gain_two, wq, wk, wv, wo, wr, ids_col, slot_row,
    normed_o, q_o, k_o, v_o, att_o, inv_o, soft_o, residual_o, nf_o, gate_o, slots_o,
):
    step = pl.program_id(0)
    rows, width = tokens.shape
    group = wq.shape[1]

    @pl.when(step == 0)
    def _():
        x = tokens[...].astype(F32)
        factor = lax.rsqrt(jnp.mean(x * x, axis=-1, keepdims=True) + EPSILON)
        normed_o[...] = (x * factor * gain_one[...]).astype(BF)
        residual_o[...] = x

    normed = normed_o[...]
    q_o[...] = dot_nn(normed, wq[...]).astype(BF)
    k_o[...] = dot_nn(normed, wk[...]).astype(BF)
    v_o[...] = dot_nn(normed, wv[...]).astype(BF)
    lane = iota((seq_len, LANES), 1)
    per_tile = LANES // head_dim
    for tile in range(group // LANES):
        cols = slice(tile * LANES, (tile + 1) * LANES)
        gathered = [None] * (rows // seq_len)
        scaled = [None] * (rows // seq_len)
        for part in range(per_tile):
            head = tile * per_tile + part
            mine = (lane >= part * head_dim) & (lane < (part + 1) * head_dim)
            row = jnp.broadcast_to(table[0, head:head + 1, :], (seq_len, LANES))
            bias = jnp.concatenate(
                [
                    jnp.take_along_axis(
                        row, ids[:, c:c + LANES], axis=1, mode="promise_in_bounds"
                    )
                    for c in range(0, seq_len, LANES)
                ],
                axis=1,
            )
            for seq in range(rows // seq_len):
                span = slice(seq * seq_len, (seq + 1) * seq_len)
                query = jnp.where(mine, q_o[span, cols] * 0.125, 0).astype(BF)
                scores = dot_nt(query, k_o[span, cols]) + bias
                weights = jnp.exp(scores - jnp.max(scores, axis=-1, keepdims=True))
                inverse = 1.0 / jnp.sum(weights, axis=-1, keepdims=True)
                low = weights.astype(BF)
                soft_o[head, seq] = low
                out = dot_nn(low, v_o[span, cols]) * inverse
                inverse = jnp.broadcast_to(inverse, (seq_len, LANES))
                if part == 0:
                    gathered[seq], scaled[seq] = out, inverse
                else:
                    gathered[seq] = jnp.where(mine, out, gathered[seq])
                    scaled[seq] = jnp.where(mine, inverse, scaled[seq])
        for seq in range(rows // seq_len):
            span = slice(seq * seq_len, (seq + 1) * seq_len)
            att_o[span, cols] = gathered[seq].astype(BF)
            inv_o[span, cols] = scaled[seq]
    residual_o[...] += dot_nn(att_o[...], wo[...])

    @pl.when(step == pl.num_programs(0) - 1)
    def _():
        residual = residual_o[...]
        factor = lax.rsqrt(jnp.mean(residual * residual, axis=-1, keepdims=True) + EPSILON)
        low = (residual * factor * gain_two[...]).astype(BF)
        nf_o[...] = low
        logits = dot_nn(low, wr[...])
        weights = jnp.exp(logits - jnp.max(logits, axis=-1, keepdims=True))
        probs = weights / jnp.sum(weights, axis=-1, keepdims=True)
        hot = ids_col[...] == iota(logits.shape, 1)
        gate_o[...] = jnp.sum(jnp.where(hot, probs, 0.0), axis=1, keepdims=True)
        pick = (iota((slots_o.shape[0], rows), 0) == slot_row[...]).astype(BF)
        slots_o[...] = dot_nn(pick, low).astype(BF)


def forward(tokens, bucket_ids, table, gains, weights, wr, expert_ids, slot_row, slots, head_dim):
    rows, width = tokens.shape
    seq_len = bucket_ids.shape[0]
    groups, per_group, _ = table.shape
    group = width // groups
    heads = groups * per_group
    seqs = rows // seq_len
    cols = lambda shape: pl.BlockSpec(shape, lambda g: (0, g))
    wq, wk, wv, wo = weights
    return pl.pallas_call(
        functools.partial(forward_kernel, head_dim, seq_len),
        grid=(groups,),
        in_specs=[
            whole((rows, width)),
            whole((seq_len, seq_len)),
            pl.BlockSpec((1, per_group, LANES), lambda g: (g, 0, 0)),
            whole((1, width)),
            whole((1, width)),
            cols((width, group)),
            cols((width, group)),
            cols((width, group)),
            pl.BlockSpec((group, width), lambda g: (g, 0)),
            whole(wr.shape),
            whole((rows, 1)),
            whole((1, rows)),
        ],
        out_specs=(
            whole((rows, width)),
            cols((rows, group)),
            cols((rows, group)),
            cols((rows, group)),
            cols((rows, group)),
            cols((rows, group)),
            pl.BlockSpec((per_group, seqs, seq_len, seq_len), lambda g: (g, 0, 0, 0)),
            whole((rows, width)),
            whole((rows, width)),
            whole((rows, 1)),
            whole((slots, width)),
        ),
        out_shape=(
            jax.ShapeDtypeStruct((rows, width), BF),
            jax.ShapeDtypeStruct((rows, width), BF),
            jax.ShapeDtypeStruct((rows, width), BF),
            jax.ShapeDtypeStruct((rows, width), BF),
            jax.ShapeDtypeStruct((rows, width), BF),
            jax.ShapeDtypeStruct((rows, width), F32),
            jax.ShapeDtypeStruct((heads, seqs, seq_len, seq_len), BF),
            jax.ShapeDtypeStruct((rows, width), F32),
            jax.ShapeDtypeStruct((rows, width), BF),
            jax.ShapeDtypeStruct((rows, 1), F32),
            jax.ShapeDtypeStruct((slots, width), BF),
        ),
        compiler_params=params(dimension_semantics=("arbitrary",)),
        cost_estimate=pl.CostEstimate(
            flops=2 * rows * width * (4 * width + 2 * seq_len * 4),
            bytes_accessed=40 << 20,
            transcendentals=heads * rows * seq_len,
        ),
        name="forward",
    )(tokens, bucket_ids, table, *gains, wq, wk, wv, wo, wr, expert_ids, slot_row)


def bits_of(size):
    return [1 << i for i in range(size.bit_length() - 1)]


def flip(index, bit):
    return index + bit * (1 - 2 * ((index // bit) % 2))


def flip_all(index, mask, bits):
    for bit in bits:
        index = jnp.where((mask // bit) % 2 == 1, flip(index, bit), index)
    return index


def experts_kernel(
    ranks, copies,
    x_send, raw, weight_in, weight_out, wr,
    returned_o, back_o, router_o, next_in_o, keep_in_o, next_out_o, keep_out_o,
    x_recv, back_send, win, wout, grads_in, grads_out, got_in, got_out,
    scaled, probs_s, back_sum, result_sum, result,
    x_ss, x_rs, b_ss, b_rs, w_sem, first_ss, first_rs, result_sem, out_sem,
):
    local, cap, width = x_send.shape[1:]
    rows = ranks * cap
    chunk = win.shape[2]
    steps = copies
    bits = bits_of(copies)
    orders = (bits, bits[::-1])
    me = lax.axis_index("expert")
    copy = lax.axis_index("dp")
    mesh_id = pl.DeviceIdType.MESH

    barrier = pltpu.get_barrier_semaphore()

    def greet(d, carry):
        pl.semaphore_signal(
            barrier, inc=1, device_id={"expert": (me + d) % ranks}, device_id_type=mesh_id
        )
        return carry

    lax.fori_loop(1, ranks, greet, 0)
    for bit in bits:
        pl.semaphore_signal(
            barrier, inc=1, device_id={"dp": flip(copy, bit)}, device_id_type=mesh_id
        )

    def load(s):
        e, j = s // steps, steps - 1 - s % steps
        at = pl.multiple_of(flip_all(copy, j, bits) * chunk, chunk)
        return (
            pltpu.make_async_copy(
                weight_in.at[e, :, pl.ds(at, chunk)], win.at[s % 2], w_sem.at[0, s % 2]
            ),
            pltpu.make_async_copy(
                weight_out.at[e, pl.ds(at, chunk), :], wout.at[s % 2], w_sem.at[1, s % 2]
            ),
        )

    for one in load(0):
        one.start()
    pl.semaphore_wait(barrier, ranks - 1 + len(bits))


    def row_copy(out, e, at, peer):
        if out:
            source, target, sends, recvs = x_send.at[peer, e], x_recv.at[e, at], x_ss, x_rs
        else:
            source, target, sends, recvs = back_send.at[e, peer], back_o.at[at, e], b_ss, b_rs
        return pltpu.make_async_remote_copy(
            src_ref=source,
            dst_ref=target,
            send_sem=sends.at[e, peer],
            recv_sem=recvs.at[e, at],
            device_id={"expert": peer},
            device_id_type=mesh_id,
        )

    def stay(out, e):
        if out:
            return pltpu.make_async_copy(x_send.at[me, e], x_recv.at[e, me], x_rs.at[e, me])
        return pltpu.make_async_copy(back_send.at[e, me], back_o.at[me, e], b_rs.at[e, me])

    def send(out, e):
        def one(d, carry):
            row_copy(out, e, me, (me + d) % ranks).start()
            return carry

        lax.fori_loop(1, ranks, one, 0)
        stay(out, e).start()

    def arrive(out, e):
        def one(d, carry):
            peer = (me + ranks - d) % ranks
            row_copy(out, e, peer, peer).wait_recv()
            return carry

        lax.fori_loop(1, ranks, one, 0)
        stay(out, e).wait()

    def leave(out, e):
        def one(d, carry):
            row_copy(out, e, me, (me + d) % ranks).wait_send()
            return carry

        lax.fori_loop(1, ranks, one, 0)

    moves = (
        (grads_in, got_in, bits[0], next_in_o, keep_in_o),
        (grads_out, got_out, bits[1], next_out_o, keep_out_o),
    )
    spare, kept = steps, steps + 1

    def first_copy(k, e, j):
        grads, got, bit = moves[k][:3]
        at = 2 if e else (0 if j == steps - 1 else 1)
        return pltpu.make_async_remote_copy(
            src_ref=grads.at[spare if e else j],
            dst_ref=got.at[at],
            send_sem=first_ss.at[k, at],
            recv_sem=first_rs.at[k, at],
            device_id={"dp": flip(copy, bit)},
            device_id_type=mesh_id,
        )

    def store(k, t):
        grads, _, _, following, keep = moves[k]
        target = keep.at[1] if t == steps - 1 else following.at[2]
        return pltpu.make_async_copy(grads.at[steps - 1], target, out_sem.at[k, 0])

    def out_copy(k, at):
        grads, _, bit, following, keep = moves[k]
        source, target = (
            (grads.at[steps - 1 - bit], following.at[0]),
            (grads.at[0], keep.at[0]),
            (grads.at[kept], following.at[1]),
        )[at]
        return pltpu.make_async_copy(source, target, out_sem.at[k, 1 + at])

    def keep_result(e):
        return pltpu.make_async_copy(result, returned_o.at[e], result_sem)

    send(True, 0)
    router_o[...] = jnp.zeros_like(router_o)

    def body(s, carry):
        e, t = s // steps, s % steps
        j = steps - 1 - t

        @pl.when(s + 1 < local * steps)
        def _():
            for one in load(s + 1):
                one.start()

        @pl.when(t == 0)
        def _():
            arrive(True, e)

            @pl.when(e + 1 < local)
            def _():
                send(True, e + 1)

            logits = dot_nn(x_recv[e].reshape(rows, width), wr[...])
            weights = jnp.exp(logits - jnp.max(logits, axis=-1, keepdims=True))
            probs = weights / jnp.sum(weights, axis=-1, keepdims=True)
            probs_s[...] = probs
            hot = iota(logits.shape, 1) == me * local + e
            gate = jnp.sum(jnp.where(hot, probs, 0.0), axis=1, keepdims=True)

            scaled[...] = (gate * raw[:, e].reshape(rows, width).astype(F32)).astype(BF)
            back_sum[...] = jnp.zeros_like(back_sum)
            result_sum[...] = jnp.zeros_like(result_sum)

        for one in load(s):
            one.wait()

        late_at = [steps - 1 - moves[k][2] for k in range(2)]
        slots = [
            jnp.where(
                e == 0, j, jnp.where(t == 0, spare, jnp.where(j == late_at[k], kept, steps - 1))
            )
            for k in range(2)
        ]
        for k in range(2):
            bit = moves[k][2]

            @pl.when((e > 0) & (j == bit))
            def _():
                first_copy(k, 0, steps - 1).wait_send()

            @pl.when((e > 0) & (t == steps - 1))
            def _():
                store(k, 0).wait()

        own_in, own_out = win[s % 2], wout[s % 2]
        taken = x_recv[e].reshape(rows, width)
        grads = scaled[...]
        pre = dot_nn(taken, own_in)
        grad_hidden = dot_nt(grads, own_out)
        scale = 0.7978845608028654
        square = pre * pre
        bent = jnp.tanh(scale * (pre + 0.044715 * (pre * square)))
        half = 0.5 * (1.0 + bent)
        hidden = (pre * half).astype(BF)
        slope = half + (0.5 * scale) * pre * (1.0 - bent * bent) * (1.0 + 0.134145 * square)
        grad_pre = (grad_hidden * slope).astype(BF)
        grads_in[slots[0]] = dot_tn(taken, grad_pre).astype(BF)
        grads_out[slots[1]] = dot_tn(hidden, grads).astype(BF)

        for k in range(2):
            bit = moves[k][2]
            for at in (steps - 1, bit):
                @pl.when((e == 0) & (j == at))
                def _():
                    first_copy(k, 0, at).start()

            @pl.when((e > 0) & (t == 0))
            def _():
                first_copy(k, 1, steps - 1).start()

            @pl.when((e > 0) & (j == bit))
            def _():
                store(k, 0).start()

            @pl.when((e > 0) & (t == steps - 1))
            def _():
                store(k, steps - 1).start()

        result_sum[...] += dot_nn(hidden, own_out)
        back_sum[...] += dot_nt(grad_pre, own_in)

        @pl.when(t == steps - 1)
        def _():
            returned = result_sum[...].astype(BF)

            @pl.when(e > 0)
            def _():
                keep_result(e - 1).wait()

            result[...] = returned.reshape(result.shape)
            keep_result(e).start()
            probs = probs_s[...]
            hot = iota(probs.shape, 1) == me * local + e
            gate = jnp.sum(jnp.where(hot, probs, 0.0), axis=1, keepdims=True)

            grad_gate = jnp.sum(
                raw[:, e].reshape(rows, width).astype(F32) * returned.astype(F32), axis=1, keepdims=True
            )
            slope = jnp.where(hot, 1.0, 0.0) - gate
            grad_logits = (probs * slope * grad_gate).astype(BF)
            router_o[...] += dot_tn(grad_logits, x_recv[e].reshape(rows, width))
            back = (back_sum[...] + dot_nt(grad_logits, wr[...])).astype(BF)
            back_send[e] = back.reshape(ranks, cap, width)
            send(False, e)

        return carry

    lax.fori_loop(0, local * steps, body, 0)

    for at in range(2):
        for k in range(2):
            grads, got, bit = moves[k][:3]
            into = (steps - 1 - bit, 0)[at]
            first_copy(k, 0, (steps - 1, bit)[at]).wait_recv()
            grads[into] = (grads[into].astype(F32) + got[at].astype(F32)).astype(BF)
            out_copy(k, at).start()
    for e in range(local):
        arrive(False, e)
    for k in range(2):
        grads, got = moves[k][:2]
        first_copy(k, 1, steps - 1).wait_recv()
        grads[kept] = (grads[kept].astype(F32) + got[2].astype(F32)).astype(BF)
        out_copy(k, 2).start()
    for k in range(2):
        first_copy(k, 0, moves[k][2]).wait_send()
        first_copy(k, 1, steps - 1).wait_send()
        store(k, steps - 1).wait()
        for at in range(3):
            out_copy(k, at).wait()
    keep_result(local - 1).wait()
    for e in range(local):
        leave(True, e)
        leave(False, e)


def run_experts(x_send, raw, weight_in, weight_out, wr, copies):
    ranks, local, cap, width = x_send.shape
    rows = ranks * cap
    hidden = weight_in.shape[2]
    chunk = hidden // copies
    experts = wr.shape[1]
    vmem = pl.BlockSpec(memory_space=pltpu.VMEM)
    hbm = pl.BlockSpec(memory_space=pl.ANY)
    block = (ranks, cap, width)
    dma = pltpu.SemaphoreType.DMA
    return pl.pallas_call(
        functools.partial(experts_kernel, ranks, copies),
        in_specs=[hbm, vmem, hbm, hbm, vmem],
        out_specs=(hbm, hbm, vmem) + (hbm,) * 4,
        out_shape=(
            jax.ShapeDtypeStruct((local,) + block, BF),
            jax.ShapeDtypeStruct(x_send.shape, BF),
            jax.ShapeDtypeStruct((experts, width), F32),
            jax.ShapeDtypeStruct((3, width, chunk), BF),
            jax.ShapeDtypeStruct((2, width, chunk), BF),
            jax.ShapeDtypeStruct((3, chunk, width), BF),
            jax.ShapeDtypeStruct((2, chunk, width), BF),
        ),
        scratch_shapes=[
            pltpu.VMEM((local,) + block, BF),
            pltpu.VMEM((local,) + block, BF),
            pltpu.VMEM((2, width, chunk), BF),
            pltpu.VMEM((2, chunk, width), BF),
            pltpu.VMEM((copies + 2, width, chunk), BF),
            pltpu.VMEM((copies + 2, chunk, width), BF),
            pltpu.VMEM((3, width, chunk), BF),
            pltpu.VMEM((3, chunk, width), BF),
            pltpu.VMEM((rows, width), BF),
            pltpu.VMEM((rows, experts), F32),
            pltpu.VMEM((rows, width), F32),
            pltpu.VMEM((rows, width), F32),
            pltpu.VMEM(block, BF),
            dma((local, ranks)),
            dma((local, ranks)),
            dma((local, ranks)),
            dma((local, ranks)),
            dma((2, 2)),
            dma((2, 3)),
            dma((2, 3)),
            dma,
            dma((2, 4)),
        ],
        compiler_params=params(collective_id=0, has_side_effects=True),
        cost_estimate=pl.CostEstimate(
            flops=12 * local * rows * width * hidden,
            bytes_accessed=8 * local * width * hidden,
            transcendentals=local * rows * hidden,
        ),
        name="experts",
    )(x_send, raw, weight_in, weight_out, wr)


PIECES = 4


def sums_inside(width, copies, ranks):
    return ranks == 2 * copies and width % (16 * copies * copies) == 0


def backward_kernel(
    head_dim, seq_len, buckets, copies, ranks,
    tokens, gain_one, normed, ids, q, k, v, att, inv, soft, wq, wk, wv,
    back, slot_col, residual, grad, gain_two, wo, gate, router,
    returned, next_in, next_out,
    grad_tokens_o, mixed_o, pieces_o, small_o, got_in_o, got_out_o,
    score_sums, normed_sum, low_res, grad_att, grad_gain_two, results, parts, part_got, level_got, level_sum, last_got, last_sum,
    small_s, small_all, small_core, small_line, small_plane, small_half,
    r_ss, r_rs, c_ss, c_rs, l1_ss, l1_rs, l2_ss, l2_rs, g2_ss, g2_rs, g1_ss, g1_rs, h_ss, h_rs,
    own_sem, w_ss, w_rs, m_ss, m_rs,
):
    step = pl.program_id(0)
    steps = pl.num_programs(0)
    rows, width = tokens.shape
    group = wq.shape[1]
    seqs = rows // seq_len
    local = returned.shape[0]
    bits = bits_of(copies)
    me = lax.axis_index("expert")
    copy = lax.axis_index("dp")
    core = me % 2
    line = me // 2
    mesh_id = pl.DeviceIdType.MESH
    inside = sums_inside(width, copies, ranks)
    count = copies

    def remote(source, target, sends, recvs, device):
        return pltpu.make_async_remote_copy(
            src_ref=source, dst_ref=target, send_sem=sends, recv_sem=recvs,
            device_id=device, device_id_type=mesh_id,
        )


    def result_copy(e, at, peer):
        return remote(
            returned.at[e, peer], results.at[at, e], r_ss.at[e, peer], r_rs.at[e, at],
            {"expert": peer},
        )

    def result_stay(e):
        return pltpu.make_async_copy(returned.at[e, me], results.at[me, e], r_rs.at[e, me])

    def results_start(e):
        def one(d, carry):
            result_copy(e, me, (me + d) % ranks).start()
            return carry

        lax.fori_loop(1, ranks, one, 0)
        result_stay(e).start()

    def results_wait(e):
        def one(d, carry):
            peer = (me + ranks - d) % ranks
            result_copy(e, peer, peer).wait_recv()
            result_copy(e, me, (me + d) % ranks).wait_send()
            return carry

        lax.fori_loop(1, ranks, one, 0)
        result_stay(e).wait()


    moves = (
        (next_in, got_in_o, bits[0], bits[1]),
        (next_out, got_out_o, bits[1], bits[0]),
    )
    shares = 3 * PARTS

    def share_copy(which, n, late):
        source, target, first, second = moves[which]
        at = 2 if late else (n - PARTS) // PARTS
        height = source.shape[1] // PARTS
        span = pl.ds(pl.multiple_of((n % PARTS) * height, 16), height)
        return remote(
            source.at[at, span], target.at[at, span], w_ss.at[which, n], w_rs.at[which, n],
            {"dp": flip(copy, first if late else second)},
        )

    def pump(first, count):
        def one(n, carry):
            @pl.when(n < PARTS)
            def _():
                for which in range(2):
                    share_copy(which, n, True).start()

            @pl.when(n >= PARTS)
            def _():
                for which in (1, 0):
                    share_copy(which, n, False).start()

            return carry

        if count:
            lax.fori_loop(first, jnp.minimum(first + count, shares), one, 0)

    def shares_end():
        def late(n, carry):
            for which in range(2):
                share_copy(which, n, True).wait()
            return carry

        def rest(n, carry):
            for which in range(2):
                share_copy(which, n, False).wait()
            return carry

        lax.fori_loop(0, PARTS, late, 0)
        lax.fori_loop(PARTS, shares, rest, 0)

    def paced(at):
        for p, stage in PLAN.get(at, ()):
            if p == "ret":
                results_start(stage)
            elif inside:
                if p == "small":
                    small_stages[stage]()
                else:
                    stages[stage](p)


    def levels(p):
        along = (line, lambda i: {"expert": 2 * i + core})
        across = (copy, lambda i: {"dp": i})
        return (along, across) if p in ALONG_FIRST else (across, along)

    def core_copy(p):
        return remote(
            parts.at[p, 1 - core], part_got.at[p], c_ss.at[p], c_rs.at[p], {"expert": me + 1 - 2 * core}
        )

    def first_copy(p, peer, at):
        (_, device), _ = levels(p)
        return remote(
            parts.at[p, core, pl.ds(peer * count, count)], level_got.at[p, at],
            l1_ss.at[p, peer], l1_rs.at[p, at], device(peer),
        )

    def second_copy(p, peer, at):
        _, (_, device) = levels(p)
        return remote(
            level_sum.at[p, peer], last_got.at[p, at], l2_ss.at[p, peer], l2_rs.at[p, at],
            device(peer),
        )

    def give_second(p, peer, at):
        (mine, _), (_, device) = levels(p)
        return remote(
            last_sum.at[p], pieces_o.at[p, core, mine * count + at],
            g2_ss.at[p, peer], g2_rs.at[p, at], device(peer),
        )

    def give_own(p):
        (mine, _), (own, _) = levels(p)
        return pltpu.make_async_copy(
            last_sum.at[p], pieces_o.at[p, core, mine * count + own], own_sem.at[p]
        )

    def give_first(p, peer, at):
        (_, device), _ = levels(p)
        block = pieces_o.at[p, core, pl.ds(at * count, count)]
        return remote(block, block, g1_ss.at[p, peer], g1_rs.at[p, at], device(peer))

    def give_core(p, half):
        block = pieces_o.at[p, half]
        return remote(block, block, h_ss.at[p], h_rs.at[p], {"expert": me + 1 - 2 * core})

    def others(own):
        return [(own + d) % count for d in range(1, count)]

    def piece_0(p):
        core_copy(p).start()

    def piece_1(p):
        (own, _), _ = levels(p)
        core_copy(p).wait_recv()
        parts[p, core] = (parts[p, core].astype(F32) + part_got[p].astype(F32)).astype(BF)
        for peer in others(own):
            first_copy(p, peer, own).start()

    def piece_2(p):
        (first, _), (own, _) = levels(p)
        total = parts[p, core, pl.ds(first * count, count)].astype(F32)
        for peer in others(first):
            first_copy(p, peer, peer).wait_recv()
            total += level_got[p, peer].astype(F32)
        level_sum[p] = total.astype(BF)
        for peer in others(own):
            second_copy(p, peer, own).start()

    def piece_3(p):
        _, (own, _) = levels(p)
        total = level_sum[p, own].astype(F32)
        for peer in others(own):
            second_copy(p, peer, peer).wait_recv()
            total += last_got[p, peer].astype(F32)
        last_sum[p] = total.astype(BF)
        for peer in others(own):
            give_second(p, peer, own).start()
        give_own(p).start()

    def piece_4(p):
        (first, _), (own, _) = levels(p)
        for peer in others(own):
            give_second(p, peer, peer).wait_recv()
        give_own(p).wait()
        for peer in others(first):
            give_first(p, peer, first).start()

    def piece_5(p):
        (first, _), _ = levels(p)
        for peer in others(first):
            give_first(p, peer, peer).wait_recv()
        give_core(p, core).start()

    def piece_6(p):
        (first, _), (own, _) = levels(p)
        give_core(p, 1 - core).wait_recv()
        core_copy(p).wait_send()
        give_core(p, core).wait_send()
        for peer in others(first):
            first_copy(p, peer, first).wait_send()
            give_first(p, peer, first).wait_send()
        for peer in others(own):
            second_copy(p, peer, own).wait_send()
            give_second(p, peer, own).wait_send()

    stages = (piece_0, piece_1, piece_2, piece_3, piece_4, piece_5, piece_6)


    half = small_half.shape[0]

    def small_copy(stage, peer, at):
        if stage == 0:
            source, target, device = small_s, small_core, {"expert": me + 1 - 2 * core}
        elif stage == 1:
            source, target, device = small_half, small_line.at[at], {"expert": 2 * peer + core}
        elif stage == 2:
            source, target, device = small_half, small_plane.at[at], {"dp": peer}
        else:
            source = small_all.at[pl.ds(pl.multiple_of(core * half, 8), half)]
            target, device = source, {"expert": me + 1 - 2 * core}
        return remote(source, target, m_ss.at[stage, peer], m_rs.at[stage, at], device)

    def small_0():
        small_copy(0, 0, 0).start()

    def small_1():
        small_copy(0, 0, 0).wait()
        span = pl.ds(pl.multiple_of(core * half, 8), half)
        small_half[...] = small_s[span] + small_core[span]
        for peer in others(line):
            small_copy(1, peer, line).start()

    def small_2():
        total = small_half[...]
        for peer in others(line):
            small_copy(1, peer, peer).wait_recv()
            total += small_line[peer]
        for peer in others(line):
            small_copy(1, peer, line).wait_send()
        small_half[...] = total
        for peer in others(copy):
            small_copy(2, peer, copy).start()

    def small_3():
        total = small_half[...]
        for peer in others(copy):
            small_copy(2, peer, peer).wait_recv()
            total += small_plane[peer]
        small_all[pl.ds(pl.multiple_of(core * half, 8), half)] = total
        small_copy(3, 0, 0).start()

    def small_4():
        for peer in others(copy):
            small_copy(2, peer, copy).wait_send()
        small_copy(3, 0, 0).wait()

    small_stages = (small_0, small_1, small_2, small_3, small_4)

    @pl.when(step == 0)
    def _():
        barrier = pltpu.get_barrier_semaphore()

        def greet(axis, own, size):
            def one(d, carry):
                pl.semaphore_signal(
                    barrier, inc=1, device_id={axis: (own + d) % size}, device_id_type=mesh_id
                )
                return carry

            lax.fori_loop(1, size, one, 0)

        greet("expert", me, ranks)
        greet("dp", copy, copies)
        pl.semaphore_wait(barrier, ranks + copies - 2)
        pump(0, PUMP_FIRST)
        paced("start")


        height = rows // 4

        def block(i, gain):
            pump(PUMP_FIRST + PUMP_MIDDLE * i, PUMP_MIDDLE)
            span = pl.ds(pl.multiple_of(i * height, height), height)
            pick = (slot_col[span, :] == iota((height, back.shape[0]), 1)).astype(BF)
            upstream = dot_nn(pick, back[...])
            values = residual[span, :]
            factor = lax.rsqrt(jnp.mean(values * values, axis=-1, keepdims=True) + EPSILON)
            weighted = upstream * gain_two[...]
            mean = jnp.mean(weighted * values, axis=-1, keepdims=True)
            grad_residual = (
                grad[span, :].astype(F32)
                + factor * weighted
                - values * (factor * factor * factor) * mean
            )
            grad_tokens_o[span, :] = grad_residual
            low = grad_residual.astype(BF)
            low_res[span, :] = low
            grad_att[span, :] = dot_nt(low, wo[...]).astype(BF)
            return gain + jnp.sum(upstream * values * factor, axis=0, keepdims=True)

        grad_gain_two[...] = lax.fori_loop(0, 4, block, jnp.zeros((1, width), F32))
        grad_wo = dot_tn(att[...], low_res[...]).astype(BF)
        for side in range(2):
            across = slice(side * (width // 2), (side + 1) * (width // 2))
            parts[PIECES - 1, side] = grad_wo[:, across].reshape(parts.shape[2:])
        paced("middle")


    per_step = group // head_dim
    here = pl.ds(pl.multiple_of(step * group, group), group)
    lane = iota((seq_len, group), 1)
    grads = [[None] * seqs for _ in range(3)]
    for seq in range(seqs):
        span = slice(seq * seq_len, (seq + 1) * seq_len)
        low_grad = (grad_att[span, here].astype(F32) * inv[span, :]).astype(BF)
        inner = low_grad.astype(F32) * att[span, here].astype(F32)
        grad_t = low_grad.T
        query_t = q[span, :].T
        query_sum = None
        key_rows, value_rows = [], []
        for head in range(per_step):
            mine = (lane >= head * head_dim) & (lane < (head + 1) * head_dim)
            own = slice(head * head_dim, (head + 1) * head_dim)
            grad_probs = dot_nt(jnp.where(mine, low_grad, 0).astype(BF), v[span, :])
            row_inner = jnp.sum(jnp.where(mine, inner, 0.0), axis=-1, keepdims=True)
            low_soft = soft[head, seq]
            scores = (low_soft.astype(F32) * (grad_probs - row_inner)).astype(BF)
            at = step * per_step + head
            if seq == 0:
                score_sums[at] = scores
            else:
                score_sums[at] = (score_sums[at].astype(F32) + scores.astype(F32)).astype(BF)
            value_rows.append(dot_nn(grad_t[own, :], low_soft))
            key_rows.append(dot_nn(query_t[own, :], scores))
            grad_query = dot_nn(scores, k[span, :])
            query_sum = grad_query if head == 0 else jnp.where(mine, grad_query, query_sum)
        grads[0][seq] = (query_sum * 0.125).astype(BF)
        grads[1][seq] = (jnp.concatenate(key_rows, axis=0).T * 0.125).astype(BF)
        grads[2][seq] = jnp.concatenate(value_rows, axis=0).T.astype(BF)
        if seq < seqs - 1:
            pump(PUMP_FIRST + 4 * PUMP_MIDDLE + 2 * PUMP_STEP * step, PUMP_STEP)
            for after in range(width // group):
                if (after, 0) in PLAN:
                    @pl.when(step == after)
                    def _():
                        paced((after, 0))
    grads = jnp.concatenate([jnp.concatenate(one, axis=0) for one in grads], axis=1)
    weights = jnp.concatenate([wq[...], wk[...], wv[...]], axis=1)
    parts[step // 2, step % 2] = dot_tn(normed[...], grads).astype(BF).reshape(parts.shape[2:])
    part = dot_nt(grads, weights)

    @pl.when(step == 0)
    def _():
        normed_sum[...] = part

    @pl.when(step > 0)
    def _():
        normed_sum[...] += part

    pump(PUMP_FIRST + 4 * PUMP_MIDDLE + 2 * PUMP_STEP * step + PUMP_STEP, PUMP_STEP)
    for after in range(width // group):
        if (after, 1) in PLAN:
            @pl.when(step == after)
            def _():
                paced((after, 1))

    @pl.when(step == steps - 1)
    def _():
        upstream = normed_sum[...]
        values = tokens[...].astype(F32)
        factor = lax.rsqrt(jnp.mean(values * values, axis=-1, keepdims=True) + EPSILON)
        weighted = upstream * gain_one[...]
        mean = jnp.mean(weighted * values, axis=-1, keepdims=True)
        gain = jnp.sum(upstream * values * factor, axis=0, keepdims=True)
        grad_tokens_o[...] = (
            grad_tokens_o[...]
            + factor * weighted
            - values * (factor * factor * factor) * mean
        )
        pump(PUMP_FIRST + 4 * PUMP_MIDDLE + 2 * PUMP_STEP * (width // group), PUMP_LAST)
        paced("norm")
        heads = score_sums.shape[0]
        rows_at = 16

        def add(block, sums):
            at = pl.multiple_of(block * rows_at, rows_at)
            own = ids[pl.ds(at, rows_at), :]
            hot = own[:, None, :] == iota((rows_at, buckets, seq_len), 1)
            hot = hot.astype(BF).reshape(rows_at * buckets, seq_len)
            scores = score_sums[:, pl.ds(at, rows_at), :].reshape(heads * rows_at, seq_len)
            return sums + dot_nt(hot, scores)

        sums = jnp.zeros((rows_at * buckets, heads * rows_at), F32)
        sums = lax.fori_loop(0, seq_len // rows_at, add, sums)
        sums = sums.reshape(rows_at, buckets, heads * rows_at)
        across = iota(sums.shape, 2)
        keep = iota(sums.shape, 0) == across % rows_at
        sums = jnp.sum(jnp.where(keep, sums, 0.0), axis=0)
        into = iota((heads * rows_at, LANES), 0) // rows_at == iota((heads * rows_at, LANES), 1)
        bucket = lax.dot_general(
            sums, into.astype(F32), (((1,), (0,)), ((), ())),
            precision=lax.Precision.HIGHEST, preferred_element_type=F32,
        )
        small_s[...] = jnp.zeros_like(small_s)
        tiles = width // LANES
        experts = router.shape[0]
        for tile in range(tiles):
            cols = slice(tile * LANES, (tile + 1) * LANES)
            small_s[tile:tile + 1, :] = gain[:, cols]
            small_s[8 + tile:9 + tile, :] = grad_gain_two[:, cols]
            at = 16 + buckets + tile * experts
            small_s[at:at + experts, :] = router[:, cols]
        small_s[16:16 + buckets, :] = bucket
        pump(PUMP_FIRST + 4 * PUMP_MIDDLE + 2 * PUMP_STEP * (width // group) + PUMP_LAST, shares)
        paced("bucket")
        small_o[...] = small_all[...] if inside else small_s[...]
        for e in range(local):
            results_wait(e)

        height = rows // 4

        def mix(i, carry):
            span = pl.ds(pl.multiple_of(i * height, height), height)
            pick = (slot_col[span, :] == iota((height, back.shape[0]), 1)).astype(BF)
            combined = dot_nn(pick, results[...].reshape(back.shape))
            mixed_o[span, :] = (residual[span, :] + gate[span, :] * combined).astype(BF)
            return carry

        lax.fori_loop(0, 4, mix, 0)
        paced("mixed")
        shares_end()
        if not inside:
            for p in range(PIECES):
                out = pltpu.make_async_copy(parts.at[p], pieces_o.at[p], own_sem.at[p])
                out.start()
                out.wait()


ALONG_FIRST = (3, 0)
PARTS = 12
PUMP_FIRST, PUMP_MIDDLE, PUMP_STEP, PUMP_LAST = 4, 1, 2, 2
PLAN = {
    "start": (("ret", 0),),
    (0, 0): ((3, 0),),
    (0, 1): ((3, 1),),
    (1, 1): ((0, 0),),
    (2, 0): ((0, 1), (3, 2)),
    (3, 0): ((3, 3), ("ret", 1)),
    (3, 1): ((1, 0), (1, 1)),
    (4, 0): ((0, 2), (3, 4)),
    (4, 1): ((1, 2),),
    (5, 1): ((3, 5), (2, 0), (2, 1)),
    "norm": ((0, 3), (1, 3)),
    "bucket": (
        (2, 2), ("small", 0), ("small", 1), (2, 3), ("small", 2), (2, 4), (0, 4), ("small", 3), (1, 4),
        ("small", 4),
    ),
    "mixed": ((2, 5), (0, 5), (1, 5), (2, 6), (3, 6), (0, 6), (1, 6)),
}


def backward(
    tokens, gain_one, normed, bucket_ids, q, k, v, att, inv, soft, weights,
    back, slot_col, residual, grad, gain_two, wo, gate, router, returned, shares,
    head_dim, buckets, copies, ranks,
):
    rows, width = tokens.shape
    seq_len = bucket_ids.shape[0]
    heads, seqs = soft.shape[:2]
    local = returned.shape[0]
    experts = router.shape[0]
    chunk = shares[0].shape[2]
    slots = back.shape[0]
    group = LANES
    steps = width // group
    per_step = heads // steps
    inside = sums_inside(width, copies, ranks)
    chips = copies * copies if inside else 1
    block = (width // chips, width // 2)
    small_rows = -(-(16 + buckets + width // LANES * experts) // 16) * 16
    cols = lambda shape: pl.BlockSpec(shape, lambda g: (0, g))
    once = lambda shape: pl.BlockSpec(
        shape, lambda g: (0,) * len(shape), pipeline_mode=pl.Buffered(1)
    )
    hbm = pl.BlockSpec(memory_space=pl.ANY)
    dma = pltpu.SemaphoreType.DMA
    each = dma((PIECES, copies))
    return pl.pallas_call(
        functools.partial(backward_kernel, head_dim, seq_len, buckets, copies, ranks),
        grid=(steps,),
        in_specs=[
            once((rows, width)),
            once((1, width)),
            once((rows, width)),
            once((seq_len, seq_len)),
            cols((rows, group)),
            cols((rows, group)),
            cols((rows, group)),
            once((rows, width)),
            cols((rows, group)),
            pl.BlockSpec((per_step, seqs, seq_len, seq_len), lambda g: (g, 0, 0, 0)),
            cols((width, group)),
            cols((width, group)),
            cols((width, group)),
            once((slots, width)),
            once((rows, 1)),
            once((rows, width)),
            once((rows, width)),
            once((1, width)),
            once((width, width)),
            once((rows, 1)),
            once((experts, width)),
        ]
        + [hbm] * 3,
        out_specs=(
            once((rows, width)),
            once((rows, width)),
            hbm,
            once((small_rows, LANES)),
            hbm,
            hbm,
        ),
        scratch_shapes=[
            pltpu.VMEM((heads, seq_len, seq_len), BF),
            pltpu.VMEM((rows, width), F32),
            pltpu.VMEM((rows, width), BF),
            pltpu.VMEM((rows, width), BF),
            pltpu.VMEM((1, width), F32),
            pltpu.VMEM((ranks, local) + returned.shape[2:], BF),
            pltpu.VMEM((PIECES, 2, chips) + block, BF),
            pltpu.VMEM((PIECES, chips) + block, BF),
            pltpu.VMEM((PIECES, copies, copies) + block if inside else (8, LANES), BF),
            pltpu.VMEM((PIECES, copies) + block if inside else (8, LANES), BF),
            pltpu.VMEM((PIECES, copies) + block if inside else (8, LANES), BF),
            pltpu.VMEM((PIECES,) + block, BF),
            pltpu.VMEM((small_rows, LANES), F32),
            pltpu.VMEM((small_rows, LANES), F32),
            pltpu.VMEM((small_rows, LANES), F32),
            pltpu.VMEM((copies, small_rows // 2, LANES), F32),
            pltpu.VMEM((copies, small_rows // 2, LANES), F32),
            pltpu.VMEM((small_rows // 2, LANES), F32),
            dma((local, ranks)),
            dma((local, ranks)),
            dma((PIECES,)),
            dma((PIECES,)),
            each, each, each, each, each, each, each, each,
            dma((PIECES,)),
            dma((PIECES,)),
            dma((PIECES,)),
            dma((2, 3 * PARTS)),
            dma((2, 3 * PARTS)),
            dma((4, copies)),
            dma((4, copies)),
        ],
        out_shape=(
            jax.ShapeDtypeStruct((rows, width), F32),
            jax.ShapeDtypeStruct((rows, width), BF),
            jax.ShapeDtypeStruct((PIECES, 2, chips) + block, BF),
            jax.ShapeDtypeStruct((small_rows, LANES), F32),
            jax.ShapeDtypeStruct((3, width, chunk), BF),
            jax.ShapeDtypeStruct((3, chunk, width), BF),
        ),
        compiler_params=params(
            dimension_semantics=("arbitrary",), collective_id=1, has_side_effects=True
        ),
        cost_estimate=pl.CostEstimate(
            flops=2 * rows * width * (6 * width + 5 * seq_len * 4),
            bytes_accessed=50 << 20,
            transcendentals=0,
        ),
        name="backward",
    )(
        tokens, gain_one, normed, bucket_ids, q, k, v, att, inv, soft, *weights,
        back, slot_col, residual, grad, gain_two, wo, gate, router, returned, *shares,
    )


def finish_kernel(pieces, keep_in, got_in, keep_out, got_out, wq_o, wk_o, wv_o, wo_o, grad_in_o, grad_out_o):
    width = wo_o.shape[1]
    half = width // 2
    part = half // 3
    for step in range(width // part):
        block = pieces[step // 2, step % 2].astype(F32)
        for at, out in enumerate((wq_o, wk_o, wv_o)):
            out[:, step * part:(step + 1) * part] = block[:, at * part:(at + 1) * part]
    for side in range(2):
        wo_o[:, side * half:(side + 1) * half] = pieces[PIECES - 1, side].astype(F32)
    for keep, got, out in ((keep_in, got_in, grad_in_o), (keep_out, got_out, grad_out_o)):
        out[0] = keep[0].astype(F32) + got[0].astype(F32)
        out[1] = keep[1].astype(F32) + got[1].astype(F32) + got[2].astype(F32)


def finish(pieces, keep_in, got_in, keep_out, got_out):
    width, chunk = keep_in.shape[1:]
    count = 8
    pieces = pieces.reshape(PIECES, 2, width, width // 2)
    part = width // count
    rows = pl.BlockSpec((part, width), lambda i: (i, 0))
    square = jax.ShapeDtypeStruct((width, width), F32)
    by_in = lambda lead: pl.BlockSpec((lead, part, chunk), lambda i: (0, i, 0))
    by_out = lambda lead: pl.BlockSpec((lead, chunk // count, width), lambda i: (0, i, 0))
    return pl.pallas_call(
        finish_kernel,
        grid=(count,),
        in_specs=[
            pl.BlockSpec((PIECES, 2, part, width // 2), lambda i: (0, 0, i, 0)),
            by_in(2),
            by_in(3),
            by_out(2),
            by_out(3),
        ],
        out_specs=(rows, rows, rows, rows, by_in(2), by_out(2)),
        out_shape=(
            square,
            square,
            square,
            square,
            jax.ShapeDtypeStruct((2, width, chunk), F32),
            jax.ShapeDtypeStruct((2, chunk, width), F32),
        ),
        compiler_params=params(dimension_semantics=("arbitrary",)),
        cost_estimate=pl.CostEstimate(flops=1 << 20, bytes_accessed=30 << 20, transcendentals=0),
        name="finish",
    )(pieces, keep_in, got_in, keep_out, got_out)


def per_device(
    tokens,
    expert_ids,
    bucket_ids,
    attn_gain,
    ffn_gain,
    query_weight,
    key_weight,
    value_weight,
    output_weight,
    router_weight,
    bucket_bias,
    expert_in,
    expert_out,
    grad_output,
):
    tok_rows, width = tokens.shape
    buckets, heads = bucket_bias.shape
    head_dim = width // heads
    local = expert_in.shape[0]
    ranks = lax.axis_size("expert")
    copies = lax.axis_size("dp")
    experts = local * ranks
    cap = (5 * tok_rows + 4 * experts - 1) // (4 * experts)
    room = -(-cap // 16) * 16
    slots = experts * room
    per_group = 4
    groups = heads // per_group
    table = jnp.pad(bucket_bias.T, ((0, 0), (0, LANES - buckets)))
    table = table.reshape(groups, per_group, LANES)
    gains = (attn_gain.reshape(1, width), ffn_gain.reshape(1, width))

    slot_col, slot_row, grad_slots = make_slots(
        ranks, local, cap, room, expert_ids, grad_output
    )
    blocks = (ranks, local, room, width)
    grad_slots = lax.all_to_all(
        grad_slots.reshape(blocks), "expert", split_axis=0, concat_axis=0, tiled=True
    )
    (
        normed, q, k, v, att, inv, soft, residual, nf, gate, row_slots
    ) = forward(
        tokens, bucket_ids, table, gains,
        (query_weight, key_weight, value_weight, output_weight),
        router_weight, expert_ids, slot_row, slots, head_dim,
    )
    returned, back, router, next_in, keep_in, next_out, keep_out = run_experts(
        row_slots.reshape(blocks), grad_slots, expert_in, expert_out, router_weight, copies,
    )
    grad_tokens, mixed, pieces, small, got_in, got_out = backward(
        tokens, gains[0], normed, bucket_ids, q, k, v, att, inv, soft,
        (query_weight, key_weight, value_weight), back.reshape(slots, width), slot_col, residual,
        grad_output, gains[1], output_weight, gate, router, returned, (next_in, next_out),
        head_dim, buckets, copies, ranks,
    )
    if not sums_inside(width, copies, ranks):
        pieces = lax.psum(pieces.astype(F32), ("dp", "expert"))
        small = lax.psum(small, ("dp", "expert"))
    grad_wq, grad_wk, grad_wv, grad_wo, grad_expert_in, grad_expert_out = finish(
        pieces, keep_in, got_in, keep_out, got_out
    )
    tiles = width // LANES
    grad_attn_gain = small[:tiles].reshape(width)
    grad_ffn_gain = small[8:8 + tiles].reshape(width)
    grad_bucket = small[16:16 + buckets, :heads]
    at = 16 + buckets
    grad_router = small[at:at + experts * tiles].reshape(tiles, experts, LANES)
    grad_router = grad_router.transpose(0, 2, 1).reshape(width, experts)
    return (
        mixed,
        grad_tokens,
        grad_attn_gain,
        grad_ffn_gain,
        grad_wq,
        grad_wk,
        grad_wv,
        grad_wo,
        grad_router,
        grad_bucket,
        grad_expert_in,
        grad_expert_out,
    )


def solution(mesh):
    shared = P()
    rows = P(("dp", "expert"), None)
    expert = P("expert", None, None)
    return jax.shard_map(
        per_device,
        mesh=mesh,
        in_specs=(rows, rows) + (shared,) * 9 + (expert, expert, rows),
        out_specs=(rows, rows) + (shared,) * 8 + (P("expert", None, "dp"), P("expert", "dp", None)),
        check_vma=False,
    )
```

```python
import functools

import jax
import jax.numpy as jnp
from jax import lax
from jax.experimental import pallas as pl
from jax.experimental.pallas import tpu as pltpu
from jax.sharding import PartitionSpec as P

EPSILON = 1e-06
BF = jnp.bfloat16
F32 = jnp.float32
LANES = 128
VMEM_BYTES = 62 * 1024 * 1024


def dot_nn(left, right):
    return lax.dot_general(left, right, (((1,), (0,)), ((), ())), preferred_element_type=F32)


def dot_nt(left, right):
    return lax.dot_general(left, right, (((1,), (1,)), ((), ())), preferred_element_type=F32)


def dot_tn(left, right):
    return lax.dot_general(left, right, (((0,), (0,)), ((), ())), preferred_element_type=F32)


def iota(shape, axis):
    return lax.broadcasted_iota(jnp.int32, shape, axis)


def whole(shape):
    return pl.BlockSpec(shape, lambda *_: (0,) * len(shape))


def nth_far(i, size):
    return size // 2 + ((i + 1) // 2) * (2 * (i % 2) - 1)


def params(**more):
    return pltpu.CompilerParams(vmem_limit_bytes=VMEM_BYTES, **more)


def forward_kernel(
    head_dim, seq_len, cap, late_rows,
    tokens, ids, table, gain_one, gain_two, wq, wk, wv, wo, wr, ids_row, grad,
    normed_o, q_o, k_o, v_o, att_o, inv_o, soft_o, residual_o, gate_o, slot_col_o, slots_o, raw_o,
    late_o,
    slot_row, grad_slots, send_sem, recv_sem, own_sem,
):
    step = pl.program_id(0)
    rows, width = tokens.shape
    group = wq.shape[1]
    ranks, local, room = grad_slots.shape[:3]
    experts = ranks * local
    me = lax.axis_index("expert")

    early = room - late_rows

    def raw_span(e):
        return pl.ds(0, early if e else room)

    def raw_copy(e, at, peer):
        return pltpu.make_async_remote_copy(
            src_ref=grad_slots.at[peer, e, raw_span(e)],
            dst_ref=raw_o.at[at, e, raw_span(e)],
            send_sem=send_sem.at[e, peer],
            recv_sem=recv_sem.at[e, at],
            device_id={"expert": peer},
            device_id_type=pl.DeviceIdType.MESH,
        )

    def raw_stay(e):
        return pltpu.make_async_copy(
            grad_slots.at[me, e, raw_span(e)], raw_o.at[me, e, raw_span(e)], own_sem.at[e]
        )

    def late_keep(e):
        return pltpu.make_async_copy(
            grad_slots.at[:, e, pl.ds(early, room - early)], late_o.at[e - 1], own_sem.at[local + e]
        )

    def column(row):
        return jnp.broadcast_to(row, (8, rows)).T[:, :1]

    @pl.when(step == 0)
    def _():
        barrier = pltpu.get_barrier_semaphore()

        def greet(d, carry):
            pl.semaphore_signal(
                barrier, inc=1, device_id={"expert": (me + d) % ranks},
                device_id_type=pl.DeviceIdType.MESH,
            )
            return carry

        lax.fori_loop(1, ranks, greet, 0)
        hot = ids_row[...] == iota((experts, rows), 0)
        earlier = (iota((rows, rows), 0) < iota((rows, rows), 1)).astype(BF)
        counts = dot_nn(hot.astype(BF), earlier)
        place = jnp.sum(jnp.where(hot, counts, 0.0), axis=0, keepdims=True).astype(jnp.int32)
        slot = jnp.where(place < cap, ids_row[...] * room + place, -1)
        slot_row[...] = slot
        slot_col_o[...] = column(slot)
        pick = (iota((experts * room, rows), 0) == slot).astype(BF)
        grad_slots[...] = dot_nn(pick, grad[...]).astype(BF).reshape(grad_slots.shape)
        pl.semaphore_wait(barrier, ranks - 1)

        for e in range(local):
            def send(i, carry):
                raw_copy(e, me, (me + nth_far(i, ranks)) % ranks).start()
                return carry

            lax.fori_loop(0, ranks - 1, send, 0)
            raw_stay(e).start()
            if e and early < room:
                late_keep(e).start()
        x = tokens[...].astype(F32)
        factor = lax.rsqrt(jnp.mean(x * x, axis=-1, keepdims=True) + EPSILON)
        normed_o[...] = (x * factor * gain_one[...]).astype(BF)
        residual_o[...] = x

    normed = normed_o[...]
    q_o[...] = dot_nn(normed, wq[...]).astype(BF)
    k_o[...] = dot_nn(normed, wk[...]).astype(BF)
    v_o[...] = dot_nn(normed, wv[...]).astype(BF)
    lane = iota((seq_len, LANES), 1)
    per_tile = LANES // head_dim
    for tile in range(group // LANES):
        cols = slice(tile * LANES, (tile + 1) * LANES)
        gathered = [None] * (rows // seq_len)
        scaled = [None] * (rows // seq_len)
        for part in range(per_tile):
            head = tile * per_tile + part
            mine = (lane >= part * head_dim) & (lane < (part + 1) * head_dim)
            row = jnp.broadcast_to(table[0, head:head + 1, :], (seq_len, LANES))
            bias = jnp.concatenate(
                [
                    jnp.take_along_axis(
                        row, ids[:, c:c + LANES], axis=1, mode="promise_in_bounds"
                    )
                    for c in range(0, seq_len, LANES)
                ],
                axis=1,
            )
            for seq in range(rows // seq_len):
                span = slice(seq * seq_len, (seq + 1) * seq_len)
                query = jnp.where(mine, q_o[span, cols] * 0.125, 0).astype(BF)
                scores = dot_nt(query, k_o[span, cols]) + bias
                weights = jnp.exp(scores - jnp.max(scores, axis=-1, keepdims=True))
                inverse = 1.0 / jnp.sum(weights, axis=-1, keepdims=True)
                low = weights.astype(BF)
                soft_o[head, seq] = low
                out = dot_nn(low, v_o[span, cols]) * inverse
                inverse = jnp.broadcast_to(inverse, (seq_len, LANES))
                if part == 0:
                    gathered[seq], scaled[seq] = out, inverse
                else:
                    gathered[seq] = jnp.where(mine, out, gathered[seq])
                    scaled[seq] = jnp.where(mine, inverse, scaled[seq])
        for seq in range(rows // seq_len):
            span = slice(seq * seq_len, (seq + 1) * seq_len)
            att_o[span, cols] = gathered[seq].astype(BF)
            inv_o[span, cols] = scaled[seq]
    residual_o[...] += dot_nn(att_o[...], wo[...])

    @pl.when(step == pl.num_programs(0) - 1)
    def _():
        residual = residual_o[...]
        factor = lax.rsqrt(jnp.mean(residual * residual, axis=-1, keepdims=True) + EPSILON)
        low = (residual * factor * gain_two[...]).astype(BF)
        logits = dot_nt(low, wr[...])
        weights = jnp.exp(logits - jnp.max(logits, axis=-1, keepdims=True))
        probs = weights / jnp.sum(weights, axis=-1, keepdims=True)
        hot = column(ids_row[...]) == iota(logits.shape, 1)
        gate_o[...] = jnp.sum(jnp.where(hot, probs, 0.0), axis=1, keepdims=True)
        pick = (iota((slots_o.shape[0], rows), 0) == slot_row[...]).astype(BF)
        slots_o[...] = dot_nn(pick, low).astype(BF)

        for e in range(local):
            def finish(d, carry):
                peer = (me + ranks - d) % ranks
                raw_copy(e, peer, peer).wait_recv()
                raw_copy(e, me, (me + d) % ranks).wait_send()
                return carry

            lax.fori_loop(1, ranks, finish, 0)
            raw_stay(e).wait()
            if e and early < room:
                late_keep(e).wait()


def forward(
    tokens, bucket_ids, table, gains, weights, wr, ids_row, grad, blocks, late, cap, head_dim
):
    rows, width = tokens.shape
    seq_len = bucket_ids.shape[0]
    groups, per_group, _ = table.shape
    group = width // groups
    heads = groups * per_group
    seqs = rows // seq_len
    ranks, local, room = blocks[:3]
    slots = ranks * local * room
    dma = pltpu.SemaphoreType.DMA
    cols = lambda shape: pl.BlockSpec(shape, lambda g: (0, g))
    wq, wk, wv, wo = weights
    return pl.pallas_call(
        functools.partial(forward_kernel, head_dim, seq_len, cap, late),
        grid=(groups,),
        in_specs=[
            whole((rows, width)),
            whole((seq_len, seq_len)),
            pl.BlockSpec((1, per_group, LANES), lambda g: (g, 0, 0)),
            whole((1, width)),
            whole((1, width)),
            cols((width, group)),
            cols((width, group)),
            cols((width, group)),
            pl.BlockSpec((group, width), lambda g: (g, 0)),
            whole(wr.shape),
            whole((1, rows)),
            whole((rows, width)),
        ],
        out_specs=(
            whole((rows, width)),
            cols((rows, group)),
            cols((rows, group)),
            cols((rows, group)),
            cols((rows, group)),
            cols((rows, group)),
            pl.BlockSpec((per_group, seqs, seq_len, seq_len), lambda g: (g, 0, 0, 0)),
            whole((rows, width)),
            whole((rows, 1)),
            whole((rows, 1)),
            whole((slots, width)),
            pl.BlockSpec(memory_space=pl.ANY),
            pl.BlockSpec(memory_space=pl.ANY),
        ),
        scratch_shapes=[
            pltpu.VMEM((1, rows), jnp.int32),
            pltpu.VMEM(blocks, BF),
            dma((local, ranks)),
            dma((local, ranks)),
            dma((2 * local,)),
        ],
        out_shape=(
            jax.ShapeDtypeStruct((rows, width), BF),
            jax.ShapeDtypeStruct((rows, width), BF),
            jax.ShapeDtypeStruct((rows, width), BF),
            jax.ShapeDtypeStruct((rows, width), BF),
            jax.ShapeDtypeStruct((rows, width), BF),
            jax.ShapeDtypeStruct((rows, width), F32),
            jax.ShapeDtypeStruct((heads, seqs, seq_len, seq_len), BF),
            jax.ShapeDtypeStruct((rows, width), F32),
            jax.ShapeDtypeStruct((rows, 1), F32),
            jax.ShapeDtypeStruct((rows, 1), jnp.int32),
            jax.ShapeDtypeStruct((slots, width), BF),
            jax.ShapeDtypeStruct(blocks, BF),
            jax.ShapeDtypeStruct((local - 1, ranks, max(late, 16), width), BF),
        ),
        compiler_params=params(
            dimension_semantics=("arbitrary",), collective_id=2, has_side_effects=True
        ),
        cost_estimate=pl.CostEstimate(
            flops=2 * rows * width * (4 * width + 2 * seq_len * 4),
            bytes_accessed=40 << 20,
            transcendentals=heads * rows * seq_len,
        ),
        name="forward",
    )(tokens, bucket_ids, table, *gains, wq, wk, wv, wo, wr, ids_row, grad)


LATE_TENTHS = 6


def bits_of(size):
    return [1 << i for i in range(size.bit_length() - 1)]


def flip(index, bit):
    return index + bit * (1 - 2 * ((index // bit) % 2))


def flip_all(index, mask, bits):
    for bit in bits:
        index = jnp.where((mask // bit) % 2 == 1, flip(index, bit), index)
    return index


def experts_kernel(
    ranks, copies, late,
    x_send, raw_i, late_i, weight_in, weight_out, wr,
    returned_o, back_o, router_o, next_in_o, keep_in_o, next_out_o, keep_out_o,
    x_recv, raw, back_send, win, wout, grads_in, grads_out, got_in, got_out,
    scaled, probs_s, back_sum, result_sum, result,
    x_ss, x_rs, b_ss, b_rs, l_ss, l_rs, raw_sem, w_sem, first_ss, first_rs, result_sem, out_sem,
):
    local, cap, width = x_send.shape[1:]
    rows = ranks * cap
    chunk = win.shape[2]
    steps = copies
    bits = bits_of(copies)
    orders = (bits, bits[::-1])
    me = lax.axis_index("expert")
    copy = lax.axis_index("dp")
    mesh_id = pl.DeviceIdType.MESH

    barrier = pltpu.get_barrier_semaphore()

    def greet(d, carry):
        pl.semaphore_signal(
            barrier, inc=1, device_id={"expert": (me + d) % ranks}, device_id_type=mesh_id
        )
        return carry

    lax.fori_loop(1, ranks, greet, 0)
    for bit in bits:
        pl.semaphore_signal(
            barrier, inc=1, device_id={"dp": flip(copy, bit)}, device_id_type=mesh_id
        )

    def load(s):
        e, j = s // steps, steps - 1 - s % steps
        at = pl.multiple_of(flip_all(copy, j, bits) * chunk, chunk)
        return (
            pltpu.make_async_copy(
                weight_in.at[e, :, pl.ds(at, chunk)], win.at[s % 2], w_sem.at[0, s % 2]
            ),
            pltpu.make_async_copy(
                weight_out.at[e, pl.ds(at, chunk), :], wout.at[s % 2], w_sem.at[1, s % 2]
            ),
        )

    for one in load(0):
        one.start()
    pl.semaphore_wait(barrier, ranks - 1 + len(bits))


    early = cap - late

    def raw_load(e):
        span = pl.ds(0, early if e else cap)
        return pltpu.make_async_copy(
            raw_i.at[:, e, span], raw.at[e, :, span], raw_sem.at[e]
        )

    def row_copy(out, e, at, peer):
        if out is None:
            source = late_i.at[e - 1, peer]
            target, sends, recvs = raw.at[e, at, pl.ds(early, late)], l_ss, l_rs
        elif out:
            source, target, sends, recvs = x_send.at[peer, e], x_recv.at[e, at], x_ss, x_rs
        else:
            source, target, sends, recvs = back_send.at[e, peer], back_o.at[at, e], b_ss, b_rs
        return pltpu.make_async_remote_copy(
            src_ref=source,
            dst_ref=target,
            send_sem=sends.at[e, peer],
            recv_sem=recvs.at[e, at],
            device_id={"expert": peer},
            device_id_type=mesh_id,
        )

    def stay(out, e):
        if out is None:
            return pltpu.make_async_copy(
                late_i.at[e - 1, me], raw.at[e, me, pl.ds(early, late)], l_rs.at[e, me]
            )
        if out:
            return pltpu.make_async_copy(x_send.at[me, e], x_recv.at[e, me], x_rs.at[e, me])
        return pltpu.make_async_copy(back_send.at[e, me], back_o.at[me, e], b_rs.at[e, me])

    def send(out, e):
        def one(i, carry):
            row_copy(out, e, me, (me + nth_far(i, ranks)) % ranks).start()
            return carry

        lax.fori_loop(0, ranks - 1, one, 0)
        stay(out, e).start()

    def arrive(out, e):
        def one(d, carry):
            peer = (me + ranks - d) % ranks
            row_copy(out, e, peer, peer).wait_recv()
            return carry

        lax.fori_loop(1, ranks, one, 0)
        stay(out, e).wait()

    def leave(out, e):
        def one(d, carry):
            row_copy(out, e, me, (me + d) % ranks).wait_send()
            return carry

        lax.fori_loop(1, ranks, one, 0)

    moves = (
        (grads_in, got_in, bits[0], next_in_o, keep_in_o),
        (grads_out, got_out, bits[1], next_out_o, keep_out_o),
    )
    spare, kept = steps, steps + 1

    def first_copy(k, e, j):
        grads, got, bit = moves[k][:3]
        at = 2 if e else (0 if j == steps - 1 else 1)
        return pltpu.make_async_remote_copy(
            src_ref=grads.at[spare if e else j],
            dst_ref=got.at[at],
            send_sem=first_ss.at[k, at],
            recv_sem=first_rs.at[k, at],
            device_id={"dp": flip(copy, bit)},
            device_id_type=mesh_id,
        )

    def store(k, t):
        grads, _, _, following, keep = moves[k]
        target = keep.at[1] if t == steps - 1 else following.at[2]
        return pltpu.make_async_copy(grads.at[steps - 1], target, out_sem.at[k, 0])

    def out_copy(k, at):
        grads, _, bit, following, keep = moves[k]
        source, target = (
            (grads.at[steps - 1 - bit], following.at[0]),
            (grads.at[0], keep.at[0]),
            (grads.at[kept], following.at[1]),
        )[at]
        return pltpu.make_async_copy(source, target, out_sem.at[k, 1 + at])

    def keep_result(e):
        return pltpu.make_async_copy(result, returned_o.at[e], result_sem)

    send(True, 0)
    for e in range(local):
        raw_load(e).start()
    router_o[...] = jnp.zeros_like(router_o)

    def body(s, carry):
        e, t = s // steps, s % steps
        j = steps - 1 - t

        @pl.when(s + 1 < local * steps)
        def _():
            for one in load(s + 1):
                one.start()

        @pl.when(t == 0)
        def _():
            arrive(True, e)

            @pl.when(e == 0)
            def _():
                raw_load(0).wait()
                for other in range(1, local):
                    if late:
                        send(None, other)
                    send(True, other)

            @pl.when(e > 0)
            def _():
                raw_load(1).wait()
                if late:
                    arrive(None, e)

            logits = dot_nt(x_recv[e].reshape(rows, width), wr[...])
            weights = jnp.exp(logits - jnp.max(logits, axis=-1, keepdims=True))
            probs = weights / jnp.sum(weights, axis=-1, keepdims=True)
            probs_s[...] = probs
            hot = iota(logits.shape, 1) == me * local + e
            gate = jnp.sum(jnp.where(hot, probs, 0.0), axis=1, keepdims=True)

            scaled[...] = (gate * raw[e].reshape(rows, width).astype(F32)).astype(BF)
            back_sum[...] = jnp.zeros_like(back_sum)
            result_sum[...] = jnp.zeros_like(result_sum)

        for one in load(s):
            one.wait()

        late_at = [steps - 1 - moves[k][2] for k in range(2)]
        slots = [
            jnp.where(
                e == 0, j, jnp.where(t == 0, spare, jnp.where(j == late_at[k], kept, steps - 1))
            )
            for k in range(2)
        ]
        for k in range(2):
            bit = moves[k][2]

            @pl.when((e > 0) & (j == bit))
            def _():
                first_copy(k, 0, steps - 1).wait_send()

            @pl.when((e > 0) & (t == steps - 1))
            def _():
                store(k, 0).wait()

        own_in, own_out = win[s % 2], wout[s % 2]
        taken = x_recv[e].reshape(rows, width)
        grads = scaled[...]
        pre = dot_nn(taken, own_in)
        grad_hidden = dot_nt(grads, own_out)
        scale = 0.7978845608028654
        square = pre * pre
        bent = jnp.tanh(scale * (pre + 0.044715 * (pre * square)))
        half = 0.5 * (1.0 + bent)
        hidden = (pre * half).astype(BF)
        slope = half + (0.5 * scale) * pre * (1.0 - bent * bent) * (1.0 + 0.134145 * square)
        grad_pre = (grad_hidden * slope).astype(BF)
        grads_in[slots[0]] = dot_tn(taken, grad_pre).astype(BF)
        grads_out[slots[1]] = dot_tn(hidden, grads).astype(BF)

        for k in range(2):
            bit = moves[k][2]
            for at in (steps - 1, bit):
                @pl.when((e == 0) & (j == at))
                def _():
                    first_copy(k, 0, at).start()

            @pl.when((e > 0) & (t == 0))
            def _():
                first_copy(k, 1, steps - 1).start()

            @pl.when((e > 0) & (j == bit))
            def _():
                store(k, 0).start()

            @pl.when((e > 0) & (t == steps - 1))
            def _():
                store(k, steps - 1).start()

        result_sum[...] += dot_nn(hidden, own_out)
        back_sum[...] += dot_nt(grad_pre, own_in)

        @pl.when(t == steps - 1)
        def _():
            returned = result_sum[...].astype(BF)

            @pl.when(e > 0)
            def _():
                keep_result(e - 1).wait()

            result[...] = returned.reshape(result.shape)
            keep_result(e).start()
            probs = probs_s[...]
            hot = iota(probs.shape, 1) == me * local + e
            gate = jnp.sum(jnp.where(hot, probs, 0.0), axis=1, keepdims=True)

            grad_gate = jnp.sum(
                raw[e].reshape(rows, width).astype(F32) * returned.astype(F32), axis=1, keepdims=True
            )
            slope = jnp.where(hot, 1.0, 0.0) - gate
            grad_logits = (probs * slope * grad_gate).astype(BF)
            router_o[...] += dot_tn(grad_logits, x_recv[e].reshape(rows, width))
            back = (back_sum[...] + dot_nn(grad_logits, wr[...])).astype(BF)
            back_send[e] = back.reshape(ranks, cap, width)
            send(False, e)

        return carry

    lax.fori_loop(0, local * steps, body, 0)

    for at in range(2):
        for k in range(2):
            grads, got, bit = moves[k][:3]
            into = (steps - 1 - bit, 0)[at]
            first_copy(k, 0, (steps - 1, bit)[at]).wait_recv()
            grads[into] = (grads[into].astype(F32) + got[at].astype(F32)).astype(BF)
            out_copy(k, at).start()
    for e in range(local):
        arrive(False, e)
    for k in range(2):
        grads, got = moves[k][:2]
        first_copy(k, 1, steps - 1).wait_recv()
        grads[kept] = (grads[kept].astype(F32) + got[2].astype(F32)).astype(BF)
        out_copy(k, 2).start()
    for k in range(2):
        first_copy(k, 0, moves[k][2]).wait_send()
        first_copy(k, 1, steps - 1).wait_send()
        store(k, steps - 1).wait()
        for at in range(3):
            out_copy(k, at).wait()
    keep_result(local - 1).wait()
    for e in range(local):
        leave(True, e)
        leave(False, e)
        if e and late:
            leave(None, e)


def run_experts(x_send, raw, late_rows, late, weight_in, weight_out, wr, copies):
    ranks, local, cap, width = x_send.shape
    rows = ranks * cap
    hidden = weight_in.shape[2]
    chunk = hidden // copies
    experts = wr.shape[0]
    vmem = pl.BlockSpec(memory_space=pltpu.VMEM)
    hbm = pl.BlockSpec(memory_space=pl.ANY)
    block = (ranks, cap, width)
    dma = pltpu.SemaphoreType.DMA
    return pl.pallas_call(
        functools.partial(experts_kernel, ranks, copies, late),
        in_specs=[hbm, hbm, hbm, hbm, hbm, vmem],
        out_specs=(hbm, hbm, vmem) + (hbm,) * 4,
        out_shape=(
            jax.ShapeDtypeStruct((local,) + block, BF),
            jax.ShapeDtypeStruct(x_send.shape, BF),
            jax.ShapeDtypeStruct((experts, width), F32),
            jax.ShapeDtypeStruct((3, width, chunk), BF),
            jax.ShapeDtypeStruct((2, width, chunk), BF),
            jax.ShapeDtypeStruct((3, chunk, width), BF),
            jax.ShapeDtypeStruct((2, chunk, width), BF),
        ),
        scratch_shapes=[
            pltpu.VMEM((local,) + block, BF),
            pltpu.VMEM((local,) + block, BF),
            pltpu.VMEM((local,) + block, BF),
            pltpu.VMEM((2, width, chunk), BF),
            pltpu.VMEM((2, chunk, width), BF),
            pltpu.VMEM((copies + 2, width, chunk), BF),
            pltpu.VMEM((copies + 2, chunk, width), BF),
            pltpu.VMEM((3, width, chunk), BF),
            pltpu.VMEM((3, chunk, width), BF),
            pltpu.VMEM((rows, width), BF),
            pltpu.VMEM((rows, experts), F32),
            pltpu.VMEM((rows, width), F32),
            pltpu.VMEM((rows, width), F32),
            pltpu.VMEM(block, BF),
            dma((local, ranks)),
            dma((local, ranks)),
            dma((local, ranks)),
            dma((local, ranks)),
            dma((local, ranks)),
            dma((local, ranks)),
            dma((local,)),
            dma((2, 2)),
            dma((2, 3)),
            dma((2, 3)),
            dma,
            dma((2, 4)),
        ],
        compiler_params=params(collective_id=0, has_side_effects=True),
        cost_estimate=pl.CostEstimate(
            flops=12 * local * rows * width * hidden,
            bytes_accessed=8 * local * width * hidden,
            transcendentals=local * rows * hidden,
        ),
        name="experts",
    )(x_send, raw, late_rows, weight_in, weight_out, wr)


PIECES = 4


def sums_inside(width, copies, ranks):
    return ranks == 2 * copies and width % (16 * copies * copies) == 0


def backward_kernel(
    head_dim, seq_len, buckets, copies, ranks,
    tokens_i, gain_one, normed_i, ids_i, q, k, v, att_i, inv, soft, wq, wk, wv,
    back_i, slot_col_i, residual_i, grad_i, gain_two, wo_i, gate_i, router,
    returned, next_in, next_out,
    grad_tokens_o, mixed_o, pieces_o, small_o, got_in_o, got_out_o,
    back, slot_col, residual, grad, wo, att, normed, ids, gate,
    score_sums, normed_sum, low_res, grad_att, grad_gain_two, results, parts, part_got, level_got, level_sum, last_got, last_sum,
    small_s, small_all, small_core, small_line, small_plane, small_half,
    r_ss, r_rs, c_ss, c_rs, l1_ss, l1_rs, l2_ss, l2_rs, g2_ss, g2_rs, g1_ss, g1_rs, h_ss, h_rs,
    own_sem, w_ss, w_rs, m_ss, m_rs, load_sem,
):
    step = pl.program_id(0)
    steps = pl.num_programs(0)
    rows, width = residual.shape
    group = wq.shape[1]
    seqs = rows // seq_len
    local = returned.shape[0]
    bits = bits_of(copies)
    me = lax.axis_index("expert")
    copy = lax.axis_index("dp")
    core = me % 2
    line = me // 2
    mesh_id = pl.DeviceIdType.MESH
    inside = sums_inside(width, copies, ranks)
    count = copies

    def remote(source, target, sends, recvs, device):
        return pltpu.make_async_remote_copy(
            src_ref=source, dst_ref=target, send_sem=sends, recv_sem=recvs,
            device_id=device, device_id_type=mesh_id,
        )


    def result_copy(e, at, peer):
        return remote(
            returned.at[e, peer], results.at[at, e], r_ss.at[e, peer], r_rs.at[e, at],
            {"expert": peer},
        )

    def result_stay(e):
        return pltpu.make_async_copy(returned.at[e, me], results.at[me, e], r_rs.at[e, me])

    def results_start(e):
        def one(d, carry):
            result_copy(e, me, (me + d) % ranks).start()
            return carry

        lax.fori_loop(1, ranks, one, 0)
        result_stay(e).start()

    def results_wait(e):
        def one(d, carry):
            peer = (me + ranks - d) % ranks
            result_copy(e, peer, peer).wait_recv()
            result_copy(e, me, (me + d) % ranks).wait_send()
            return carry

        lax.fori_loop(1, ranks, one, 0)
        result_stay(e).wait()


    moves = (
        (next_in, got_in_o, bits[0], bits[1]),
        (next_out, got_out_o, bits[1], bits[0]),
    )
    shares = 3 * PARTS

    def share_copy(which, n, late):
        source, target, first, second = moves[which]
        at = 2 if late else (n - PARTS) // PARTS
        height = source.shape[1] // PARTS
        span = pl.ds(pl.multiple_of((n % PARTS) * height, 16), height)
        return remote(
            source.at[at, span], target.at[at, span], w_ss.at[which, n], w_rs.at[which, n],
            {"dp": flip(copy, first if late else second)},
        )

    def pump(first, count):
        def one(n, carry):
            @pl.when(n < PARTS)
            def _():
                for which in range(2):
                    share_copy(which, n, True).start()

            @pl.when(n >= PARTS)
            def _():
                for which in (1, 0):
                    share_copy(which, n, False).start()

            return carry

        if count:
            lax.fori_loop(first, jnp.minimum(first + count, shares), one, 0)

    def shares_end():
        def late(n, carry):
            for which in range(2):
                share_copy(which, n, True).wait()
            return carry

        def rest(n, carry):
            for which in range(2):
                share_copy(which, n, False).wait()
            return carry

        lax.fori_loop(0, PARTS, late, 0)
        lax.fori_loop(PARTS, shares, rest, 0)

    def paced(at):
        for p, stage in PLAN.get(at, ()):
            if p == "ret":
                results_start(stage)
            elif inside:
                if p == "small":
                    small_stages[stage]()
                else:
                    stages[stage](p)


    def levels(p):
        along = (line, lambda i: {"expert": 2 * i + core})
        across = (copy, lambda i: {"dp": i})
        return (along, across) if p in ALONG_FIRST else (across, along)

    def core_copy(p):
        return remote(
            parts.at[p, 1 - core], part_got.at[p], c_ss.at[p], c_rs.at[p], {"expert": me + 1 - 2 * core}
        )

    def first_copy(p, peer, at):
        (_, device), _ = levels(p)
        return remote(
            parts.at[p, core, pl.ds(peer * count, count)], level_got.at[p, at],
            l1_ss.at[p, peer], l1_rs.at[p, at], device(peer),
        )

    def second_copy(p, peer, at):
        _, (_, device) = levels(p)
        return remote(
            level_sum.at[p, peer], last_got.at[p, at], l2_ss.at[p, peer], l2_rs.at[p, at],
            device(peer),
        )

    def give_second(p, peer, at):
        (mine, _), (_, device) = levels(p)
        return remote(
            last_sum.at[p], pieces_o.at[p, core, mine * count + at],
            g2_ss.at[p, peer], g2_rs.at[p, at], device(peer),
        )

    def give_own(p):
        (mine, _), (own, _) = levels(p)
        return pltpu.make_async_copy(
            last_sum.at[p], pieces_o.at[p, core, mine * count + own], own_sem.at[p]
        )

    def give_first(p, peer, at):
        (_, device), _ = levels(p)
        block = pieces_o.at[p, core, pl.ds(at * count, count)]
        return remote(block, block, g1_ss.at[p, peer], g1_rs.at[p, at], device(peer))

    def give_core(p, half):
        block = pieces_o.at[p, half]
        return remote(block, block, h_ss.at[p], h_rs.at[p], {"expert": me + 1 - 2 * core})

    def others(own):
        return [(own + d) % count for d in range(1, count)]

    def piece_0(p):
        core_copy(p).start()

    def piece_1(p):
        (own, _), _ = levels(p)
        core_copy(p).wait_recv()
        parts[p, core] = (parts[p, core].astype(F32) + part_got[p].astype(F32)).astype(BF)
        for peer in others(own):
            first_copy(p, peer, own).start()

    def piece_2(p):
        (first, _), (own, _) = levels(p)
        total = parts[p, core, pl.ds(first * count, count)].astype(F32)
        for peer in others(first):
            first_copy(p, peer, peer).wait_recv()
            total += level_got[p, peer].astype(F32)
        level_sum[p] = total.astype(BF)
        for peer in others(own):
            second_copy(p, peer, own).start()

    def piece_3(p):
        _, (own, _) = levels(p)
        total = level_sum[p, own].astype(F32)
        for peer in others(own):
            second_copy(p, peer, peer).wait_recv()
            total += last_got[p, peer].astype(F32)
        last_sum[p] = total.astype(BF)
        for peer in others(own):
            give_second(p, peer, own).start()
        give_own(p).start()

    def piece_4(p):
        (first, _), (own, _) = levels(p)
        for peer in others(own):
            give_second(p, peer, peer).wait_recv()
        give_own(p).wait()
        for peer in others(first):
            give_first(p, peer, first).start()

    def piece_5(p):
        (first, _), _ = levels(p)
        for peer in others(first):
            give_first(p, peer, peer).wait_recv()
        give_core(p, core).start()

    def piece_6(p):
        (first, _), (own, _) = levels(p)
        give_core(p, 1 - core).wait_recv()
        core_copy(p).wait_send()
        give_core(p, core).wait_send()
        for peer in others(first):
            first_copy(p, peer, first).wait_send()
            give_first(p, peer, first).wait_send()
        for peer in others(own):
            second_copy(p, peer, own).wait_send()
            give_second(p, peer, own).wait_send()

    stages = (piece_0, piece_1, piece_2, piece_3, piece_4, piece_5, piece_6)


    half = small_half.shape[0]

    def small_copy(stage, peer, at):
        if stage == 0:
            source, target, device = small_s, small_core, {"expert": me + 1 - 2 * core}
        elif stage == 1:
            source, target, device = small_half, small_line.at[at], {"expert": 2 * peer + core}
        elif stage == 2:
            source, target, device = small_half, small_plane.at[at], {"dp": peer}
        else:
            source = small_all.at[pl.ds(pl.multiple_of(core * half, 8), half)]
            target, device = source, {"expert": me + 1 - 2 * core}
        return remote(source, target, m_ss.at[stage, peer], m_rs.at[stage, at], device)

    def small_0():
        small_copy(0, 0, 0).start()

    def small_1():
        small_copy(0, 0, 0).wait()
        span = pl.ds(pl.multiple_of(core * half, 8), half)
        small_half[...] = small_s[span] + small_core[span]
        for peer in others(line):
            small_copy(1, peer, line).start()

    def small_2():
        total = small_half[...]
        for peer in others(line):
            small_copy(1, peer, peer).wait_recv()
            total += small_line[peer]
        for peer in others(line):
            small_copy(1, peer, line).wait_send()
        small_half[...] = total
        for peer in others(copy):
            small_copy(2, peer, copy).start()

    def small_3():
        total = small_half[...]
        for peer in others(copy):
            small_copy(2, peer, peer).wait_recv()
            total += small_plane[peer]
        small_all[pl.ds(pl.multiple_of(core * half, 8), half)] = total
        small_copy(3, 0, 0).start()

    def small_4():
        for peer in others(copy):
            small_copy(2, peer, copy).wait_send()
        small_copy(3, 0, 0).wait()

    def load_tokens():
        return pltpu.make_async_copy(tokens_i, low_res, load_sem.at[9])

    small_stages = (small_0, small_1, small_2, small_3, small_4)

    @pl.when(step == 0)
    def _():
        barrier = pltpu.get_barrier_semaphore()

        def greet(axis, own, size):
            def one(d, carry):
                pl.semaphore_signal(
                    barrier, inc=1, device_id={axis: (own + d) % size}, device_id_type=mesh_id
                )
                return carry

            lax.fori_loop(1, size, one, 0)

        greet("expert", me, ranks)
        greet("dp", copy, copies)
        pl.semaphore_wait(barrier, ranks + copies - 2)
        pump(0, PUMP_FIRST)
        paced("start")
        loads = [
            pltpu.make_async_copy(source, target, load_sem.at[at])
            for at, (source, target) in enumerate((
                (back_i, back), (slot_col_i, slot_col), (residual_i, residual), (grad_i, grad),
                (wo_i, wo), (att_i, att), (normed_i, normed), (ids_i, ids), (gate_i, gate),
            ))
        ]
        for one in loads:
            one.start()
        for one in loads[:6]:
            one.wait()


        height = rows // 4

        def block(i, gain):
            pump(PUMP_FIRST + PUMP_MIDDLE * i, PUMP_MIDDLE)
            span = pl.ds(pl.multiple_of(i * height, height), height)
            pick = (slot_col[span, :] == iota((height, back.shape[0]), 1)).astype(BF)
            upstream = dot_nn(pick, back[...])
            values = residual[span, :]
            factor = lax.rsqrt(jnp.mean(values * values, axis=-1, keepdims=True) + EPSILON)
            weighted = upstream * gain_two[...]
            mean = jnp.mean(weighted * values, axis=-1, keepdims=True)
            grad_residual = (
                grad[span, :].astype(F32)
                + factor * weighted
                - values * (factor * factor * factor) * mean
            )
            grad_tokens_o[span, :] = grad_residual
            low = grad_residual.astype(BF)
            low_res[span, :] = low
            grad_att[span, :] = dot_nt(low, wo[...]).astype(BF)
            return gain + jnp.sum(upstream * values * factor, axis=0, keepdims=True)

        grad_gain_two[...] = lax.fori_loop(0, 4, block, jnp.zeros((1, width), F32))
        grad_wo = dot_tn(att[...], low_res[...]).astype(BF)
        for side in range(2):
            across = slice(side * (width // 2), (side + 1) * (width // 2))
            parts[PIECES - 1, side] = grad_wo[:, across].reshape(parts.shape[2:])
        for one in loads[6:]:
            one.wait()
        load_tokens().start()
        paced("middle")


    per_step = group // head_dim
    here = pl.ds(pl.multiple_of(step * group, group), group)
    lane = iota((seq_len, group), 1)
    grads = [[None] * seqs for _ in range(3)]
    for seq in range(seqs):
        span = slice(seq * seq_len, (seq + 1) * seq_len)
        low_grad = (grad_att[span, here].astype(F32) * inv[span, :]).astype(BF)
        inner = low_grad.astype(F32) * att[span, here].astype(F32)
        grad_t = low_grad.T
        query_t = q[span, :].T
        query_sum = None
        key_rows, value_rows = [], []
        for head in range(per_step):
            mine = (lane >= head * head_dim) & (lane < (head + 1) * head_dim)
            own = slice(head * head_dim, (head + 1) * head_dim)
            grad_probs = dot_nt(jnp.where(mine, low_grad, 0).astype(BF), v[span, :])
            row_inner = jnp.sum(jnp.where(mine, inner, 0.0), axis=-1, keepdims=True)
            low_soft = soft[head, seq]
            scores = (low_soft.astype(F32) * (grad_probs - row_inner)).astype(BF)
            at = step * per_step + head
            if seq == 0:
                score_sums[at] = scores
            else:
                score_sums[at] = (score_sums[at].astype(F32) + scores.astype(F32)).astype(BF)
            value_rows.append(dot_nn(grad_t[own, :], low_soft))
            key_rows.append(dot_nn(query_t[own, :], scores))
            grad_query = dot_nn(scores, k[span, :])
            query_sum = grad_query if head == 0 else jnp.where(mine, grad_query, query_sum)
        grads[0][seq] = (query_sum * 0.125).astype(BF)
        grads[1][seq] = (jnp.concatenate(key_rows, axis=0).T * 0.125).astype(BF)
        grads[2][seq] = jnp.concatenate(value_rows, axis=0).T.astype(BF)
        if seq < seqs - 1:
            pump(PUMP_FIRST + 4 * PUMP_MIDDLE + 2 * PUMP_STEP * step, PUMP_STEP)
            for after in range(width // group):
                if (after, 0) in PLAN:
                    @pl.when(step == after)
                    def _():
                        paced((after, 0))
    grads = jnp.concatenate([jnp.concatenate(one, axis=0) for one in grads], axis=1)
    weights = jnp.concatenate([wq[...], wk[...], wv[...]], axis=1)
    parts[step // 2, step % 2] = dot_tn(normed[...], grads).astype(BF).reshape(parts.shape[2:])
    part = dot_nt(grads, weights)

    @pl.when(step == 0)
    def _():
        normed_sum[...] = part

    @pl.when(step > 0)
    def _():
        normed_sum[...] += part

    pump(PUMP_FIRST + 4 * PUMP_MIDDLE + 2 * PUMP_STEP * step + PUMP_STEP, PUMP_STEP)
    for after in range(width // group):
        if (after, 1) in PLAN:
            @pl.when(step == after)
            def _():
                paced((after, 1))

    @pl.when(step == steps - 1)
    def _():
        load_tokens().wait()
        upstream = normed_sum[...]
        values = low_res[...].astype(F32)
        factor = lax.rsqrt(jnp.mean(values * values, axis=-1, keepdims=True) + EPSILON)
        weighted = upstream * gain_one[...]
        mean = jnp.mean(weighted * values, axis=-1, keepdims=True)
        gain = jnp.sum(upstream * values * factor, axis=0, keepdims=True)
        grad_tokens_o[...] = (
            grad_tokens_o[...]
            + factor * weighted
            - values * (factor * factor * factor) * mean
        )
        pump(PUMP_FIRST + 4 * PUMP_MIDDLE + 2 * PUMP_STEP * (width // group), PUMP_LAST)
        paced("norm")
        heads = score_sums.shape[0]
        rows_at = 16

        def add(block, sums):
            at = pl.multiple_of(block * rows_at, rows_at)
            own = ids[pl.ds(at, rows_at), :]
            hot = own[:, None, :] == iota((rows_at, buckets, seq_len), 1)
            hot = hot.astype(BF).reshape(rows_at * buckets, seq_len)
            scores = score_sums[:, pl.ds(at, rows_at), :].reshape(heads * rows_at, seq_len)
            return sums + dot_nt(hot, scores)

        sums = jnp.zeros((rows_at * buckets, heads * rows_at), F32)
        sums = lax.fori_loop(0, seq_len // rows_at, add, sums)
        sums = sums.reshape(rows_at, buckets, heads * rows_at)
        across = iota(sums.shape, 2)
        keep = iota(sums.shape, 0) == across % rows_at
        sums = jnp.sum(jnp.where(keep, sums, 0.0), axis=0)
        into = iota((heads * rows_at, LANES), 0) // rows_at == iota((heads * rows_at, LANES), 1)
        bucket = lax.dot_general(
            sums, into.astype(F32), (((1,), (0,)), ((), ())),
            precision=lax.Precision.HIGHEST, preferred_element_type=F32,
        )
        small_s[...] = jnp.zeros_like(small_s)
        tiles = width // LANES
        experts = router.shape[0]
        for tile in range(tiles):
            cols = slice(tile * LANES, (tile + 1) * LANES)
            small_s[tile:tile + 1, :] = gain[:, cols]
            small_s[8 + tile:9 + tile, :] = grad_gain_two[:, cols]
            at = 16 + buckets + tile * experts
            small_s[at:at + experts, :] = router[:, cols]
        small_s[16:16 + buckets, :] = bucket
        pump(PUMP_FIRST + 4 * PUMP_MIDDLE + 2 * PUMP_STEP * (width // group) + PUMP_LAST, shares)
        paced("bucket")
        small_o[...] = small_all[...] if inside else small_s[...]
        for e in range(local):
            results_wait(e)

        height = rows // 4

        def mix(i, carry):
            span = pl.ds(pl.multiple_of(i * height, height), height)
            pick = (slot_col[span, :] == iota((height, back.shape[0]), 1)).astype(BF)
            combined = dot_nn(pick, results[...].reshape(back.shape))
            grad[span, :] = (residual[span, :] + gate[span, :] * combined).astype(BF)
            return carry

        lax.fori_loop(0, 4, mix, 0)
        out = pltpu.make_async_copy(grad, mixed_o, load_sem.at[0])
        out.start()
        paced("mixed")
        shares_end()
        out.wait()
        if not inside:
            for p in range(PIECES):
                out = pltpu.make_async_copy(parts.at[p], pieces_o.at[p], own_sem.at[p])
                out.start()
                out.wait()


ALONG_FIRST = (3, 1)
PARTS = 12
PUMP_FIRST, PUMP_MIDDLE, PUMP_STEP, PUMP_LAST = 3, 1, 2, 2
PLAN = {
    "start": (("ret", 0),),
    "middle": ((3, 0),),
    (0, 1): ((3, 1), ("ret", 1)),
    (1, 1): ((0, 0),),
    (3, 0): ((3, 2), (0, 1)),
    (3, 1): ((3, 3),),
    (4, 0): ((1, 0),),
    (4, 1): ((1, 1), (0, 2)),
    (5, 0): ((3, 4),),
    (5, 1): ((1, 2), (2, 0), (0, 3), (2, 1), (1, 3)),
    "norm": ((2, 2), (3, 5), (0, 4)),
    "bucket": (
        (2, 3), ("small", 0), (0, 5), ("small", 1), (1, 4), ("small", 2), (2, 4), ("small", 3),
        ("small", 4),
    ),
    "mixed": ((1, 5), (0, 6), (3, 6), (2, 5), (1, 6), (2, 6)),
}


def backward(
    tokens, gain_one, normed, bucket_ids, q, k, v, att, inv, soft, weights,
    back, slot_col, residual, grad, gain_two, wo, gate, router, returned, shares,
    head_dim, buckets, copies, ranks,
):
    rows, width = tokens.shape
    seq_len = bucket_ids.shape[0]
    heads, seqs = soft.shape[:2]
    local = returned.shape[0]
    experts = router.shape[0]
    chunk = shares[0].shape[2]
    slots = back.shape[0]
    group = LANES
    steps = width // group
    per_step = heads // steps
    inside = sums_inside(width, copies, ranks)
    chips = copies * copies if inside else 1
    block = (width // chips, width // 2)
    small_rows = -(-(16 + buckets + width // LANES * experts) // 16) * 16
    cols = lambda shape: pl.BlockSpec(shape, lambda g: (0, g))
    once = lambda shape: pl.BlockSpec(
        shape, lambda g: (0,) * len(shape), pipeline_mode=pl.Buffered(1)
    )
    hbm = pl.BlockSpec(memory_space=pl.ANY)
    dma = pltpu.SemaphoreType.DMA
    each = dma((PIECES, copies))
    return pl.pallas_call(
        functools.partial(backward_kernel, head_dim, seq_len, buckets, copies, ranks),
        grid=(steps,),
        in_specs=[
            hbm,
            once((1, width)),
            hbm,
            hbm,
            cols((rows, group)),
            cols((rows, group)),
            cols((rows, group)),
            hbm,
            cols((rows, group)),
            pl.BlockSpec((per_step, seqs, seq_len, seq_len), lambda g: (g, 0, 0, 0)),
            cols((width, group)),
            cols((width, group)),
            cols((width, group)),
            hbm,
            hbm,
            hbm,
            hbm,
            once((1, width)),
            hbm,
            hbm,
            once((experts, width)),
        ]
        + [hbm] * 3,
        out_specs=(
            once((rows, width)),
            hbm,
            hbm,
            once((small_rows, LANES)),
            hbm,
            hbm,
        ),
        scratch_shapes=[
            pltpu.VMEM((slots, width), BF),
            pltpu.VMEM((rows, 1), jnp.int32),
            pltpu.VMEM((rows, width), F32),
            pltpu.VMEM((rows, width), BF),
            pltpu.VMEM((width, width), BF),
            pltpu.VMEM((rows, width), BF),
            pltpu.VMEM((rows, width), BF),
            pltpu.VMEM((seq_len, seq_len), jnp.int32),
            pltpu.VMEM((rows, 1), F32),
            pltpu.VMEM((heads, seq_len, seq_len), BF),
            pltpu.VMEM((rows, width), F32),
            pltpu.VMEM((rows, width), BF),
            pltpu.VMEM((rows, width), BF),
            pltpu.VMEM((1, width), F32),
            pltpu.VMEM((ranks, local) + returned.shape[2:], BF),
            pltpu.VMEM((PIECES, 2, chips) + block, BF),
            pltpu.VMEM((PIECES, chips) + block, BF),
            pltpu.VMEM((PIECES, copies, copies) + block if inside else (8, LANES), BF),
            pltpu.VMEM((PIECES, copies) + block if inside else (8, LANES), BF),
            pltpu.VMEM((PIECES, copies) + block if inside else (8, LANES), BF),
            pltpu.VMEM((PIECES,) + block, BF),
            pltpu.VMEM((small_rows, LANES), F32),
            pltpu.VMEM((small_rows, LANES), F32),
            pltpu.VMEM((small_rows, LANES), F32),
            pltpu.VMEM((copies, small_rows // 2, LANES), F32),
            pltpu.VMEM((copies, small_rows // 2, LANES), F32),
            pltpu.VMEM((small_rows // 2, LANES), F32),
            dma((local, ranks)),
            dma((local, ranks)),
            dma((PIECES,)),
            dma((PIECES,)),
            each, each, each, each, each, each, each, each,
            dma((PIECES,)),
            dma((PIECES,)),
            dma((PIECES,)),
            dma((2, 3 * PARTS)),
            dma((2, 3 * PARTS)),
            dma((4, copies)),
            dma((4, copies)),
            dma((10,)),
        ],
        out_shape=(
            jax.ShapeDtypeStruct((rows, width), F32),
            jax.ShapeDtypeStruct((rows, width), BF),
            jax.ShapeDtypeStruct((PIECES, 2, chips) + block, BF),
            jax.ShapeDtypeStruct((small_rows, LANES), F32),
            jax.ShapeDtypeStruct((3, width, chunk), BF),
            jax.ShapeDtypeStruct((3, chunk, width), BF),
        ),
        compiler_params=params(
            dimension_semantics=("arbitrary",), collective_id=1, has_side_effects=True
        ),
        cost_estimate=pl.CostEstimate(
            flops=2 * rows * width * (6 * width + 5 * seq_len * 4),
            bytes_accessed=50 << 20,
            transcendentals=0,
        ),
        name="backward",
    )(
        tokens, gain_one, normed, bucket_ids, q, k, v, att, inv, soft, *weights,
        back, slot_col, residual, grad, gain_two, wo, gate, router, returned, *shares,
    )


def finish_kernel(pieces, keep_in, got_in, keep_out, got_out, wq_o, wk_o, wv_o, wo_o, grad_in_o, grad_out_o):
    width = wo_o.shape[1]
    half = width // 2
    part = half // 3
    for step in range(width // part):
        block = pieces[step // 2, step % 2].astype(F32)
        for at, out in enumerate((wq_o, wk_o, wv_o)):
            out[:, step * part:(step + 1) * part] = block[:, at * part:(at + 1) * part]
    for side in range(2):
        wo_o[:, side * half:(side + 1) * half] = pieces[PIECES - 1, side].astype(F32)
    for keep, got, out in ((keep_in, got_in, grad_in_o), (keep_out, got_out, grad_out_o)):
        out[0] = keep[0].astype(F32) + got[0].astype(F32)
        out[1] = keep[1].astype(F32) + got[1].astype(F32) + got[2].astype(F32)


def finish(pieces, keep_in, got_in, keep_out, got_out):
    width, chunk = keep_in.shape[1:]
    count = 8
    pieces = pieces.reshape(PIECES, 2, width, width // 2)
    part = width // count
    rows = pl.BlockSpec((part, width), lambda i: (i, 0))
    square = jax.ShapeDtypeStruct((width, width), F32)
    by_in = lambda lead: pl.BlockSpec((lead, part, chunk), lambda i: (0, i, 0))
    by_out = lambda lead: pl.BlockSpec((lead, chunk // count, width), lambda i: (0, i, 0))
    return pl.pallas_call(
        finish_kernel,
        grid=(count,),
        in_specs=[
            pl.BlockSpec((PIECES, 2, part, width // 2), lambda i: (0, 0, i, 0)),
            by_in(2),
            by_in(3),
            by_out(2),
            by_out(3),
        ],
        out_specs=(rows, rows, rows, rows, by_in(2), by_out(2)),
        out_shape=(
            square,
            square,
            square,
            square,
            jax.ShapeDtypeStruct((2, width, chunk), F32),
            jax.ShapeDtypeStruct((2, chunk, width), F32),
        ),
        compiler_params=params(dimension_semantics=("arbitrary",)),
        cost_estimate=pl.CostEstimate(flops=1 << 20, bytes_accessed=30 << 20, transcendentals=0),
        name="finish",
    )(pieces, keep_in, got_in, keep_out, got_out)


def per_device(
    tokens,
    expert_ids,
    bucket_ids,
    attn_gain,
    ffn_gain,
    query_weight,
    key_weight,
    value_weight,
    output_weight,
    router_weight,
    bucket_bias,
    expert_in,
    expert_out,
    grad_output,
):
    tok_rows, width = tokens.shape
    buckets, heads = bucket_bias.shape
    head_dim = width // heads
    local = expert_in.shape[0]
    ranks = lax.axis_size("expert")
    copies = lax.axis_size("dp")
    experts = local * ranks
    cap = (5 * tok_rows + 4 * experts - 1) // (4 * experts)
    room = -(-cap // 16) * 16
    slots = experts * room
    per_group = 4
    groups = heads // per_group
    table = jnp.pad(bucket_bias.T, ((0, 0), (0, LANES - buckets)))
    table = table.reshape(groups, per_group, LANES)
    gains = (attn_gain.reshape(1, width), ffn_gain.reshape(1, width))

    blocks = (ranks, local, room, width)
    late = (room * LATE_TENTHS // 10) // 16 * 16 if room > 16 else 0
    router_rows = router_weight.T
    (
        normed, q, k, v, att, inv, soft, residual, gate, slot_col, row_slots, grad_slots, late_grads
    ) = forward(
        tokens, bucket_ids, table, gains,
        (query_weight, key_weight, value_weight, output_weight),
        router_rows, expert_ids.reshape(1, tok_rows), grad_output, blocks, late, cap, head_dim,
    )
    returned, back, router, next_in, keep_in, next_out, keep_out = run_experts(
        row_slots.reshape(blocks), grad_slots, late_grads, late, expert_in, expert_out, router_rows, copies,
    )
    grad_tokens, mixed, pieces, small, got_in, got_out = backward(
        tokens, gains[0], normed, bucket_ids, q, k, v, att, inv, soft,
        (query_weight, key_weight, value_weight), back.reshape(slots, width), slot_col, residual,
        grad_output, gains[1], output_weight, gate, router, returned, (next_in, next_out),
        head_dim, buckets, copies, ranks,
    )
    if not sums_inside(width, copies, ranks):
        pieces = lax.psum(pieces.astype(F32), ("dp", "expert"))
        small = lax.psum(small, ("dp", "expert"))
    grad_wq, grad_wk, grad_wv, grad_wo, grad_expert_in, grad_expert_out = finish(
        pieces, keep_in, got_in, keep_out, got_out
    )
    tiles = width // LANES
    grad_attn_gain = small[:tiles].reshape(width)
    grad_ffn_gain = small[8:8 + tiles].reshape(width)
    grad_bucket = small[16:16 + buckets, :heads]
    at = 16 + buckets
    grad_router = small[at:at + experts * tiles].reshape(tiles, experts, LANES)
    grad_router = grad_router.transpose(0, 2, 1).reshape(width, experts)
    return (
        mixed,
        grad_tokens,
        grad_attn_gain,
        grad_ffn_gain,
        grad_wq,
        grad_wk,
        grad_wv,
        grad_wo,
        grad_router,
        grad_bucket,
        grad_expert_in,
        grad_expert_out,
    )


def solution(mesh):
    shared = P()
    rows = P(("dp", "expert"), None)
    expert = P("expert", None, None)
    return jax.shard_map(
        per_device,
        mesh=mesh,
        in_specs=(rows, rows) + (shared,) * 9 + (expert, expert, rows),
        out_specs=(rows, rows) + (shared,) * 8 + (P("expert", None, "dp"), P("expert", "dp", None)),
        check_vma=False,
    )
```

```python
import functools

import jax
import jax.numpy as jnp
from jax import lax
from jax.experimental import pallas as pl
from jax.experimental.pallas import tpu as pltpu
from jax.sharding import PartitionSpec as P

EPSILON = 1e-06
BF = jnp.bfloat16
F32 = jnp.float32
LANES = 128
VMEM_BYTES = 62 * 1024 * 1024


def dot_nn(left, right):
    return lax.dot_general(left, right, (((1,), (0,)), ((), ())), preferred_element_type=F32)


def dot_nt(left, right):
    return lax.dot_general(left, right, (((1,), (1,)), ((), ())), preferred_element_type=F32)


def dot_tn(left, right):
    return lax.dot_general(left, right, (((0,), (0,)), ((), ())), preferred_element_type=F32)


def iota(shape, axis):
    return lax.broadcasted_iota(jnp.int32, shape, axis)


def whole(shape):
    return pl.BlockSpec(shape, lambda *_: (0,) * len(shape))


def nth_far(i, size):
    return size // 2 + ((i + 1) // 2) * (2 * (i % 2) - 1)


def params(**more):
    return pltpu.CompilerParams(vmem_limit_bytes=VMEM_BYTES, **more)


def forward_kernel(
    head_dim, seq_len, cap, late_rows,
    tokens, ids, table, gain_one, gain_two, wq, wk, wv, wo, wr, ids_row, grad,
    normed_o, q_o, k_o, v_o, att_o, inv_o, soft_o, residual_o, gate_o, slot_col_o, slots_o, raw_o,
    late_o,
    slot_row, grad_slots, table_s, send_sem, recv_sem, own_sem,
):
    step = pl.program_id(0)
    rows, width = tokens.shape
    group = wq.shape[1]
    ranks, local, room = grad_slots.shape[:3]
    experts = ranks * local
    me = lax.axis_index("expert")

    early = room - late_rows

    def raw_span(e):
        return pl.ds(0, early if e else room)

    def raw_copy(e, at, peer):
        return pltpu.make_async_remote_copy(
            src_ref=grad_slots.at[peer, e, raw_span(e)],
            dst_ref=raw_o.at[at, e, raw_span(e)],
            send_sem=send_sem.at[e, peer],
            recv_sem=recv_sem.at[e, at],
            device_id={"expert": peer},
            device_id_type=pl.DeviceIdType.MESH,
        )

    def raw_stay(e):
        return pltpu.make_async_copy(
            grad_slots.at[me, e, raw_span(e)], raw_o.at[me, e, raw_span(e)], own_sem.at[e]
        )

    def late_keep(e):
        return pltpu.make_async_copy(
            grad_slots.at[:, e, pl.ds(early, room - early)], late_o.at[e - 1], own_sem.at[local + e]
        )

    def column(row):
        return jnp.broadcast_to(row, (8, rows)).T[:, :1]

    @pl.when(step == 0)
    def _():
        barrier = pltpu.get_barrier_semaphore()

        def greet(d, carry):
            pl.semaphore_signal(
                barrier, inc=1, device_id={"expert": (me + d) % ranks},
                device_id_type=pl.DeviceIdType.MESH,
            )
            return carry

        lax.fori_loop(1, ranks, greet, 0)
        table_s[...] = jnp.zeros_like(table_s)
        table_s[:, :table.shape[1]] = table[...]
        hot = ids_row[...] == iota((experts, rows), 0)
        earlier = (iota((rows, rows), 0) < iota((rows, rows), 1)).astype(BF)
        counts = dot_nn(hot.astype(BF), earlier)
        place = jnp.sum(jnp.where(hot, counts, 0.0), axis=0, keepdims=True).astype(jnp.int32)
        slot = jnp.where(place < cap, ids_row[...] * room + place, -1)
        slot_row[...] = slot
        slot_col_o[...] = column(slot)
        pl.semaphore_wait(barrier, ranks - 1)

        def pick_rows(peer):
            each = local * room
            pick = (iota((each, rows), 0) + peer * each == slot).astype(BF)
            grad_slots[peer] = dot_nn(pick, grad[...]).astype(BF).reshape(local, room, width)

        for e in range(local):
            def send(i, carry):
                peer = (me + nth_far(i, ranks)) % ranks
                if e == 0:
                    pick_rows(peer)
                raw_copy(e, me, peer).start()
                return carry

            lax.fori_loop(0, ranks - 1, send, 0)
            if e == 0:
                pick_rows(me)
            raw_stay(e).start()
            if e and early < room:
                late_keep(e).start()
        x = tokens[...].astype(F32)
        factor = lax.rsqrt(jnp.mean(x * x, axis=-1, keepdims=True) + EPSILON)
        normed_o[...] = (x * factor * gain_one[...][None, :]).astype(BF)
        residual_o[...] = x

    normed = normed_o[...]
    q_o[...] = dot_nn(normed, wq[...]).astype(BF)
    k_o[...] = dot_nn(normed, wk[...]).astype(BF)
    v_o[...] = dot_nn(normed, wv[...]).astype(BF)
    lane = iota((seq_len, LANES), 1)
    per_tile = LANES // head_dim
    per_group = group // head_dim
    for tile in range(group // LANES):
        cols = slice(tile * LANES, (tile + 1) * LANES)
        gathered = [None] * (rows // seq_len)
        scaled = [None] * (rows // seq_len)
        for part in range(per_tile):
            head = tile * per_tile + part
            mine = (lane >= part * head_dim) & (lane < (part + 1) * head_dim)
            row = jnp.broadcast_to(table_s[pl.ds(step * per_group + head, 1), :], (seq_len, LANES))
            bias = jnp.concatenate(
                [
                    jnp.take_along_axis(
                        row, ids[:, c:c + LANES], axis=1, mode="promise_in_bounds"
                    )
                    for c in range(0, seq_len, LANES)
                ],
                axis=1,
            )
            for seq in range(rows // seq_len):
                span = slice(seq * seq_len, (seq + 1) * seq_len)
                query = jnp.where(mine, q_o[span, cols] * 0.125, 0).astype(BF)
                scores = dot_nt(query, k_o[span, cols]) + bias
                low = jnp.exp(scores - jnp.max(scores, axis=-1, keepdims=True)).astype(BF)
                soft_o[head, seq] = low
                out = dot_nn(low, jnp.where(mine, v_o[span, cols], 1.0).astype(BF))
                inverse = 1.0 / pltpu.roll(out, head_dim, 1)
                out = out * inverse
                if part == 0:
                    gathered[seq], scaled[seq] = out, inverse
                else:
                    gathered[seq] = jnp.where(mine, out, gathered[seq])
                    scaled[seq] = jnp.where(mine, inverse, scaled[seq])
        for seq in range(rows // seq_len):
            span = slice(seq * seq_len, (seq + 1) * seq_len)
            att_o[span, cols] = gathered[seq].astype(BF)
            inv_o[span, cols] = scaled[seq]
    residual_o[...] += dot_nn(att_o[...], wo[...])

    @pl.when(step == pl.num_programs(0) - 1)
    def _():
        residual = residual_o[...]
        factor = lax.rsqrt(jnp.mean(residual * residual, axis=-1, keepdims=True) + EPSILON)
        low = (residual * factor * gain_two[...][None, :]).astype(BF)
        logits = dot_nt(low, wr[...])
        weights = jnp.exp(logits - jnp.max(logits, axis=-1, keepdims=True))
        probs = weights / jnp.sum(weights, axis=-1, keepdims=True)
        hot = column(ids_row[...]) == iota(logits.shape, 1)
        gate_o[...] = jnp.sum(jnp.where(hot, probs, 0.0), axis=1, keepdims=True)
        pick = (iota((slots_o.shape[0], rows), 0) == slot_row[...]).astype(BF)
        slots_o[...] = dot_nn(pick, low).astype(BF)

        for e in range(local):
            def finish(d, carry):
                peer = (me + ranks - d) % ranks
                raw_copy(e, peer, peer).wait_recv()
                raw_copy(e, me, (me + d) % ranks).wait_send()
                return carry

            lax.fori_loop(1, ranks, finish, 0)
            raw_stay(e).wait()
            if e and early < room:
                late_keep(e).wait()


def forward(
    tokens, bucket_ids, table, gains, weights, wr, ids_row, grad, blocks, late, cap, head_dim
):
    rows, width = tokens.shape
    seq_len = bucket_ids.shape[0]
    heads = table.shape[0]
    per_group = 4
    groups = heads // per_group
    group = width // groups
    seqs = rows // seq_len
    ranks, local, room = blocks[:3]
    slots = ranks * local * room
    dma = pltpu.SemaphoreType.DMA
    cols = lambda shape: pl.BlockSpec(shape, lambda g: (0, g))
    wq, wk, wv, wo = weights
    return pl.pallas_call(
        functools.partial(forward_kernel, head_dim, seq_len, cap, late),
        grid=(groups,),
        in_specs=[
            whole((rows, width)),
            whole((seq_len, seq_len)),
            whole(table.shape),
            whole((width,)),
            whole((width,)),
            cols((width, group)),
            cols((width, group)),
            cols((width, group)),
            pl.BlockSpec((group, width), lambda g: (g, 0)),
            whole(wr.shape),
            whole((1, rows)),
            whole((rows, width)),
        ],
        out_specs=(
            whole((rows, width)),
            cols((rows, group)),
            cols((rows, group)),
            cols((rows, group)),
            cols((rows, group)),
            cols((rows, group)),
            pl.BlockSpec((per_group, seqs, seq_len, seq_len), lambda g: (g, 0, 0, 0)),
            whole((rows, width)),
            whole((rows, 1)),
            whole((rows, 1)),
            whole((slots, width)),
            pl.BlockSpec(memory_space=pl.ANY),
            pl.BlockSpec(memory_space=pl.ANY),
        ),
        scratch_shapes=[
            pltpu.VMEM((1, rows), jnp.int32),
            pltpu.VMEM(blocks, BF),
            pltpu.VMEM((heads, LANES), F32),
            dma((local, ranks)),
            dma((local, ranks)),
            dma((2 * local,)),
        ],
        out_shape=(
            jax.ShapeDtypeStruct((rows, width), BF),
            jax.ShapeDtypeStruct((rows, width), BF),
            jax.ShapeDtypeStruct((rows, width), BF),
            jax.ShapeDtypeStruct((rows, width), BF),
            jax.ShapeDtypeStruct((rows, width), BF),
            jax.ShapeDtypeStruct((rows, width), F32),
            jax.ShapeDtypeStruct((heads, seqs, seq_len, seq_len), BF),
            jax.ShapeDtypeStruct((rows, width), F32),
            jax.ShapeDtypeStruct((rows, 1), F32),
            jax.ShapeDtypeStruct((rows, 1), jnp.int32),
            jax.ShapeDtypeStruct((slots, width), BF),
            jax.ShapeDtypeStruct(blocks, BF),
            jax.ShapeDtypeStruct((local - 1, ranks, max(late, 16), width), BF),
        ),
        compiler_params=params(
            dimension_semantics=("arbitrary",), collective_id=2, has_side_effects=True
        ),
        cost_estimate=pl.CostEstimate(
            flops=2 * rows * width * (4 * width + 2 * seq_len * 4),
            bytes_accessed=40 << 20,
            transcendentals=heads * rows * seq_len,
        ),
        name="forward",
    )(tokens, bucket_ids, table, *gains, wq, wk, wv, wo, wr, ids_row, grad)


LATE_TENTHS = 6


def bits_of(size):
    return [1 << i for i in range(size.bit_length() - 1)]


def flip(index, bit):
    return index + bit * (1 - 2 * ((index // bit) % 2))


def flip_all(index, mask, bits):
    for bit in bits:
        index = jnp.where((mask // bit) % 2 == 1, flip(index, bit), index)
    return index


def experts_kernel(
    ranks, copies, late,
    x_send, raw_i, late_i, weight_in, weight_out, wr,
    first_o, returned_o, back_o, router_o, next_in_o, keep_in_o, next_out_o, keep_out_o,
    x_recv, raw, back_send, win, wout, grads_in, grads_out, got_in, got_out,
    scaled, probs_s, back_sum, result_sum, result,
    x_ss, x_rs, b_ss, b_rs, l_ss, l_rs, f_ss, f_rs, raw_sem, w_sem, first_ss, first_rs, result_sem, out_sem,
):
    local, cap, width = x_send.shape[1:]
    rows = ranks * cap
    chunk = win.shape[2]
    steps = copies
    bits = bits_of(copies)
    orders = (bits, bits[::-1])
    me = lax.axis_index("expert")
    copy = lax.axis_index("dp")
    mesh_id = pl.DeviceIdType.MESH

    barrier = pltpu.get_barrier_semaphore()

    def greet(d, carry):
        pl.semaphore_signal(
            barrier, inc=1, device_id={"expert": (me + d) % ranks}, device_id_type=mesh_id
        )
        return carry

    lax.fori_loop(1, ranks, greet, 0)
    for bit in bits:
        pl.semaphore_signal(
            barrier, inc=1, device_id={"dp": flip(copy, bit)}, device_id_type=mesh_id
        )

    def load(s):
        e, j = s // steps, steps - 1 - s % steps
        at = pl.multiple_of(flip_all(copy, j, bits) * chunk, chunk)
        return (
            pltpu.make_async_copy(
                weight_in.at[e, :, pl.ds(at, chunk)], win.at[s % 2], w_sem.at[0, s % 2]
            ),
            pltpu.make_async_copy(
                weight_out.at[e, pl.ds(at, chunk), :], wout.at[s % 2], w_sem.at[1, s % 2]
            ),
        )

    for one in load(0):
        one.start()
    pl.semaphore_wait(barrier, ranks - 1 + len(bits))


    early = cap - late

    def raw_load(e):
        span = pl.ds(0, early if e else cap)
        return pltpu.make_async_copy(
            raw_i.at[:, e, span], raw.at[e, :, span], raw_sem.at[e]
        )

    def row_copy(out, e, at, peer):
        if out == "result":
            source, target, sends, recvs = result.at[peer], first_o.at[at], f_ss, f_rs
        elif out is None:
            source = late_i.at[e - 1, peer]
            target, sends, recvs = raw.at[e, at, pl.ds(early, late)], l_ss, l_rs
        elif out:
            source, target, sends, recvs = x_send.at[peer, e], x_recv.at[e, at], x_ss, x_rs
        else:
            source, target, sends, recvs = back_send.at[e, peer], back_o.at[at, e], b_ss, b_rs
        return pltpu.make_async_remote_copy(
            src_ref=source,
            dst_ref=target,
            send_sem=sends.at[e, peer],
            recv_sem=recvs.at[e, at],
            device_id={"expert": peer},
            device_id_type=mesh_id,
        )

    def stay(out, e):
        if out == "result":
            return pltpu.make_async_copy(result.at[me], first_o.at[me], f_rs.at[e, me])
        if out is None:
            return pltpu.make_async_copy(
                late_i.at[e - 1, me], raw.at[e, me, pl.ds(early, late)], l_rs.at[e, me]
            )
        if out:
            return pltpu.make_async_copy(x_send.at[me, e], x_recv.at[e, me], x_rs.at[e, me])
        return pltpu.make_async_copy(back_send.at[e, me], back_o.at[me, e], b_rs.at[e, me])

    def send(out, e):
        def one(i, carry):
            row_copy(out, e, me, (me + nth_far(i, ranks)) % ranks).start()
            return carry

        lax.fori_loop(0, ranks - 1, one, 0)
        stay(out, e).start()

    def arrive(out, e):
        def one(d, carry):
            peer = (me + ranks - d) % ranks
            row_copy(out, e, peer, peer).wait_recv()
            return carry

        lax.fori_loop(1, ranks, one, 0)
        if out != "result":
            stay(out, e).wait()

    def leave(out, e):
        def one(d, carry):
            row_copy(out, e, me, (me + d) % ranks).wait_send()
            return carry

        lax.fori_loop(1, ranks, one, 0)

    moves = (
        (grads_in, got_in, bits[0], next_in_o, keep_in_o),
        (grads_out, got_out, bits[1], next_out_o, keep_out_o),
    )
    spare, kept = steps, steps + 1

    def first_copy(k, e, j):
        grads, got, bit = moves[k][:3]
        at = 2 if e else (0 if j == steps - 1 else 1)
        return pltpu.make_async_remote_copy(
            src_ref=grads.at[spare if e else j],
            dst_ref=got.at[at],
            send_sem=first_ss.at[k, at],
            recv_sem=first_rs.at[k, at],
            device_id={"dp": flip(copy, bit)},
            device_id_type=mesh_id,
        )

    def store(k, t):
        grads, _, _, following, keep = moves[k]
        target = keep.at[1] if t == steps - 1 else following.at[2]
        return pltpu.make_async_copy(grads.at[steps - 1], target, out_sem.at[k, 0])

    def out_copy(k, at):
        grads, _, bit, following, keep = moves[k]
        source, target = (
            (grads.at[steps - 1 - bit], following.at[0]),
            (grads.at[0], keep.at[0]),
            (grads.at[kept], following.at[1]),
        )[at]
        return pltpu.make_async_copy(source, target, out_sem.at[k, 1 + at])

    def keep_result():
        return pltpu.make_async_copy(result, returned_o, result_sem)

    send(True, 0)
    for e in range(local):
        raw_load(e).start()
    router_o[...] = jnp.zeros_like(router_o)

    def body(s, carry):
        e, t = s // steps, s % steps
        j = steps - 1 - t

        @pl.when(s + 1 < local * steps)
        def _():
            for one in load(s + 1):
                one.start()

        @pl.when(t == 0)
        def _():
            arrive(True, e)

            @pl.when(e == 0)
            def _():
                raw_load(0).wait()
                for other in range(1, local):
                    if late:
                        send(None, other)
                    send(True, other)

            @pl.when(e > 0)
            def _():
                raw_load(1).wait()
                if late:
                    arrive(None, e)

            logits = dot_nt(x_recv[e].reshape(rows, width), wr[...])
            weights = jnp.exp(logits - jnp.max(logits, axis=-1, keepdims=True))
            probs = weights / jnp.sum(weights, axis=-1, keepdims=True)
            probs_s[...] = probs
            hot = iota(logits.shape, 1) == me * local + e
            gate = jnp.sum(jnp.where(hot, probs, 0.0), axis=1, keepdims=True)

            scaled[...] = (gate * raw[e].reshape(rows, width).astype(F32)).astype(BF)
            back_sum[...] = jnp.zeros_like(back_sum)
            result_sum[...] = jnp.zeros_like(result_sum)

        for one in load(s):
            one.wait()

        late_at = [steps - 1 - moves[k][2] for k in range(2)]
        slots = [
            jnp.where(
                e == 0, j, jnp.where(t == 0, spare, jnp.where(j == late_at[k], kept, steps - 1))
            )
            for k in range(2)
        ]
        for k in range(2):
            bit = moves[k][2]

            @pl.when((e > 0) & (j == bit))
            def _():
                first_copy(k, 0, steps - 1).wait_send()

            @pl.when((e > 0) & (t == steps - 1))
            def _():
                store(k, 0).wait()

        own_in, own_out = win[s % 2], wout[s % 2]
        taken = x_recv[e].reshape(rows, width)
        grads = scaled[...]


        def products(part):
            span = slice(part * (chunk // 3), (part + 1) * (chunk // 3))
            return dot_nn(taken, own_in[:, span]), dot_nt(grads, own_out[span, :])

        def activate(pre, grad_hidden):
            scale = 0.7978845608028654
            square = pre * pre
            bent = jnp.tanh(pre * (scale + (scale * 0.044715) * square))
            half = 0.5 + 0.5 * bent
            slope = half + pre * (half * (1.0 - bent)) * (scale + (scale * 0.134145) * square)
            return (pre * half).astype(BF), (grad_hidden * slope).astype(BF)

        parts = []
        ahead = products(0)
        for part in range(3):
            now, ahead = ahead, products(part + 1) if part < 2 else None
            parts.append(activate(*now))
        hidden, grad_pre = [jnp.concatenate(one, axis=1) for one in zip(*parts)]
        grads_in[slots[0]] = dot_tn(taken, grad_pre).astype(BF)
        grads_out[slots[1]] = dot_tn(hidden, grads).astype(BF)

        for k in range(2):
            bit = moves[k][2]
            for at in (steps - 1, bit):
                @pl.when((e == 0) & (j == at))
                def _():
                    first_copy(k, 0, at).start()

            @pl.when((e > 0) & (t == 0))
            def _():
                first_copy(k, 1, steps - 1).start()

            @pl.when((e > 0) & (j == bit))
            def _():
                store(k, 0).start()

            @pl.when((e > 0) & (t == steps - 1))
            def _():
                store(k, steps - 1).start()

        result_sum[...] += dot_nn(hidden, own_out)
        back_sum[...] += dot_nt(grad_pre, own_in)

        @pl.when(t == steps - 1)
        def _():
            returned = result_sum[...].astype(BF)

            @pl.when(e > 0)
            def _():
                leave("result", 0)
                stay("result", 0).wait()

            result[...] = returned.reshape(result.shape)

            @pl.when(e > 0)
            def _():
                keep_result().start()

            probs = probs_s[...]
            hot = iota(probs.shape, 1) == me * local + e
            gate = jnp.sum(jnp.where(hot, probs, 0.0), axis=1, keepdims=True)

            grad_gate = jnp.sum(
                raw[e].reshape(rows, width).astype(F32) * returned.astype(F32), axis=1, keepdims=True
            )
            slope = jnp.where(hot, 1.0, 0.0) - gate
            grad_logits = (probs * slope * grad_gate).astype(BF)
            router_o[...] += dot_tn(grad_logits, x_recv[e].reshape(rows, width))
            back = (back_sum[...] + dot_nn(grad_logits, wr[...])).astype(BF)
            back_send[e] = back.reshape(ranks, cap, width)
            send(False, e)

            @pl.when(e == 0)
            def _():
                send("result", 0)

        return carry

    lax.fori_loop(0, local * steps, body, 0)

    for at in range(2):
        for k in range(2):
            grads, got, bit = moves[k][:3]
            into = (steps - 1 - bit, 0)[at]
            first_copy(k, 0, (steps - 1, bit)[at]).wait_recv()
            grads[into] = (grads[into].astype(F32) + got[at].astype(F32)).astype(BF)
            out_copy(k, at).start()
    for e in range(local):
        arrive(False, e)
    for k in range(2):
        grads, got = moves[k][:2]
        first_copy(k, 1, steps - 1).wait_recv()
        grads[kept] = (grads[kept].astype(F32) + got[2].astype(F32)).astype(BF)
        out_copy(k, 2).start()
    for k in range(2):
        first_copy(k, 0, moves[k][2]).wait_send()
        first_copy(k, 1, steps - 1).wait_send()
        store(k, steps - 1).wait()
        for at in range(3):
            out_copy(k, at).wait()
    keep_result().wait()
    arrive("result", 0)
    for e in range(local):
        leave(True, e)
        leave(False, e)
        if e and late:
            leave(None, e)


def run_experts(x_send, raw, late_rows, late, weight_in, weight_out, wr, copies):
    ranks, local, cap, width = x_send.shape
    rows = ranks * cap
    hidden = weight_in.shape[2]
    chunk = hidden // copies
    experts = wr.shape[0]
    vmem = pl.BlockSpec(memory_space=pltpu.VMEM)
    hbm = pl.BlockSpec(memory_space=pl.ANY)
    block = (ranks, cap, width)
    dma = pltpu.SemaphoreType.DMA
    return pl.pallas_call(
        functools.partial(experts_kernel, ranks, copies, late),
        in_specs=[hbm, hbm, hbm, hbm, hbm, vmem],
        out_specs=(hbm, hbm, hbm, vmem) + (hbm,) * 4,
        out_shape=(
            jax.ShapeDtypeStruct(block, BF),
            jax.ShapeDtypeStruct(block, BF),
            jax.ShapeDtypeStruct(x_send.shape, BF),
            jax.ShapeDtypeStruct((experts, width), F32),
            jax.ShapeDtypeStruct((3, width, chunk), BF),
            jax.ShapeDtypeStruct((2, width, chunk), BF),
            jax.ShapeDtypeStruct((3, chunk, width), BF),
            jax.ShapeDtypeStruct((2, chunk, width), BF),
        ),
        scratch_shapes=[
            pltpu.VMEM((local,) + block, BF),
            pltpu.VMEM((local,) + block, BF),
            pltpu.VMEM((local,) + block, BF),
            pltpu.VMEM((2, width, chunk), BF),
            pltpu.VMEM((2, chunk, width), BF),
            pltpu.VMEM((copies + 2, width, chunk), BF),
            pltpu.VMEM((copies + 2, chunk, width), BF),
            pltpu.VMEM((3, width, chunk), BF),
            pltpu.VMEM((3, chunk, width), BF),
            pltpu.VMEM((rows, width), BF),
            pltpu.VMEM((rows, experts), F32),
            pltpu.VMEM((rows, width), F32),
            pltpu.VMEM((rows, width), F32),
            pltpu.VMEM(block, BF),
            dma((local, ranks)),
            dma((local, ranks)),
            dma((local, ranks)),
            dma((local, ranks)),
            dma((local, ranks)),
            dma((local, ranks)),
            dma((1, ranks)),
            dma((1, ranks)),
            dma((local,)),
            dma((2, 2)),
            dma((2, 3)),
            dma((2, 3)),
            dma,
            dma((2, 4)),
        ],
        compiler_params=params(collective_id=0, has_side_effects=True),
        cost_estimate=pl.CostEstimate(
            flops=12 * local * rows * width * hidden,
            bytes_accessed=8 * local * width * hidden,
            transcendentals=local * rows * hidden,
        ),
        name="experts",
    )(x_send, raw, late_rows, weight_in, weight_out, wr)


PIECES = 4


def sums_inside(width, copies, ranks):
    return ranks == 2 * copies and width % (16 * copies * copies) == 0


def backward_kernel(
    head_dim, seq_len, buckets, copies, ranks,
    tokens_i, gain_one, normed_i, ids_i, q, k, v, att_i, inv, soft, wq, wk, wv,
    back_i, slot_col_i, residual_i, grad_i, gain_two, wo_i, gate_i, router,
    first, returned, next_in, next_out,
    grad_tokens_o, mixed_o, pieces_o, small_o, got_in_o, got_out_o,
    back, slot_col, residual, grad, wo, att, normed, ids, gate,
    score_sums, normed_sum, low_res, grad_att, grad_gain_two, results, parts, part_got, level_got, level_sum, last_got, last_sum,
    small_s, small_all, small_core, small_line, small_plane, small_half,
    r_ss, r_rs, c_ss, c_rs, l1_ss, l1_rs, l2_ss, l2_rs, g2_ss, g2_rs, g1_ss, g1_rs, h_ss, h_rs,
    own_sem, w_ss, w_rs, m_ss, m_rs, load_sem,
):
    step = pl.program_id(0)
    steps = pl.num_programs(0)
    rows, width = residual.shape
    group = wq.shape[1]
    seqs = rows // seq_len
    bits = bits_of(copies)
    me = lax.axis_index("expert")
    copy = lax.axis_index("dp")
    core = me % 2
    line = me // 2
    mesh_id = pl.DeviceIdType.MESH
    inside = sums_inside(width, copies, ranks)
    count = copies

    def remote(source, target, sends, recvs, device):
        return pltpu.make_async_remote_copy(
            src_ref=source, dst_ref=target, send_sem=sends, recv_sem=recvs,
            device_id=device, device_id_type=mesh_id,
        )


    def result_copy(at, peer):
        return remote(
            returned.at[peer], results.at[at, 1], r_ss.at[peer], r_rs.at[at], {"expert": peer}
        )

    def result_stay():
        return pltpu.make_async_copy(returned.at[me], results.at[me, 1], r_rs.at[me])

    def results_start():
        def one(i, carry):
            result_copy(me, (me + nth_far(i, ranks)) % ranks).start()
            return carry

        lax.fori_loop(0, ranks - 1, one, 0)
        result_stay().start()

    def results_wait():
        def one(d, carry):
            peer = (me + ranks - d) % ranks
            result_copy(peer, peer).wait_recv()
            result_copy(me, (me + d) % ranks).wait_send()
            return carry

        lax.fori_loop(1, ranks, one, 0)
        result_stay().wait()


    moves = (
        (next_in, got_in_o, bits[0], bits[1]),
        (next_out, got_out_o, bits[1], bits[0]),
    )
    shares = 3 * PARTS

    def share_copy(which, n, late):
        source, target, first, second = moves[which]
        at = 2 if late else (n - PARTS) // PARTS
        height = source.shape[1] // PARTS
        span = pl.ds(pl.multiple_of((n % PARTS) * height, 16), height)
        return remote(
            source.at[at, span], target.at[at, span], w_ss.at[which, n], w_rs.at[which, n],
            {"dp": flip(copy, first if late else second)},
        )

    def pump(first, count):
        def one(n, carry):
            @pl.when(n < PARTS)
            def _():
                for which in range(2):
                    share_copy(which, n, True).start()

            @pl.when(n >= PARTS)
            def _():
                for which in (1, 0):
                    share_copy(which, n, False).start()

            return carry

        if count:
            lax.fori_loop(first, jnp.minimum(first + count, shares), one, 0)

    def shares_end():
        def late(n, carry):
            for which in range(2):
                share_copy(which, n, True).wait()
            return carry

        def rest(n, carry):
            for which in range(2):
                share_copy(which, n, False).wait()
            return carry

        lax.fori_loop(0, PARTS, late, 0)
        lax.fori_loop(PARTS, shares, rest, 0)

    def paced(at):
        for p, stage in PLAN.get(at, ()):
            if p == "ret":
                results_start()
            elif inside:
                if p == "small":
                    small_stages[stage]()
                else:
                    stages[stage](p)


    def levels(p):
        along = (line, lambda i: {"expert": 2 * i + core})
        across = (copy, lambda i: {"dp": i})
        return (along, across) if p in ALONG_FIRST else (across, along)

    def core_copy(p):
        return remote(
            parts.at[p, 1 - core], part_got.at[p], c_ss.at[p], c_rs.at[p], {"expert": me + 1 - 2 * core}
        )

    def first_copy(p, peer, at):
        (_, device), _ = levels(p)
        return remote(
            parts.at[p, core, pl.ds(peer * count, count)], level_got.at[p, at],
            l1_ss.at[p, peer], l1_rs.at[p, at], device(peer),
        )

    def second_copy(p, peer, at):
        _, (_, device) = levels(p)
        return remote(
            level_sum.at[p, peer], last_got.at[p, at], l2_ss.at[p, peer], l2_rs.at[p, at],
            device(peer),
        )

    def give_second(p, peer, at):
        (mine, _), (_, device) = levels(p)
        return remote(
            last_sum.at[p], pieces_o.at[p, core, mine * count + at],
            g2_ss.at[p, peer], g2_rs.at[p, at], device(peer),
        )

    def give_own(p):
        (mine, _), (own, _) = levels(p)
        return pltpu.make_async_copy(
            last_sum.at[p], pieces_o.at[p, core, mine * count + own], own_sem.at[p]
        )

    def give_first(p, peer, at):
        (_, device), _ = levels(p)
        block = pieces_o.at[p, core, pl.ds(at * count, count)]
        return remote(block, block, g1_ss.at[p, peer], g1_rs.at[p, at], device(peer))

    def give_core(p, half):
        block = pieces_o.at[p, half]
        return remote(block, block, h_ss.at[p], h_rs.at[p], {"expert": me + 1 - 2 * core})

    def others(own):
        return [(own + d) % count for d in range(1, count)]

    def piece_0(p):
        core_copy(p).start()

    def piece_1(p):
        (own, _), _ = levels(p)
        core_copy(p).wait_recv()
        parts[p, core] = (parts[p, core].astype(F32) + part_got[p].astype(F32)).astype(BF)
        for peer in others(own):
            first_copy(p, peer, own).start()

    def piece_2(p):
        (first, _), (own, _) = levels(p)
        total = parts[p, core, pl.ds(first * count, count)].astype(F32)
        for peer in others(first):
            first_copy(p, peer, peer).wait_recv()
            total += level_got[p, peer].astype(F32)
        level_sum[p] = total.astype(BF)
        for peer in others(own):
            second_copy(p, peer, own).start()

    def piece_3(p):
        _, (own, _) = levels(p)
        total = level_sum[p, own].astype(F32)
        for peer in others(own):
            second_copy(p, peer, peer).wait_recv()
            total += last_got[p, peer].astype(F32)
        last_sum[p] = total.astype(BF)
        for peer in others(own):
            give_second(p, peer, own).start()
        give_own(p).start()

    def piece_4(p):
        (first, _), (own, _) = levels(p)
        for peer in others(own):
            give_second(p, peer, peer).wait_recv()
        give_own(p).wait()
        for peer in others(first):
            give_first(p, peer, first).start()

    def piece_5(p):
        (first, _), _ = levels(p)
        for peer in others(first):
            give_first(p, peer, peer).wait_recv()
        give_core(p, core).start()

    def piece_6(p):
        (first, _), (own, _) = levels(p)
        give_core(p, 1 - core).wait_recv()
        core_copy(p).wait_send()
        give_core(p, core).wait_send()
        for peer in others(first):
            first_copy(p, peer, first).wait_send()
            give_first(p, peer, first).wait_send()
        for peer in others(own):
            second_copy(p, peer, own).wait_send()
            give_second(p, peer, own).wait_send()

    stages = (piece_0, piece_1, piece_2, piece_3, piece_4, piece_5, piece_6)


    half = small_half.shape[0]

    def small_copy(stage, peer, at):
        if stage == 0:
            source, target, device = small_s, small_core, {"expert": me + 1 - 2 * core}
        elif stage == 1:
            source, target, device = small_half, small_line.at[at], {"expert": 2 * peer + core}
        elif stage == 2:
            source, target, device = small_half, small_plane.at[at], {"dp": peer}
        else:
            source = small_all.at[pl.ds(pl.multiple_of(core * half, 8), half)]
            target, device = source, {"expert": me + 1 - 2 * core}
        return remote(source, target, m_ss.at[stage, peer], m_rs.at[stage, at], device)

    def small_0():
        small_copy(0, 0, 0).start()

    def small_1():
        small_copy(0, 0, 0).wait()
        span = pl.ds(pl.multiple_of(core * half, 8), half)
        small_half[...] = small_s[span] + small_core[span]
        for peer in others(line):
            small_copy(1, peer, line).start()

    def small_2():
        total = small_half[...]
        for peer in others(line):
            small_copy(1, peer, peer).wait_recv()
            total += small_line[peer]
        for peer in others(line):
            small_copy(1, peer, line).wait_send()
        small_half[...] = total
        for peer in others(copy):
            small_copy(2, peer, copy).start()

    def small_3():
        total = small_half[...]
        for peer in others(copy):
            small_copy(2, peer, peer).wait_recv()
            total += small_plane[peer]
        small_all[pl.ds(pl.multiple_of(core * half, 8), half)] = total
        small_copy(3, 0, 0).start()

    def small_4():
        for peer in others(copy):
            small_copy(2, peer, copy).wait_send()
        small_copy(3, 0, 0).wait()

    def load_tokens():
        return pltpu.make_async_copy(tokens_i, low_res, load_sem.at[10])

    small_stages = (small_0, small_1, small_2, small_3, small_4)

    @pl.when(step == 0)
    def _():
        barrier = pltpu.get_barrier_semaphore()

        def greet(axis, own, size):
            def one(d, carry):
                pl.semaphore_signal(
                    barrier, inc=1, device_id={axis: (own + d) % size}, device_id_type=mesh_id
                )
                return carry

            lax.fori_loop(1, size, one, 0)

        greet("expert", me, ranks)
        greet("dp", copy, copies)
        pl.semaphore_wait(barrier, ranks + copies - 2)
        pump(0, PUMP_FIRST)
        paced("start")
        loads = [
            pltpu.make_async_copy(source, target, load_sem.at[at])
            for at, (source, target) in enumerate((
                (back_i, back), (slot_col_i, slot_col), (residual_i, residual), (grad_i, grad),
                (wo_i, wo), (att_i, att), (normed_i, normed), (ids_i, ids), (gate_i, gate),
                (first, results.at[:, 0]),
            ))
        ]
        for one in loads:
            one.start()
        for one in loads[:6]:
            one.wait()


        height = rows // 4

        def block(i, gain):
            pump(PUMP_FIRST + PUMP_MIDDLE * i, PUMP_MIDDLE)
            span = pl.ds(pl.multiple_of(i * height, height), height)
            pick = (slot_col[span, :] == iota((height, back.shape[0]), 1)).astype(BF)
            upstream = dot_nn(pick, back[...])
            values = residual[span, :]
            factor = lax.rsqrt(jnp.mean(values * values, axis=-1, keepdims=True) + EPSILON)
            weighted = upstream * gain_two[...][None, :]
            mean = jnp.mean(weighted * values, axis=-1, keepdims=True)
            grad_residual = (
                grad[span, :].astype(F32)
                + factor * weighted
                - values * (factor * factor * factor) * mean
            )
            grad_tokens_o[span, :] = grad_residual
            low = grad_residual.astype(BF)
            low_res[span, :] = low
            grad_att[span, :] = dot_nt(low, wo[...]).astype(BF)
            return gain + jnp.sum(upstream * values * factor, axis=0, keepdims=True)

        grad_gain_two[...] = lax.fori_loop(0, 4, block, jnp.zeros((1, width), F32))
        grad_wo = dot_tn(att[...], low_res[...]).astype(BF)
        for side in range(2):
            across = slice(side * (width // 2), (side + 1) * (width // 2))
            parts[PIECES - 1, side] = grad_wo[:, across].reshape(parts.shape[2:])
        for one in loads[6:]:
            one.wait()
        load_tokens().start()
        paced("middle")


    per_step = group // head_dim
    here = pl.ds(pl.multiple_of(step * group, group), group)
    lane = iota((seq_len, group), 1)
    query_sum = [None] * seqs
    key_rows = [[] for _ in range(seqs)]
    value_rows = [[] for _ in range(seqs)]
    low_grads, inners, grads_t, queries_t = [], [], [], []
    for seq in range(seqs):
        span = slice(seq * seq_len, (seq + 1) * seq_len)
        low_grads.append((grad_att[span, here].astype(F32) * inv[span, :]).astype(BF))
        inners.append(low_grads[seq].astype(F32) * att[span, here].astype(F32))
        grads_t.append(low_grads[seq].T)
        queries_t.append(q[span, :].T)
    for head in range(per_step):
        mine = (lane >= head * head_dim) & (lane < (head + 1) * head_dim)
        own = slice(head * head_dim, (head + 1) * head_dim)
        total = None
        for seq in range(seqs):
            span = slice(seq * seq_len, (seq + 1) * seq_len)
            grad_probs = dot_nt(jnp.where(mine, low_grads[seq], 0).astype(BF), v[span, :])
            row_inner = jnp.sum(jnp.where(mine, inners[seq], 0.0), axis=-1, keepdims=True)
            low_soft = soft[head, seq]
            scores = (low_soft.astype(F32) * (grad_probs - row_inner)).astype(BF)
            total = scores if seq == 0 else total + scores
            value_rows[seq].append(dot_nn(grads_t[seq][own, :], low_soft))
            key_rows[seq].append(dot_nn(queries_t[seq][own, :], scores))
            grad_query = dot_nn(scores, k[span, :])
            query_sum[seq] = grad_query if head == 0 else jnp.where(mine, grad_query, query_sum[seq])
        score_sums[step * per_step + head] = total
        if head < per_step - 1:
            pump(PUMP_FIRST + 4 * PUMP_MIDDLE + 2 * PUMP_STEP * step, PUMP_STEP)
            for after in range(width // group):
                if (after, 0) in PLAN:
                    @pl.when(step == after)
                    def _():
                        paced((after, 0))
    grads = [
        [(one * 0.125).astype(BF) for one in query_sum],
        [(jnp.concatenate(one, axis=0).T * 0.125).astype(BF) for one in key_rows],
        [jnp.concatenate(one, axis=0).T.astype(BF) for one in value_rows],
    ]
    grads = jnp.concatenate([jnp.concatenate(one, axis=0) for one in grads], axis=1)
    weights = jnp.concatenate([wq[...], wk[...], wv[...]], axis=1)
    parts[step // 2, step % 2] = dot_tn(normed[...], grads).astype(BF).reshape(parts.shape[2:])
    part = dot_nt(grads, weights)

    @pl.when(step == 0)
    def _():
        normed_sum[...] = part

    @pl.when(step > 0)
    def _():
        normed_sum[...] += part

    pump(PUMP_FIRST + 4 * PUMP_MIDDLE + 2 * PUMP_STEP * step + PUMP_STEP, PUMP_STEP)
    for after in range(width // group):
        if (after, 1) in PLAN:
            @pl.when(step == after)
            def _():
                paced((after, 1))

    @pl.when(step == steps - 1)
    def _():
        load_tokens().wait()
        upstream = normed_sum[...]
        values = low_res[...].astype(F32)
        factor = lax.rsqrt(jnp.mean(values * values, axis=-1, keepdims=True) + EPSILON)
        weighted = upstream * gain_one[...][None, :]
        mean = jnp.mean(weighted * values, axis=-1, keepdims=True)
        gain = jnp.sum(upstream * values * factor, axis=0, keepdims=True)
        grad_tokens_o[...] = (
            grad_tokens_o[...]
            + factor * weighted
            - values * (factor * factor * factor) * mean
        )
        pump(PUMP_FIRST + 4 * PUMP_MIDDLE + 2 * PUMP_STEP * (width // group), PUMP_LAST)
        paced("norm")
        heads = score_sums.shape[0]
        rows_at = 16

        def add(block, sums):
            at = pl.multiple_of(block * rows_at, rows_at)
            own = ids[pl.ds(at, rows_at), :]
            hot = own[:, None, :] == iota((rows_at, buckets, seq_len), 1)
            hot = hot.astype(BF).reshape(rows_at * buckets, seq_len)
            scores = score_sums[:, pl.ds(at, rows_at), :].reshape(heads * rows_at, seq_len)
            return sums + dot_nt(hot, scores)

        sums = jnp.zeros((rows_at * buckets, heads * rows_at), F32)
        sums = lax.fori_loop(0, seq_len // rows_at, add, sums)
        sums = sums.reshape(rows_at, buckets, heads * rows_at)
        across = iota(sums.shape, 2)
        keep = iota(sums.shape, 0) == across % rows_at
        sums = jnp.sum(jnp.where(keep, sums, 0.0), axis=0)
        into = iota((heads * rows_at, LANES), 0) // rows_at == iota((heads * rows_at, LANES), 1)
        bucket = lax.dot_general(
            sums, into.astype(F32), (((1,), (0,)), ((), ())),
            precision=lax.Precision.HIGHEST, preferred_element_type=F32,
        )
        small_s[...] = jnp.zeros_like(small_s)
        tiles = width // LANES
        experts = router.shape[0]
        for tile in range(tiles):
            cols = slice(tile * LANES, (tile + 1) * LANES)
            small_s[tile:tile + 1, :] = gain[:, cols]
            small_s[8 + tile:9 + tile, :] = grad_gain_two[:, cols]
            at = 16 + buckets + tile * experts
            small_s[at:at + experts, :] = router[:, cols]
        small_s[16:16 + buckets, :] = bucket
        pump(PUMP_FIRST + 4 * PUMP_MIDDLE + 2 * PUMP_STEP * (width // group) + PUMP_LAST, shares)
        paced("bucket")
        small_o[...] = small_all[...] if inside else small_s[...]
        results_wait()

        height = rows // 4

        def mix(i, carry):
            span = pl.ds(pl.multiple_of(i * height, height), height)
            pick = (slot_col[span, :] == iota((height, back.shape[0]), 1)).astype(BF)
            combined = dot_nn(pick, results[...].reshape(back.shape))
            grad[span, :] = (residual[span, :] + gate[span, :] * combined).astype(BF)
            return carry

        lax.fori_loop(0, 4, mix, 0)
        out = pltpu.make_async_copy(grad, mixed_o, load_sem.at[0])
        out.start()
        paced("mixed")
        shares_end()
        out.wait()
        if not inside:
            for p in range(PIECES):
                out = pltpu.make_async_copy(parts.at[p], pieces_o.at[p], own_sem.at[p])
                out.start()
                out.wait()


ALONG_FIRST = (3, 0, 1)
PARTS = 12
PUMP_FIRST, PUMP_MIDDLE, PUMP_STEP, PUMP_LAST = 2, 1, 2, 2
PLAN = {
    "start": (("ret", 1),),
    "middle": ((3, 0),),
    (1, 0): ((3, 1),),
    (2, 0): ((0, 0),),
    (2, 1): ((0, 1),),
    (3, 0): ((3, 2),),
    (3, 1): ((1, 0), (1, 1), (3, 3)),
    (4, 1): ((3, 4), (0, 2)),
    (5, 0): ((0, 3),),
    (5, 1): ((1, 2), (2, 0), (0, 4), (2, 1)),
    "norm": ((3, 5), (1, 3)),
    "bucket": (
        ("small", 0), (2, 2), ("small", 1), (2, 3), ("small", 2), (1, 4), ("small", 3), (2, 4),
        ("small", 4), (0, 5),
    ),
    "mixed": ((2, 5), (0, 6), (1, 5), (3, 6), (2, 6), (1, 6)),
}


def backward(
    tokens, gain_one, normed, bucket_ids, q, k, v, att, inv, soft, weights,
    back, slot_col, residual, grad, gain_two, wo, gate, router, first, returned, shares,
    head_dim, buckets, copies, ranks,
):
    rows, width = tokens.shape
    seq_len = bucket_ids.shape[0]
    heads, seqs = soft.shape[:2]
    local = 2
    experts = router.shape[0]
    chunk = shares[0].shape[2]
    slots = back.shape[0]
    group = LANES
    steps = width // group
    per_step = heads // steps
    inside = sums_inside(width, copies, ranks)
    chips = copies * copies if inside else 1
    block = (width // chips, width // 2)
    small_rows = -(-(16 + buckets + width // LANES * experts) // 16) * 16
    cols = lambda shape: pl.BlockSpec(shape, lambda g: (0, g))
    once = lambda shape: pl.BlockSpec(
        shape, lambda g: (0,) * len(shape), pipeline_mode=pl.Buffered(1)
    )
    hbm = pl.BlockSpec(memory_space=pl.ANY)
    dma = pltpu.SemaphoreType.DMA
    each = dma((PIECES, copies))
    return pl.pallas_call(
        functools.partial(backward_kernel, head_dim, seq_len, buckets, copies, ranks),
        grid=(steps,),
        in_specs=[
            hbm,
            once((width,)),
            hbm,
            hbm,
            cols((rows, group)),
            cols((rows, group)),
            cols((rows, group)),
            hbm,
            cols((rows, group)),
            pl.BlockSpec((per_step, seqs, seq_len, seq_len), lambda g: (g, 0, 0, 0)),
            cols((width, group)),
            cols((width, group)),
            cols((width, group)),
            hbm,
            hbm,
            hbm,
            hbm,
            once((width,)),
            hbm,
            hbm,
            once((experts, width)),
        ]
        + [hbm] * 4,
        out_specs=(
            once((rows, width)),
            hbm,
            hbm,
            once((small_rows, LANES)),
            hbm,
            hbm,
        ),
        scratch_shapes=[
            pltpu.VMEM((slots, width), BF),
            pltpu.VMEM((rows, 1), jnp.int32),
            pltpu.VMEM((rows, width), F32),
            pltpu.VMEM((rows, width), BF),
            pltpu.VMEM((width, width), BF),
            pltpu.VMEM((rows, width), BF),
            pltpu.VMEM((rows, width), BF),
            pltpu.VMEM((seq_len, seq_len), jnp.int32),
            pltpu.VMEM((rows, 1), F32),
            pltpu.VMEM((heads, seq_len, seq_len), BF),
            pltpu.VMEM((rows, width), F32),
            pltpu.VMEM((rows, width), BF),
            pltpu.VMEM((rows, width), BF),
            pltpu.VMEM((1, width), F32),
            pltpu.VMEM((ranks, local) + returned.shape[1:], BF),
            pltpu.VMEM((PIECES, 2, chips) + block, BF),
            pltpu.VMEM((PIECES, chips) + block, BF),
            pltpu.VMEM((PIECES, copies, copies) + block if inside else (8, LANES), BF),
            pltpu.VMEM((PIECES, copies) + block if inside else (8, LANES), BF),
            pltpu.VMEM((PIECES, copies) + block if inside else (8, LANES), BF),
            pltpu.VMEM((PIECES,) + block, BF),
            pltpu.VMEM((small_rows, LANES), F32),
            pltpu.VMEM((small_rows, LANES), F32),
            pltpu.VMEM((small_rows, LANES), F32),
            pltpu.VMEM((copies, small_rows // 2, LANES), F32),
            pltpu.VMEM((copies, small_rows // 2, LANES), F32),
            pltpu.VMEM((small_rows // 2, LANES), F32),
            dma((ranks,)),
            dma((ranks,)),
            dma((PIECES,)),
            dma((PIECES,)),
            each, each, each, each, each, each, each, each,
            dma((PIECES,)),
            dma((PIECES,)),
            dma((PIECES,)),
            dma((2, 3 * PARTS)),
            dma((2, 3 * PARTS)),
            dma((4, copies)),
            dma((4, copies)),
            dma((11,)),
        ],
        out_shape=(
            jax.ShapeDtypeStruct((rows, width), F32),
            jax.ShapeDtypeStruct((rows, width), BF),
            jax.ShapeDtypeStruct((PIECES, 2, chips) + block, BF),
            jax.ShapeDtypeStruct((small_rows, LANES), F32),
            jax.ShapeDtypeStruct((3, width, chunk), BF),
            jax.ShapeDtypeStruct((3, chunk, width), BF),
        ),
        compiler_params=params(
            dimension_semantics=("arbitrary",), collective_id=1, has_side_effects=True
        ),
        cost_estimate=pl.CostEstimate(
            flops=2 * rows * width * (6 * width + 5 * seq_len * 4),
            bytes_accessed=50 << 20,
            transcendentals=0,
        ),
        name="backward",
    )(
        tokens, gain_one, normed, bucket_ids, q, k, v, att, inv, soft, *weights,
        back, slot_col, residual, grad, gain_two, wo, gate, router, first, returned, *shares,
    )


def finish_kernel(
    pieces, keep_in, got_in, keep_out, got_out, small, wq_o, wk_o, wv_o, wo_o, grad_in_o, grad_out_o,
    gain_one_o, gain_two_o, router_o, bucket_o,
):
    width = wo_o.shape[1]
    half = width // 2
    part = half // 3
    for step in range(width // part):
        block = pieces[step // 2, step % 2].astype(F32)
        for at, out in enumerate((wq_o, wk_o, wv_o)):
            out[:, step * part:(step + 1) * part] = block[:, at * part:(at + 1) * part]
    for side in range(2):
        wo_o[:, side * half:(side + 1) * half] = pieces[PIECES - 1, side].astype(F32)
    for keep, got, out in ((keep_in, got_in, grad_in_o), (keep_out, got_out, grad_out_o)):
        out[0] = keep[0].astype(F32) + got[0].astype(F32)
        out[1] = keep[1].astype(F32) + got[1].astype(F32) + got[2].astype(F32)

    @pl.when(pl.program_id(0) == 0)
    def _():
        heads, buckets = bucket_o.shape
        experts = router_o.shape[0]
        for tile in range(width // LANES):
            cols = slice(tile * LANES, (tile + 1) * LANES)
            gain_one_o[cols] = small[tile, :]
            gain_two_o[cols] = small[8 + tile, :]
            at = 16 + buckets + tile * experts
            router_o[:, cols] = small[at:at + experts, :]
        bucket_o[...] = small[16:16 + buckets, :].T[:heads, :]


def finish(pieces, keep_in, got_in, keep_out, got_out, small, experts, heads, buckets):
    width, chunk = keep_in.shape[1:]
    count = 2
    pieces = pieces.reshape(PIECES, 2, width, width // 2)
    part = width // count
    rows = pl.BlockSpec((part, width), lambda i: (i, 0))
    square = jax.ShapeDtypeStruct((width, width), F32)
    little = ((width,), (width,), (experts, width), (heads, buckets))
    by_in = lambda lead: pl.BlockSpec((lead, part, chunk), lambda i: (0, i, 0))
    by_out = lambda lead: pl.BlockSpec((lead, chunk // count, width), lambda i: (0, i, 0))
    return pl.pallas_call(
        finish_kernel,
        grid=(count,),
        in_specs=[
            pl.BlockSpec((PIECES, 2, part, width // 2), lambda i: (0, 0, i, 0)),
            by_in(2),
            by_in(3),
            by_out(2),
            by_out(3),
            whole(small.shape),
        ],
        out_specs=(rows, rows, rows, rows, by_in(2), by_out(2))
        + tuple(whole(shape) for shape in little),
        out_shape=(
            square,
            square,
            square,
            square,
            jax.ShapeDtypeStruct((2, width, chunk), F32),
            jax.ShapeDtypeStruct((2, chunk, width), F32),
        )
        + tuple(jax.ShapeDtypeStruct(shape, F32) for shape in little),
        compiler_params=params(dimension_semantics=("arbitrary",)),
        cost_estimate=pl.CostEstimate(flops=1 << 20, bytes_accessed=30 << 20, transcendentals=0),
        name="finish",
    )(pieces, keep_in, got_in, keep_out, got_out, small)


def per_device(
    tokens,
    expert_ids,
    bucket_ids,
    attn_gain,
    ffn_gain,
    query_weight,
    key_weight,
    value_weight,
    output_weight,
    router_weight,
    bucket_bias,
    expert_in,
    expert_out,
    grad_output,
):
    tok_rows, width = tokens.shape
    buckets, heads = bucket_bias.shape
    head_dim = width // heads
    local = expert_in.shape[0]
    ranks = lax.axis_size("expert")
    copies = lax.axis_size("dp")
    experts = local * ranks
    cap = (5 * tok_rows + 4 * experts - 1) // (4 * experts)
    room = -(-cap // 16) * 16
    slots = experts * room
    gains = (attn_gain, ffn_gain)

    blocks = (ranks, local, room, width)
    late = (room * LATE_TENTHS // 10) // 16 * 16 if room > 16 else 0
    router_rows = router_weight.T
    (
        normed, q, k, v, att, inv, soft, residual, gate, slot_col, row_slots, grad_slots, late_grads
    ) = forward(
        tokens, bucket_ids, bucket_bias.T, gains,
        (query_weight, key_weight, value_weight, output_weight),
        router_rows, expert_ids.reshape(1, tok_rows), grad_output, blocks, late, cap, head_dim,
    )
    first, returned, back, router, next_in, keep_in, next_out, keep_out = run_experts(
        row_slots.reshape(blocks), grad_slots, late_grads, late, expert_in, expert_out, router_rows, copies,
    )
    grad_tokens, mixed, pieces, small, got_in, got_out = backward(
        tokens, gains[0], normed, bucket_ids, q, k, v, att, inv, soft,
        (query_weight, key_weight, value_weight), back.reshape(slots, width), slot_col, residual,
        grad_output, gains[1], output_weight, gate, router, first, returned, (next_in, next_out),
        head_dim, buckets, copies, ranks,
    )
    if not sums_inside(width, copies, ranks):
        pieces = lax.psum(pieces.astype(F32), ("dp", "expert"))
        small = lax.psum(small, ("dp", "expert"))
    (
        grad_wq, grad_wk, grad_wv, grad_wo, grad_expert_in, grad_expert_out,
        grad_attn_gain, grad_ffn_gain, grad_router, grad_bucket,
    ) = finish(pieces, keep_in, got_in, keep_out, got_out, small, experts, heads, buckets)
    return (
        mixed,
        grad_tokens,
        grad_attn_gain,
        grad_ffn_gain,
        grad_wq,
        grad_wk,
        grad_wv,
        grad_wo,
        grad_router.T,
        grad_bucket.T,
        grad_expert_in,
        grad_expert_out,
    )


def solution(mesh):
    shared = P()
    rows = P(("dp", "expert"), None)
    expert = P("expert", None, None)
    return jax.shard_map(
        per_device,
        mesh=mesh,
        in_specs=(rows, rows) + (shared,) * 9 + (expert, expert, rows),
        out_specs=(rows, rows) + (shared,) * 8 + (P("expert", None, "dp"), P("expert", "dp", None)),
        check_vma=False,
    )
```

```python
import functools

import jax
import jax.numpy as jnp
from jax import lax
from jax.experimental import pallas as pl
from jax.experimental.pallas import tpu as pltpu
from jax.sharding import PartitionSpec as P

EPSILON = 1e-06
BF = jnp.bfloat16
F32 = jnp.float32
LANES = 128
VMEM_BYTES = 62 * 1024 * 1024


def dot_nn(left, right):
    return lax.dot_general(left, right, (((1,), (0,)), ((), ())), preferred_element_type=F32)


def dot_nt(left, right):
    return lax.dot_general(left, right, (((1,), (1,)), ((), ())), preferred_element_type=F32)


def dot_tn(left, right):
    return lax.dot_general(left, right, (((0,), (0,)), ((), ())), preferred_element_type=F32)


def iota(shape, axis):
    return lax.broadcasted_iota(jnp.int32, shape, axis)


def whole(shape):
    return pl.BlockSpec(shape, lambda *_: (0,) * len(shape))


def nth_far(i, size):
    return size // 2 + ((i + 1) // 2) * (2 * (i % 2) - 1)


def params(**more):
    return pltpu.CompilerParams(vmem_limit_bytes=VMEM_BYTES, **more)


def forward_kernel(
    head_dim, seq_len, cap, late_rows,
    tokens, ids, table, gain_one, gain_two, wq, wk, wv, wo, wr, ids_row, grad,
    normed_o, q_o, k_o, v_o, att_o, inv_o, soft_o, residual_o, gate_o, slot_col_o, slots_o, raw_o,
    late_o,
    slot_row, grad_slots, table_s, send_sem, recv_sem, own_sem,
):
    step = pl.program_id(0)
    rows, width = tokens.shape
    group = wq.shape[1]
    ranks, local, room = grad_slots.shape[:3]
    experts = ranks * local
    me = lax.axis_index("expert")

    early = room - late_rows

    def raw_span(e):
        return pl.ds(0, early if e else room)

    def raw_copy(e, at, peer):
        return pltpu.make_async_remote_copy(
            src_ref=grad_slots.at[peer, e, raw_span(e)],
            dst_ref=raw_o.at[at, e, raw_span(e)],
            send_sem=send_sem.at[e, peer],
            recv_sem=recv_sem.at[e, at],
            device_id={"expert": peer},
            device_id_type=pl.DeviceIdType.MESH,
        )

    def raw_stay(e):
        return pltpu.make_async_copy(
            grad_slots.at[me, e, raw_span(e)], raw_o.at[me, e, raw_span(e)], own_sem.at[e]
        )

    def late_keep(e):
        return pltpu.make_async_copy(
            grad_slots.at[:, e, pl.ds(early, room - early)], late_o.at[e - 1], own_sem.at[local + e]
        )

    def column(row):
        return jnp.broadcast_to(row, (8, rows)).T[:, :1]

    @pl.when(step == 0)
    def _():
        barrier = pltpu.get_barrier_semaphore()

        def greet(d, carry):
            pl.semaphore_signal(
                barrier, inc=1, device_id={"expert": (me + d) % ranks},
                device_id_type=pl.DeviceIdType.MESH,
            )
            return carry

        lax.fori_loop(1, ranks, greet, 0)
        table_s[...] = jnp.zeros_like(table_s)
        table_s[:, :table.shape[1]] = table[...]
        hot = ids_row[...] == iota((experts, rows), 0)
        earlier = (iota((rows, rows), 0) < iota((rows, rows), 1)).astype(BF)
        counts = dot_nn(hot.astype(BF), earlier)
        place = jnp.sum(jnp.where(hot, counts, 0.0), axis=0, keepdims=True).astype(jnp.int32)
        slot = jnp.where(place < cap, ids_row[...] * room + place, -1)
        slot_row[...] = slot
        pl.semaphore_wait(barrier, ranks - 1)

        def pick_rows(peer):
            each = local * room
            pick = (iota((each, rows), 0) + peer * each == slot).astype(BF)
            grad_slots[peer] = dot_nn(pick, grad[...]).astype(BF).reshape(local, room, width)

        for e in range(local):
            def send(i, carry):
                peer = (me + nth_far(i, ranks)) % ranks
                if e == 0:
                    pick_rows(peer)
                raw_copy(e, me, peer).start()
                return carry

            lax.fori_loop(0, ranks - 1, send, 0)
            if e == 0:
                pick_rows(me)
            raw_stay(e).start()
            if e and early < room:
                late_keep(e).start()
        slot_col_o[...] = column(slot)
        x = tokens[...].astype(F32)
        factor = lax.rsqrt(jnp.mean(x * x, axis=-1, keepdims=True) + EPSILON)
        normed_o[...] = (x * factor * gain_one[...][None, :]).astype(BF)
        residual_o[...] = x

    normed = normed_o[...]
    q_o[...] = dot_nn(normed, wq[...]).astype(BF)
    k_o[...] = dot_nn(normed, wk[...]).astype(BF)
    v_o[...] = dot_nn(normed, wv[...]).astype(BF)
    lane = iota((seq_len, LANES), 1)
    per_tile = LANES // head_dim
    per_group = group // head_dim
    for tile in range(group // LANES):
        cols = slice(tile * LANES, (tile + 1) * LANES)
        gathered = [None] * (rows // seq_len)
        scaled = [None] * (rows // seq_len)
        for part in range(per_tile):
            head = tile * per_tile + part
            mine = (lane >= part * head_dim) & (lane < (part + 1) * head_dim)
            row = jnp.broadcast_to(table_s[pl.ds(step * per_group + head, 1), :], (seq_len, LANES))
            bias = jnp.concatenate(
                [
                    jnp.take_along_axis(
                        row, ids[:, c:c + LANES], axis=1, mode="promise_in_bounds"
                    )
                    for c in range(0, seq_len, LANES)
                ],
                axis=1,
            )
            for seq in range(rows // seq_len):
                span = slice(seq * seq_len, (seq + 1) * seq_len)
                query = jnp.where(mine, q_o[span, cols] * 0.125, 0).astype(BF)
                scores = dot_nt(query, k_o[span, cols]) + bias
                low = jnp.exp(scores - jnp.max(scores, axis=-1, keepdims=True)).astype(BF)
                soft_o[head, seq] = low
                out = dot_nn(low, jnp.where(mine, v_o[span, cols], 1.0).astype(BF))
                inverse = 1.0 / pltpu.roll(out, head_dim, 1)
                out = out * inverse
                if part == 0:
                    gathered[seq], scaled[seq] = out, inverse
                else:
                    gathered[seq] = jnp.where(mine, out, gathered[seq])
                    scaled[seq] = jnp.where(mine, inverse, scaled[seq])
        for seq in range(rows // seq_len):
            span = slice(seq * seq_len, (seq + 1) * seq_len)
            att_o[span, cols] = gathered[seq].astype(BF)
            inv_o[span, cols] = scaled[seq]
    residual_o[...] += dot_nn(att_o[...], wo[...])

    @pl.when(step == pl.num_programs(0) - 1)
    def _():
        residual = residual_o[...]
        factor = lax.rsqrt(jnp.mean(residual * residual, axis=-1, keepdims=True) + EPSILON)
        low = (residual * factor * gain_two[...][None, :]).astype(BF)
        logits = dot_nt(low, wr[...])
        weights = jnp.exp(logits - jnp.max(logits, axis=-1, keepdims=True))
        probs = weights / jnp.sum(weights, axis=-1, keepdims=True)
        hot = column(ids_row[...]) == iota(logits.shape, 1)
        gate_o[...] = jnp.sum(jnp.where(hot, probs, 0.0), axis=1, keepdims=True)
        pick = (iota((slots_o.shape[0], rows), 0) == slot_row[...]).astype(BF)
        slots_o[...] = dot_nn(pick, low).astype(BF)

        for e in range(local):
            def finish(d, carry):
                peer = (me + ranks - d) % ranks
                raw_copy(e, peer, peer).wait_recv()
                raw_copy(e, me, (me + d) % ranks).wait_send()
                return carry

            lax.fori_loop(1, ranks, finish, 0)
            raw_stay(e).wait()
            if e and early < room:
                late_keep(e).wait()


def forward(
    tokens, bucket_ids, table, gains, weights, wr, ids_row, grad, blocks, late, cap, head_dim
):
    rows, width = tokens.shape
    seq_len = bucket_ids.shape[0]
    heads = table.shape[0]
    per_group = 4
    groups = heads // per_group
    group = width // groups
    seqs = rows // seq_len
    ranks, local, room = blocks[:3]
    slots = ranks * local * room
    dma = pltpu.SemaphoreType.DMA
    cols = lambda shape: pl.BlockSpec(shape, lambda g: (0, g))
    wq, wk, wv, wo = weights
    return pl.pallas_call(
        functools.partial(forward_kernel, head_dim, seq_len, cap, late),
        grid=(groups,),
        in_specs=[
            whole((rows, width)),
            whole((seq_len, seq_len)),
            whole(table.shape),
            whole((width,)),
            whole((width,)),
            cols((width, group)),
            cols((width, group)),
            cols((width, group)),
            pl.BlockSpec((group, width), lambda g: (g, 0)),
            whole(wr.shape),
            whole((1, rows)),
            whole((rows, width)),
        ],
        out_specs=(
            whole((rows, width)),
            cols((rows, group)),
            cols((rows, group)),
            cols((rows, group)),
            cols((rows, group)),
            cols((rows, group)),
            pl.BlockSpec((per_group, seqs, seq_len, seq_len), lambda g: (g, 0, 0, 0)),
            whole((rows, width)),
            whole((rows, 1)),
            whole((rows, 1)),
            whole((slots, width)),
            pl.BlockSpec(memory_space=pl.ANY),
            pl.BlockSpec(memory_space=pl.ANY),
        ),
        scratch_shapes=[
            pltpu.VMEM((1, rows), jnp.int32),
            pltpu.VMEM(blocks, BF),
            pltpu.VMEM((heads, LANES), F32),
            dma((local, ranks)),
            dma((local, ranks)),
            dma((2 * local,)),
        ],
        out_shape=(
            jax.ShapeDtypeStruct((rows, width), BF),
            jax.ShapeDtypeStruct((rows, width), BF),
            jax.ShapeDtypeStruct((rows, width), BF),
            jax.ShapeDtypeStruct((rows, width), BF),
            jax.ShapeDtypeStruct((rows, width), BF),
            jax.ShapeDtypeStruct((rows, width), F32),
            jax.ShapeDtypeStruct((heads, seqs, seq_len, seq_len), BF),
            jax.ShapeDtypeStruct((rows, width), F32),
            jax.ShapeDtypeStruct((rows, 1), F32),
            jax.ShapeDtypeStruct((rows, 1), jnp.int32),
            jax.ShapeDtypeStruct((slots, width), BF),
            jax.ShapeDtypeStruct(blocks, BF),
            jax.ShapeDtypeStruct((local - 1, ranks, max(late, 16), width), BF),
        ),
        compiler_params=params(
            dimension_semantics=("arbitrary",), collective_id=2, has_side_effects=True
        ),
        cost_estimate=pl.CostEstimate(
            flops=2 * rows * width * (4 * width + 2 * seq_len * 4),
            bytes_accessed=40 << 20,
            transcendentals=heads * rows * seq_len,
        ),
        name="forward",
    )(tokens, bucket_ids, table, *gains, wq, wk, wv, wo, wr, ids_row, grad)


LATE_TENTHS = 6


def bits_of(size):
    return [1 << i for i in range(size.bit_length() - 1)]


def flip(index, bit):
    return index + bit * (1 - 2 * ((index // bit) % 2))


def flip_all(index, mask, bits):
    for bit in bits:
        index = jnp.where((mask // bit) % 2 == 1, flip(index, bit), index)
    return index


def experts_kernel(
    ranks, copies, late,
    x_send, raw_i, late_i, weight_in, weight_out, wr,
    returned_o, back_o, router_o, next_in_o, keep_in_o, next_out_o, keep_out_o,
    x_recv, raw, back_send, win, wout, grads_in, grads_out, got_in, got_out,
    scaled, probs_s, back_sum, result_sum, result,
    x_ss, x_rs, b_ss, b_rs, l_ss, l_rs, raw_sem, w_sem, first_ss, first_rs, result_sem, out_sem,
):
    local, cap, width = x_send.shape[1:]
    rows = ranks * cap
    chunk = win.shape[2]
    steps = copies
    bits = bits_of(copies)
    orders = (bits, bits[::-1])
    me = lax.axis_index("expert")
    copy = lax.axis_index("dp")
    mesh_id = pl.DeviceIdType.MESH

    barrier = pltpu.get_barrier_semaphore()

    def greet(d, carry):
        pl.semaphore_signal(
            barrier, inc=1, device_id={"expert": (me + d) % ranks}, device_id_type=mesh_id
        )
        return carry

    lax.fori_loop(1, ranks, greet, 0)
    for bit in bits:
        pl.semaphore_signal(
            barrier, inc=1, device_id={"dp": flip(copy, bit)}, device_id_type=mesh_id
        )

    def load(s):
        e, j = s // steps, steps - 1 - s % steps
        at = pl.multiple_of(flip_all(copy, j, bits) * chunk, chunk)
        return (
            pltpu.make_async_copy(
                weight_in.at[e, :, pl.ds(at, chunk)], win.at[s % 2], w_sem.at[0, s % 2]
            ),
            pltpu.make_async_copy(
                weight_out.at[e, pl.ds(at, chunk), :], wout.at[s % 2], w_sem.at[1, s % 2]
            ),
        )

    for one in load(0):
        one.start()
    pl.semaphore_wait(barrier, ranks - 1 + len(bits))


    early = cap - late

    def raw_load(e):
        span = pl.ds(0, early if e else cap)
        return pltpu.make_async_copy(
            raw_i.at[:, e, span], raw.at[e, :, span], raw_sem.at[e]
        )

    def row_copy(out, e, at, peer):
        if out is None:
            source = late_i.at[e - 1, peer]
            target, sends, recvs = raw.at[e, at, pl.ds(early, late)], l_ss, l_rs
        elif out:
            source, target, sends, recvs = x_send.at[peer, e], x_recv.at[e, at], x_ss, x_rs
        else:
            source, target, sends, recvs = back_send.at[e, peer], back_o.at[at, e], b_ss, b_rs
        return pltpu.make_async_remote_copy(
            src_ref=source,
            dst_ref=target,
            send_sem=sends.at[e, peer],
            recv_sem=recvs.at[e, at],
            device_id={"expert": peer},
            device_id_type=mesh_id,
        )

    def stay(out, e):
        if out is None:
            return pltpu.make_async_copy(
                late_i.at[e - 1, me], raw.at[e, me, pl.ds(early, late)], l_rs.at[e, me]
            )
        if out:
            return pltpu.make_async_copy(x_send.at[me, e], x_recv.at[e, me], x_rs.at[e, me])
        return pltpu.make_async_copy(back_send.at[e, me], back_o.at[me, e], b_rs.at[e, me])

    def send(out, e):
        def one(i, carry):
            row_copy(out, e, me, (me + nth_far(i, ranks)) % ranks).start()
            return carry

        lax.fori_loop(0, ranks - 1, one, 0)
        stay(out, e).start()

    def arrive(out, e):
        def one(d, carry):
            peer = (me + ranks - d) % ranks
            row_copy(out, e, peer, peer).wait_recv()
            return carry

        lax.fori_loop(1, ranks, one, 0)
        stay(out, e).wait()

    def leave(out, e):
        def one(d, carry):
            row_copy(out, e, me, (me + d) % ranks).wait_send()
            return carry

        lax.fori_loop(1, ranks, one, 0)

    moves = (
        (grads_in, got_in, bits[0], next_in_o, keep_in_o),
        (grads_out, got_out, bits[1], next_out_o, keep_out_o),
    )
    spare, kept = steps, steps + 1

    def first_copy(k, e, j):
        grads, got, bit = moves[k][:3]
        at = 2 if e else (0 if j == steps - 1 else 1)
        return pltpu.make_async_remote_copy(
            src_ref=grads.at[spare if e else j],
            dst_ref=got.at[at],
            send_sem=first_ss.at[k, at],
            recv_sem=first_rs.at[k, at],
            device_id={"dp": flip(copy, bit)},
            device_id_type=mesh_id,
        )

    def store(k, t):
        grads, _, _, following, keep = moves[k]
        target = keep.at[1] if t == steps - 1 else following.at[2]
        return pltpu.make_async_copy(grads.at[steps - 1], target, out_sem.at[k, 0])

    def out_copy(k, at):
        grads, _, bit, following, keep = moves[k]
        source, target = (
            (grads.at[steps - 1 - bit], following.at[0]),
            (grads.at[0], keep.at[0]),
            (grads.at[kept], following.at[1]),
        )[at]
        return pltpu.make_async_copy(source, target, out_sem.at[k, 1 + at])

    def keep_result(e):
        return pltpu.make_async_copy(result, returned_o.at[e], result_sem)

    send(True, 0)
    for e in range(local):
        raw_load(e).start()
    router_o[...] = jnp.zeros_like(router_o)

    def body(s, carry):
        e, t = s // steps, s % steps
        j = steps - 1 - t

        @pl.when(s + 1 < local * steps)
        def _():
            for one in load(s + 1):
                one.start()

        @pl.when(t == 0)
        def _():
            arrive(True, e)

            @pl.when(e == 0)
            def _():
                raw_load(0).wait()
                for other in range(1, local):
                    if late:
                        send(None, other)
                    send(True, other)

            @pl.when(e > 0)
            def _():
                raw_load(1).wait()
                if late:
                    arrive(None, e)

            logits = dot_nt(x_recv[e].reshape(rows, width), wr[...])
            weights = jnp.exp(logits - jnp.max(logits, axis=-1, keepdims=True))
            probs = weights / jnp.sum(weights, axis=-1, keepdims=True)
            probs_s[...] = probs
            hot = iota(logits.shape, 1) == me * local + e
            gate = jnp.sum(jnp.where(hot, probs, 0.0), axis=1, keepdims=True)

            scaled[...] = (gate * raw[e].reshape(rows, width).astype(F32)).astype(BF)
            back_sum[...] = jnp.zeros_like(back_sum)
            result_sum[...] = jnp.zeros_like(result_sum)

        for one in load(s):
            one.wait()

        late_at = [steps - 1 - moves[k][2] for k in range(2)]
        slots = [
            jnp.where(
                e == 0, j, jnp.where(t == 0, spare, jnp.where(j == late_at[k], kept, steps - 1))
            )
            for k in range(2)
        ]
        for k in range(2):
            bit = moves[k][2]

            @pl.when((e > 0) & (j == bit))
            def _():
                first_copy(k, 0, steps - 1).wait_send()

            @pl.when((e > 0) & (t == steps - 1))
            def _():
                store(k, 0).wait()

        own_in, own_out = win[s % 2], wout[s % 2]
        taken = x_recv[e].reshape(rows, width)
        grads = scaled[...]


        def products(part):
            span = slice(part * (chunk // 3), (part + 1) * (chunk // 3))
            return dot_nn(taken, own_in[:, span]), dot_nt(grads, own_out[span, :])

        def activate(pre, grad_hidden):
            scale = 0.7978845608028654
            square = pre * pre
            bent = jnp.tanh(pre * (scale + (scale * 0.044715) * square))
            half = 0.5 + 0.5 * bent
            slope = half + pre * (half * (1.0 - bent)) * (scale + (scale * 0.134145) * square)
            return (pre * half).astype(BF), (grad_hidden * slope).astype(BF)

        parts = []
        ahead = products(0)
        for part in range(3):
            now, ahead = ahead, products(part + 1) if part < 2 else None
            parts.append(activate(*now))
        hidden, grad_pre = [jnp.concatenate(one, axis=1) for one in zip(*parts)]
        grads_in[slots[0]] = dot_tn(taken, grad_pre).astype(BF)
        grads_out[slots[1]] = dot_tn(hidden, grads).astype(BF)

        for k in range(2):
            bit = moves[k][2]
            for at in (steps - 1, bit):
                @pl.when((e == 0) & (j == at))
                def _():
                    first_copy(k, 0, at).start()

            @pl.when((e > 0) & (t == 0))
            def _():
                first_copy(k, 1, steps - 1).start()

            @pl.when((e > 0) & (j == bit))
            def _():
                store(k, 0).start()

            @pl.when((e > 0) & (t == steps - 1))
            def _():
                store(k, steps - 1).start()

        result_sum[...] += dot_nn(hidden, own_out)
        back_sum[...] += dot_nt(grad_pre, own_in)

        @pl.when(t == steps - 1)
        def _():
            returned = result_sum[...].astype(BF)

            @pl.when(e > 0)
            def _():
                keep_result(e - 1).wait()

            result[...] = returned.reshape(result.shape)
            keep_result(e).start()
            probs = probs_s[...]
            hot = iota(probs.shape, 1) == me * local + e
            gate = jnp.sum(jnp.where(hot, probs, 0.0), axis=1, keepdims=True)

            grad_gate = jnp.sum(
                raw[e].reshape(rows, width).astype(F32) * returned.astype(F32), axis=1, keepdims=True
            )
            slope = jnp.where(hot, 1.0, 0.0) - gate
            grad_logits = (probs * slope * grad_gate).astype(BF)
            router_o[...] += dot_tn(grad_logits, x_recv[e].reshape(rows, width))
            back = (back_sum[...] + dot_nn(grad_logits, wr[...])).astype(BF)
            back_send[e] = back.reshape(ranks, cap, width)
            send(False, e)

        return carry

    lax.fori_loop(0, local * steps, body, 0)

    for at in range(2):
        for k in range(2):
            grads, got, bit = moves[k][:3]
            into = (steps - 1 - bit, 0)[at]
            first_copy(k, 0, (steps - 1, bit)[at]).wait_recv()
            grads[into] = (grads[into].astype(F32) + got[at].astype(F32)).astype(BF)
            out_copy(k, at).start()
    for e in range(local):
        arrive(False, e)
    for k in range(2):
        grads, got = moves[k][:2]
        first_copy(k, 1, steps - 1).wait_recv()
        grads[kept] = (grads[kept].astype(F32) + got[2].astype(F32)).astype(BF)
        out_copy(k, 2).start()
    for k in range(2):
        first_copy(k, 0, moves[k][2]).wait_send()
        first_copy(k, 1, steps - 1).wait_send()
        store(k, steps - 1).wait()
        for at in range(3):
            out_copy(k, at).wait()
    keep_result(local - 1).wait()
    for e in range(local):
        leave(True, e)
        leave(False, e)
        if e and late:
            leave(None, e)


def run_experts(x_send, raw, late_rows, late, weight_in, weight_out, wr, copies):
    ranks, local, cap, width = x_send.shape
    rows = ranks * cap
    hidden = weight_in.shape[2]
    chunk = hidden // copies
    experts = wr.shape[0]
    vmem = pl.BlockSpec(memory_space=pltpu.VMEM)
    hbm = pl.BlockSpec(memory_space=pl.ANY)
    block = (ranks, cap, width)
    dma = pltpu.SemaphoreType.DMA
    return pl.pallas_call(
        functools.partial(experts_kernel, ranks, copies, late),
        in_specs=[hbm, hbm, hbm, hbm, hbm, vmem],
        out_specs=(hbm, hbm, vmem) + (hbm,) * 4,
        out_shape=(
            jax.ShapeDtypeStruct((local,) + block, BF),
            jax.ShapeDtypeStruct(x_send.shape, BF),
            jax.ShapeDtypeStruct((experts, width), F32),
            jax.ShapeDtypeStruct((3, width, chunk), BF),
            jax.ShapeDtypeStruct((2, width, chunk), BF),
            jax.ShapeDtypeStruct((3, chunk, width), BF),
            jax.ShapeDtypeStruct((2, chunk, width), BF),
        ),
        scratch_shapes=[
            pltpu.VMEM((local,) + block, BF),
            pltpu.VMEM((local,) + block, BF),
            pltpu.VMEM((local,) + block, BF),
            pltpu.VMEM((2, width, chunk), BF),
            pltpu.VMEM((2, chunk, width), BF),
            pltpu.VMEM((copies + 2, width, chunk), BF),
            pltpu.VMEM((copies + 2, chunk, width), BF),
            pltpu.VMEM((3, width, chunk), BF),
            pltpu.VMEM((3, chunk, width), BF),
            pltpu.VMEM((rows, width), BF),
            pltpu.VMEM((rows, experts), F32),
            pltpu.VMEM((rows, width), F32),
            pltpu.VMEM((rows, width), F32),
            pltpu.VMEM(block, BF),
            dma((local, ranks)),
            dma((local, ranks)),
            dma((local, ranks)),
            dma((local, ranks)),
            dma((local, ranks)),
            dma((local, ranks)),
            dma((local,)),
            dma((2, 2)),
            dma((2, 3)),
            dma((2, 3)),
            dma,
            dma((2, 4)),
        ],
        compiler_params=params(collective_id=0, has_side_effects=True),
        cost_estimate=pl.CostEstimate(
            flops=12 * local * rows * width * hidden,
            bytes_accessed=8 * local * width * hidden,
            transcendentals=local * rows * hidden,
        ),
        name="experts",
    )(x_send, raw, late_rows, weight_in, weight_out, wr)


PIECES = 4


def sums_inside(width, copies, ranks):
    return ranks == 2 * copies and width % (16 * copies * copies) == 0


def backward_kernel(
    head_dim, seq_len, buckets, copies, ranks,
    tokens_i, gain_one, normed_i, ids_i, q, k, v, att_i, inv, soft, wq, wk, wv,
    back_i, slot_col_i, residual_i, grad_i, gain_two, wo_i, gate_i, router,
    returned, next_in, next_out,
    grad_tokens_o, mixed_o, pieces_o, small_o, got_in_o, got_out_o,
    back, slot_col, residual, grad, wo, att, normed, ids, gate,
    score_sums, normed_sum, low_res, grad_att, grad_gain_two, results, parts, part_got, level_got, level_sum, last_got, last_sum,
    small_s, small_all, small_core, small_line, small_plane, small_half,
    r_ss, r_rs, c_ss, c_rs, l1_ss, l1_rs, l2_ss, l2_rs, g2_ss, g2_rs, g1_ss, g1_rs, h_ss, h_rs,
    own_sem, w_ss, w_rs, m_ss, m_rs, load_sem,
):
    step = pl.program_id(0)
    steps = pl.num_programs(0)
    rows, width = residual.shape
    group = wq.shape[1]
    seqs = rows // seq_len
    local = returned.shape[0]
    bits = bits_of(copies)
    me = lax.axis_index("expert")
    copy = lax.axis_index("dp")
    core = me % 2
    line = me // 2
    mesh_id = pl.DeviceIdType.MESH
    inside = sums_inside(width, copies, ranks)
    count = copies

    def remote(source, target, sends, recvs, device):
        return pltpu.make_async_remote_copy(
            src_ref=source, dst_ref=target, send_sem=sends, recv_sem=recvs,
            device_id=device, device_id_type=mesh_id,
        )


    def result_copy(e, at, peer):
        return remote(
            returned.at[e, peer], results.at[at, e], r_ss.at[e, peer], r_rs.at[e, at],
            {"expert": peer},
        )

    def result_stay(e):
        return pltpu.make_async_copy(returned.at[e, me], results.at[me, e], r_rs.at[e, me])

    def results_start(e):
        def one(d, carry):
            result_copy(e, me, (me + d) % ranks).start()
            return carry

        lax.fori_loop(1, ranks, one, 0)
        result_stay(e).start()

    def results_wait(e):
        def one(d, carry):
            peer = (me + ranks - d) % ranks
            result_copy(e, peer, peer).wait_recv()
            result_copy(e, me, (me + d) % ranks).wait_send()
            return carry

        lax.fori_loop(1, ranks, one, 0)
        result_stay(e).wait()


    moves = (
        (next_in, got_in_o, bits[0], bits[1]),
        (next_out, got_out_o, bits[1], bits[0]),
    )
    shares = 3 * PARTS

    def share_copy(which, n, late):
        source, target, first, second = moves[which]
        at = 2 if late else (n - PARTS) // PARTS
        height = source.shape[1] // PARTS
        span = pl.ds(pl.multiple_of((n % PARTS) * height, 16), height)
        return remote(
            source.at[at, span], target.at[at, span], w_ss.at[which, n], w_rs.at[which, n],
            {"dp": flip(copy, first if late else second)},
        )

    def pump(first, count):
        def one(n, carry):
            @pl.when(n < PARTS)
            def _():
                for which in range(2):
                    share_copy(which, n, True).start()

            @pl.when(n >= PARTS)
            def _():
                for which in (1, 0):
                    share_copy(which, n, False).start()

            return carry

        if count:
            lax.fori_loop(first, jnp.minimum(first + count, shares), one, 0)

    def shares_end():
        def late(n, carry):
            for which in range(2):
                share_copy(which, n, True).wait()
            return carry

        def rest(n, carry):
            for which in range(2):
                share_copy(which, n, False).wait()
            return carry

        lax.fori_loop(0, PARTS, late, 0)
        lax.fori_loop(PARTS, shares, rest, 0)

    def paced(at):
        for p, stage in PLAN.get(at, ()):
            if p == "ret":
                results_start(stage)
            elif inside:
                if p == "small":
                    small_stages[stage]()
                else:
                    stages[stage](p)


    def levels(p):
        along = (line, lambda i: {"expert": 2 * i + core})
        across = (copy, lambda i: {"dp": i})
        return (along, across) if p in ALONG_FIRST else (across, along)

    def core_copy(p):
        return remote(
            parts.at[p, 1 - core], part_got.at[p], c_ss.at[p], c_rs.at[p], {"expert": me + 1 - 2 * core}
        )

    def first_copy(p, peer, at):
        (_, device), _ = levels(p)
        return remote(
            parts.at[p, core, pl.ds(peer * count, count)], level_got.at[p, at],
            l1_ss.at[p, peer], l1_rs.at[p, at], device(peer),
        )

    def second_copy(p, peer, at):
        _, (_, device) = levels(p)
        return remote(
            level_sum.at[p, peer], last_got.at[p, at], l2_ss.at[p, peer], l2_rs.at[p, at],
            device(peer),
        )

    def give_second(p, peer, at):
        (mine, _), (_, device) = levels(p)
        return remote(
            last_sum.at[p], pieces_o.at[p, core, mine * count + at],
            g2_ss.at[p, peer], g2_rs.at[p, at], device(peer),
        )

    def give_own(p):
        (mine, _), (own, _) = levels(p)
        return pltpu.make_async_copy(
            last_sum.at[p], pieces_o.at[p, core, mine * count + own], own_sem.at[p]
        )

    def give_first(p, peer, at):
        (_, device), _ = levels(p)
        block = pieces_o.at[p, core, pl.ds(at * count, count)]
        return remote(block, block, g1_ss.at[p, peer], g1_rs.at[p, at], device(peer))

    def give_core(p, half):
        block = pieces_o.at[p, half]
        return remote(block, block, h_ss.at[p], h_rs.at[p], {"expert": me + 1 - 2 * core})

    def others(own):
        return [(own + d) % count for d in range(1, count)]

    def piece_0(p):
        core_copy(p).start()

    def piece_1(p):
        (own, _), _ = levels(p)
        core_copy(p).wait_recv()
        parts[p, core] = (parts[p, core].astype(F32) + part_got[p].astype(F32)).astype(BF)
        for peer in others(own):
            first_copy(p, peer, own).start()

    def piece_2(p):
        (first, _), (own, _) = levels(p)
        total = parts[p, core, pl.ds(first * count, count)].astype(F32)
        for peer in others(first):
            first_copy(p, peer, peer).wait_recv()
            total += level_got[p, peer].astype(F32)
        level_sum[p] = total.astype(BF)
        for peer in others(own):
            second_copy(p, peer, own).start()

    def piece_3(p):
        _, (own, _) = levels(p)
        total = level_sum[p, own].astype(F32)
        for peer in others(own):
            second_copy(p, peer, peer).wait_recv()
            total += last_got[p, peer].astype(F32)
        last_sum[p] = total.astype(BF)
        for peer in others(own):
            give_second(p, peer, own).start()
        give_own(p).start()

    def piece_4(p):
        (first, _), (own, _) = levels(p)
        for peer in others(own):
            give_second(p, peer, peer).wait_recv()
        give_own(p).wait()
        for peer in others(first):
            give_first(p, peer, first).start()

    def piece_5(p):
        (first, _), _ = levels(p)
        for peer in others(first):
            give_first(p, peer, peer).wait_recv()
        give_core(p, core).start()

    def piece_6(p):
        (first, _), (own, _) = levels(p)
        give_core(p, 1 - core).wait_recv()
        core_copy(p).wait_send()
        give_core(p, core).wait_send()
        for peer in others(first):
            first_copy(p, peer, first).wait_send()
            give_first(p, peer, first).wait_send()
        for peer in others(own):
            second_copy(p, peer, own).wait_send()
            give_second(p, peer, own).wait_send()

    stages = (piece_0, piece_1, piece_2, piece_3, piece_4, piece_5, piece_6)


    half = small_half.shape[0]

    def small_copy(stage, peer, at):
        if stage == 0:
            source, target, device = small_s, small_core, {"expert": me + 1 - 2 * core}
        elif stage == 1:
            source, target, device = small_half, small_line.at[at], {"expert": 2 * peer + core}
        elif stage == 2:
            source, target, device = small_half, small_plane.at[at], {"dp": peer}
        else:
            source = small_all.at[pl.ds(pl.multiple_of(core * half, 8), half)]
            target, device = source, {"expert": me + 1 - 2 * core}
        return remote(source, target, m_ss.at[stage, peer], m_rs.at[stage, at], device)

    def small_0():
        small_copy(0, 0, 0).start()

    def small_1():
        small_copy(0, 0, 0).wait()
        span = pl.ds(pl.multiple_of(core * half, 8), half)
        small_half[...] = small_s[span] + small_core[span]
        for peer in others(line):
            small_copy(1, peer, line).start()

    def small_2():
        total = small_half[...]
        for peer in others(line):
            small_copy(1, peer, peer).wait_recv()
            total += small_line[peer]
        for peer in others(line):
            small_copy(1, peer, line).wait_send()
        small_half[...] = total
        for peer in others(copy):
            small_copy(2, peer, copy).start()

    def small_3():
        total = small_half[...]
        for peer in others(copy):
            small_copy(2, peer, peer).wait_recv()
            total += small_plane[peer]
        small_all[pl.ds(pl.multiple_of(core * half, 8), half)] = total
        small_copy(3, 0, 0).start()

    def small_4():
        for peer in others(copy):
            small_copy(2, peer, copy).wait_send()
        small_copy(3, 0, 0).wait()

    def load_tokens():
        return pltpu.make_async_copy(tokens_i, low_res, load_sem.at[9])

    small_stages = (small_0, small_1, small_2, small_3, small_4)

    @pl.when(step == 0)
    def _():
        barrier = pltpu.get_barrier_semaphore()

        def greet(axis, own, size):
            def one(d, carry):
                pl.semaphore_signal(
                    barrier, inc=1, device_id={axis: (own + d) % size}, device_id_type=mesh_id
                )
                return carry

            lax.fori_loop(1, size, one, 0)

        greet("expert", me, ranks)
        greet("dp", copy, copies)
        pl.semaphore_wait(barrier, ranks + copies - 2)
        pump(0, PUMP_FIRST)
        paced("start")
        loads = [
            pltpu.make_async_copy(source, target, load_sem.at[at])
            for at, (source, target) in enumerate((
                (back_i, back), (slot_col_i, slot_col), (residual_i, residual), (grad_i, grad),
                (wo_i, wo), (att_i, att), (normed_i, normed), (ids_i, ids), (gate_i, gate),
            ))
        ]
        for one in loads:
            one.start()
        for one in loads[:6]:
            one.wait()


        height = rows // 4

        def block(i, gain):
            pump(PUMP_FIRST + PUMP_MIDDLE * i, PUMP_MIDDLE)
            span = pl.ds(pl.multiple_of(i * height, height), height)
            pick = (slot_col[span, :] == iota((height, back.shape[0]), 1)).astype(BF)
            upstream = dot_nn(pick, back[...])
            values = residual[span, :]
            factor = lax.rsqrt(jnp.mean(values * values, axis=-1, keepdims=True) + EPSILON)
            weighted = upstream * gain_two[...][None, :]
            mean = jnp.mean(weighted * values, axis=-1, keepdims=True)
            grad_residual = (
                grad[span, :].astype(F32)
                + factor * weighted
                - values * (factor * factor * factor) * mean
            )
            grad_tokens_o[span, :] = grad_residual
            low = grad_residual.astype(BF)
            low_res[span, :] = low
            grad_att[span, :] = dot_nt(low, wo[...]).astype(BF)
            return gain + jnp.sum(upstream * values * factor, axis=0, keepdims=True)

        grad_gain_two[...] = lax.fori_loop(0, 4, block, jnp.zeros((1, width), F32))
        grad_wo = dot_tn(att[...], low_res[...]).astype(BF)
        for side in range(2):
            across = slice(side * (width // 2), (side + 1) * (width // 2))
            parts[PIECES - 1, side] = grad_wo[:, across].reshape(parts.shape[2:])
        for one in loads[6:]:
            one.wait()
        load_tokens().start()
        paced("middle")


    per_step = group // head_dim
    here = pl.ds(pl.multiple_of(step * group, group), group)
    lane = iota((seq_len, group), 1)
    query_sum = [None] * seqs
    key_rows = [[] for _ in range(seqs)]
    value_rows = [[] for _ in range(seqs)]
    low_grads, inners, grads_t, queries_t = [], [], [], []
    for seq in range(seqs):
        span = slice(seq * seq_len, (seq + 1) * seq_len)
        low_grads.append((grad_att[span, here].astype(F32) * inv[span, :]).astype(BF))
        inners.append(low_grads[seq].astype(F32) * att[span, here].astype(F32))
        grads_t.append(low_grads[seq].T)
        queries_t.append(q[span, :].T)
    for head in range(per_step):
        mine = (lane >= head * head_dim) & (lane < (head + 1) * head_dim)
        own = slice(head * head_dim, (head + 1) * head_dim)
        total = None
        for seq in range(seqs):
            span = slice(seq * seq_len, (seq + 1) * seq_len)
            grad_probs = dot_nt(jnp.where(mine, low_grads[seq], 0).astype(BF), v[span, :])
            row_inner = jnp.sum(jnp.where(mine, inners[seq], 0.0), axis=-1, keepdims=True)
            low_soft = soft[head, seq]
            scores = (low_soft.astype(F32) * (grad_probs - row_inner)).astype(BF)
            total = scores if seq == 0 else total + scores
            value_rows[seq].append(dot_nn(grads_t[seq][own, :], low_soft))
            key_rows[seq].append(dot_nn(queries_t[seq][own, :], scores))
            grad_query = dot_nn(scores, k[span, :])
            query_sum[seq] = grad_query if head == 0 else jnp.where(mine, grad_query, query_sum[seq])
        score_sums[step * per_step + head] = total
        if head < per_step - 1:
            pump(PUMP_FIRST + 4 * PUMP_MIDDLE + 2 * PUMP_STEP * step, PUMP_STEP)
            for after in range(width // group):
                if (after, 0) in PLAN:
                    @pl.when(step == after)
                    def _():
                        paced((after, 0))
    grads = [
        [(one * 0.125).astype(BF) for one in query_sum],
        [(jnp.concatenate(one, axis=0).T * 0.125).astype(BF) for one in key_rows],
        [jnp.concatenate(one, axis=0).T.astype(BF) for one in value_rows],
    ]
    grads = jnp.concatenate([jnp.concatenate(one, axis=0) for one in grads], axis=1)
    weights = jnp.concatenate([wq[...], wk[...], wv[...]], axis=1)
    parts[step // 2, step % 2] = dot_tn(normed[...], grads).astype(BF).reshape(parts.shape[2:])
    part = dot_nt(grads, weights)

    @pl.when(step == 0)
    def _():
        normed_sum[...] = part

    @pl.when(step > 0)
    def _():
        normed_sum[...] += part

    pump(PUMP_FIRST + 4 * PUMP_MIDDLE + 2 * PUMP_STEP * step + PUMP_STEP, PUMP_STEP)
    for after in range(width // group):
        if (after, 1) in PLAN:
            @pl.when(step == after)
            def _():
                paced((after, 1))

    @pl.when(step == steps - 1)
    def _():
        load_tokens().wait()
        upstream = normed_sum[...]
        values = low_res[...].astype(F32)
        factor = lax.rsqrt(jnp.mean(values * values, axis=-1, keepdims=True) + EPSILON)
        weighted = upstream * gain_one[...][None, :]
        mean = jnp.mean(weighted * values, axis=-1, keepdims=True)
        gain = jnp.sum(upstream * values * factor, axis=0, keepdims=True)
        grad_tokens_o[...] = (
            grad_tokens_o[...]
            + factor * weighted
            - values * (factor * factor * factor) * mean
        )
        pump(PUMP_FIRST + 4 * PUMP_MIDDLE + 2 * PUMP_STEP * (width // group), PUMP_LAST)
        paced("norm")
        heads = score_sums.shape[0]
        rows_at = 16

        def add(block, sums):
            at = pl.multiple_of(block * rows_at, rows_at)
            own = ids[pl.ds(at, rows_at), :]
            hot = own[:, None, :] == iota((rows_at, buckets, seq_len), 1)
            hot = hot.astype(BF).reshape(rows_at * buckets, seq_len)
            scores = score_sums[:, pl.ds(at, rows_at), :].reshape(heads * rows_at, seq_len)
            return sums + dot_nt(hot, scores)

        sums = jnp.zeros((rows_at * buckets, heads * rows_at), F32)
        sums = lax.fori_loop(0, seq_len // rows_at, add, sums)
        sums = sums.reshape(rows_at, buckets, heads * rows_at)
        across = iota(sums.shape, 2)
        keep = iota(sums.shape, 0) == across % rows_at
        sums = jnp.sum(jnp.where(keep, sums, 0.0), axis=0)
        into = iota((heads * rows_at, LANES), 0) // rows_at == iota((heads * rows_at, LANES), 1)
        bucket = lax.dot_general(
            sums, into.astype(F32), (((1,), (0,)), ((), ())),
            precision=lax.Precision.HIGHEST, preferred_element_type=F32,
        )
        small_s[...] = jnp.zeros_like(small_s)
        tiles = width // LANES
        experts = router.shape[0]
        for tile in range(tiles):
            cols = slice(tile * LANES, (tile + 1) * LANES)
            small_s[tile:tile + 1, :] = gain[:, cols]
            small_s[8 + tile:9 + tile, :] = grad_gain_two[:, cols]
            at = 16 + buckets + tile * experts
            small_s[at:at + experts, :] = router[:, cols]
        small_s[16:16 + buckets, :] = bucket
        pump(PUMP_FIRST + 4 * PUMP_MIDDLE + 2 * PUMP_STEP * (width // group) + PUMP_LAST, shares)
        paced("bucket")
        small_o[...] = small_all[...] if inside else small_s[...]
        for e in range(local):
            results_wait(e)

        height = rows // 4

        def mix(i, carry):
            span = pl.ds(pl.multiple_of(i * height, height), height)
            pick = (slot_col[span, :] == iota((height, back.shape[0]), 1)).astype(BF)
            combined = dot_nn(pick, results[...].reshape(back.shape))
            grad[span, :] = (residual[span, :] + gate[span, :] * combined).astype(BF)
            return carry

        lax.fori_loop(0, 4, mix, 0)
        out = pltpu.make_async_copy(grad, mixed_o, load_sem.at[0])
        out.start()
        paced("mixed")
        shares_end()
        out.wait()
        if not inside:
            for p in range(PIECES):
                out = pltpu.make_async_copy(parts.at[p], pieces_o.at[p], own_sem.at[p])
                out.start()
                out.wait()


ALONG_FIRST = (0, 1)
PARTS = 12
PUMP_FIRST, PUMP_MIDDLE, PUMP_STEP, PUMP_LAST = 2, 1, 2, 2
PLAN = {
    "start": (("ret", 1),),
    "middle": ((3, 0),),
    (0, 1): ((3, 1),),
    (1, 1): ((0, 0),),
    (2, 0): ((0, 1),),
    (3, 1): ((1, 0), (3, 2)),
    (4, 0): ((1, 1), (0, 2)),
    (4, 1): (("ret", 0),),
    (5, 0): ((0, 3), (3, 3)),
    (5, 1): ((2, 0), (1, 2), (0, 4)),
    "norm": ((2, 1), (1, 3)),
    "bucket": (
        (2, 2), ("small", 0), ("small", 1), (2, 3), (1, 4), ("small", 2), (3, 4), (0, 5),
        ("small", 3), (0, 6), ("small", 4), (2, 4),
    ),
    "mixed": ((3, 5), (1, 5), (2, 5), (3, 6), (1, 6), (2, 6)),
}


def backward(
    tokens, gain_one, normed, bucket_ids, q, k, v, att, inv, soft, weights,
    back, slot_col, residual, grad, gain_two, wo, gate, router, returned, shares,
    head_dim, buckets, copies, ranks,
):
    rows, width = tokens.shape
    seq_len = bucket_ids.shape[0]
    heads, seqs = soft.shape[:2]
    local = returned.shape[0]
    experts = router.shape[0]
    chunk = shares[0].shape[2]
    slots = back.shape[0]
    group = LANES
    steps = width // group
    per_step = heads // steps
    inside = sums_inside(width, copies, ranks)
    chips = copies * copies if inside else 1
    block = (width // chips, width // 2)
    small_rows = -(-(16 + buckets + width // LANES * experts) // 16) * 16
    cols = lambda shape: pl.BlockSpec(shape, lambda g: (0, g))
    once = lambda shape: pl.BlockSpec(
        shape, lambda g: (0,) * len(shape), pipeline_mode=pl.Buffered(1)
    )
    hbm = pl.BlockSpec(memory_space=pl.ANY)
    dma = pltpu.SemaphoreType.DMA
    each = dma((PIECES, copies))
    return pl.pallas_call(
        functools.partial(backward_kernel, head_dim, seq_len, buckets, copies, ranks),
        grid=(steps,),
        in_specs=[
            hbm,
            once((width,)),
            hbm,
            hbm,
            cols((rows, group)),
            cols((rows, group)),
            cols((rows, group)),
            hbm,
            cols((rows, group)),
            pl.BlockSpec((per_step, seqs, seq_len, seq_len), lambda g: (g, 0, 0, 0)),
            cols((width, group)),
            cols((width, group)),
            cols((width, group)),
            hbm,
            hbm,
            hbm,
            hbm,
            once((width,)),
            hbm,
            hbm,
            once((experts, width)),
        ]
        + [hbm] * 3,
        out_specs=(
            once((rows, width)),
            hbm,
            hbm,
            once((small_rows, LANES)),
            hbm,
            hbm,
        ),
        scratch_shapes=[
            pltpu.VMEM((slots, width), BF),
            pltpu.VMEM((rows, 1), jnp.int32),
            pltpu.VMEM((rows, width), F32),
            pltpu.VMEM((rows, width), BF),
            pltpu.VMEM((width, width), BF),
            pltpu.VMEM((rows, width), BF),
            pltpu.VMEM((rows, width), BF),
            pltpu.VMEM((seq_len, seq_len), jnp.int32),
            pltpu.VMEM((rows, 1), F32),
            pltpu.VMEM((heads, seq_len, seq_len), BF),
            pltpu.VMEM((rows, width), F32),
            pltpu.VMEM((rows, width), BF),
            pltpu.VMEM((rows, width), BF),
            pltpu.VMEM((1, width), F32),
            pltpu.VMEM((ranks, local) + returned.shape[2:], BF),
            pltpu.VMEM((PIECES, 2, chips) + block, BF),
            pltpu.VMEM((PIECES, chips) + block, BF),
            pltpu.VMEM((PIECES, copies, copies) + block if inside else (8, LANES), BF),
            pltpu.VMEM((PIECES, copies) + block if inside else (8, LANES), BF),
            pltpu.VMEM((PIECES, copies) + block if inside else (8, LANES), BF),
            pltpu.VMEM((PIECES,) + block, BF),
            pltpu.VMEM((small_rows, LANES), F32),
            pltpu.VMEM((small_rows, LANES), F32),
            pltpu.VMEM((small_rows, LANES), F32),
            pltpu.VMEM((copies, small_rows // 2, LANES), F32),
            pltpu.VMEM((copies, small_rows // 2, LANES), F32),
            pltpu.VMEM((small_rows // 2, LANES), F32),
            dma((local, ranks)),
            dma((local, ranks)),
            dma((PIECES,)),
            dma((PIECES,)),
            each, each, each, each, each, each, each, each,
            dma((PIECES,)),
            dma((PIECES,)),
            dma((PIECES,)),
            dma((2, 3 * PARTS)),
            dma((2, 3 * PARTS)),
            dma((4, copies)),
            dma((4, copies)),
            dma((10,)),
        ],
        out_shape=(
            jax.ShapeDtypeStruct((rows, width), F32),
            jax.ShapeDtypeStruct((rows, width), BF),
            jax.ShapeDtypeStruct((PIECES, 2, chips) + block, BF),
            jax.ShapeDtypeStruct((small_rows, LANES), F32),
            jax.ShapeDtypeStruct((3, width, chunk), BF),
            jax.ShapeDtypeStruct((3, chunk, width), BF),
        ),
        compiler_params=params(
            dimension_semantics=("arbitrary",), collective_id=1, has_side_effects=True
        ),
        cost_estimate=pl.CostEstimate(
            flops=2 * rows * width * (6 * width + 5 * seq_len * 4),
            bytes_accessed=50 << 20,
            transcendentals=0,
        ),
        name="backward",
    )(
        tokens, gain_one, normed, bucket_ids, q, k, v, att, inv, soft, *weights,
        back, slot_col, residual, grad, gain_two, wo, gate, router, returned, *shares,
    )


def finish_kernel(
    pieces, keep_in, got_in, keep_out, got_out, small, wq_o, wk_o, wv_o, wo_o, grad_in_o, grad_out_o,
    gain_one_o, gain_two_o, router_o, bucket_o,
):
    width = wo_o.shape[1]
    half = width // 2
    part = half // 3
    for step in range(width // part):
        block = pieces[step // 2, step % 2].astype(F32)
        for at, out in enumerate((wq_o, wk_o, wv_o)):
            out[:, step * part:(step + 1) * part] = block[:, at * part:(at + 1) * part]
    for side in range(2):
        wo_o[:, side * half:(side + 1) * half] = pieces[PIECES - 1, side].astype(F32)
    for keep, got, out in ((keep_in, got_in, grad_in_o), (keep_out, got_out, grad_out_o)):
        out[0] = keep[0].astype(F32) + got[0].astype(F32)
        out[1] = keep[1].astype(F32) + got[1].astype(F32) + got[2].astype(F32)

    @pl.when(pl.program_id(0) == 0)
    def _():
        heads, buckets = bucket_o.shape
        experts = router_o.shape[0]
        for tile in range(width // LANES):
            cols = slice(tile * LANES, (tile + 1) * LANES)
            gain_one_o[cols] = small[tile, :]
            gain_two_o[cols] = small[8 + tile, :]
            at = 16 + buckets + tile * experts
            router_o[:, cols] = small[at:at + experts, :]
        bucket_o[...] = small[16:16 + buckets, :].T[:heads, :]


def finish(pieces, keep_in, got_in, keep_out, got_out, small, experts, heads, buckets):
    width, chunk = keep_in.shape[1:]
    count = 2
    pieces = pieces.reshape(PIECES, 2, width, width // 2)
    part = width // count
    rows = pl.BlockSpec((part, width), lambda i: (i, 0))
    square = jax.ShapeDtypeStruct((width, width), F32)
    little = ((width,), (width,), (experts, width), (heads, buckets))
    by_in = lambda lead: pl.BlockSpec((lead, part, chunk), lambda i: (0, i, 0))
    by_out = lambda lead: pl.BlockSpec((lead, chunk // count, width), lambda i: (0, i, 0))
    return pl.pallas_call(
        finish_kernel,
        grid=(count,),
        in_specs=[
            pl.BlockSpec((PIECES, 2, part, width // 2), lambda i: (0, 0, i, 0)),
            by_in(2),
            by_in(3),
            by_out(2),
            by_out(3),
            whole(small.shape),
        ],
        out_specs=(rows, rows, rows, rows, by_in(2), by_out(2))
        + tuple(whole(shape) for shape in little),
        out_shape=(
            square,
            square,
            square,
            square,
            jax.ShapeDtypeStruct((2, width, chunk), F32),
            jax.ShapeDtypeStruct((2, chunk, width), F32),
        )
        + tuple(jax.ShapeDtypeStruct(shape, F32) for shape in little),
        compiler_params=params(dimension_semantics=("arbitrary",)),
        cost_estimate=pl.CostEstimate(flops=1 << 20, bytes_accessed=30 << 20, transcendentals=0),
        name="finish",
    )(pieces, keep_in, got_in, keep_out, got_out, small)


def per_device(
    tokens,
    expert_ids,
    bucket_ids,
    attn_gain,
    ffn_gain,
    query_weight,
    key_weight,
    value_weight,
    output_weight,
    router_weight,
    bucket_bias,
    expert_in,
    expert_out,
    grad_output,
):
    tok_rows, width = tokens.shape
    buckets, heads = bucket_bias.shape
    head_dim = width // heads
    local = expert_in.shape[0]
    ranks = lax.axis_size("expert")
    copies = lax.axis_size("dp")
    experts = local * ranks
    cap = (5 * tok_rows + 4 * experts - 1) // (4 * experts)
    room = -(-cap // 16) * 16
    slots = experts * room
    gains = (attn_gain, ffn_gain)

    blocks = (ranks, local, room, width)
    late = (room * LATE_TENTHS // 10) // 16 * 16 if room > 16 else 0
    router_rows = router_weight.T
    (
        normed, q, k, v, att, inv, soft, residual, gate, slot_col, row_slots, grad_slots, late_grads
    ) = forward(
        tokens, bucket_ids, bucket_bias.T, gains,
        (query_weight, key_weight, value_weight, output_weight),
        router_rows, expert_ids.reshape(1, tok_rows), grad_output, blocks, late, cap, head_dim,
    )
    returned, back, router, next_in, keep_in, next_out, keep_out = run_experts(
        row_slots.reshape(blocks), grad_slots, late_grads, late, expert_in, expert_out, router_rows, copies,
    )
    grad_tokens, mixed, pieces, small, got_in, got_out = backward(
        tokens, gains[0], normed, bucket_ids, q, k, v, att, inv, soft,
        (query_weight, key_weight, value_weight), back.reshape(slots, width), slot_col, residual,
        grad_output, gains[1], output_weight, gate, router, returned, (next_in, next_out),
        head_dim, buckets, copies, ranks,
    )
    if not sums_inside(width, copies, ranks):
        pieces = lax.psum(pieces.astype(F32), ("dp", "expert"))
        small = lax.psum(small, ("dp", "expert"))
    (
        grad_wq, grad_wk, grad_wv, grad_wo, grad_expert_in, grad_expert_out,
        grad_attn_gain, grad_ffn_gain, grad_router, grad_bucket,
    ) = finish(pieces, keep_in, got_in, keep_out, got_out, small, experts, heads, buckets)
    return (
        mixed,
        grad_tokens,
        grad_attn_gain,
        grad_ffn_gain,
        grad_wq,
        grad_wk,
        grad_wv,
        grad_wo,
        grad_router.T,
        grad_bucket.T,
        grad_expert_in,
        grad_expert_out,
    )


def solution(mesh):
    shared = P()
    rows = P(("dp", "expert"), None)
    expert = P("expert", None, None)
    return jax.shard_map(
        per_device,
        mesh=mesh,
        in_specs=(rows, rows) + (shared,) * 9 + (expert, expert, rows),
        out_specs=(rows, rows) + (shared,) * 8 + (P("expert", None, "dp"), P("expert", "dp", None)),
        check_vma=False,
    )
```

```python
import functools

import jax
import jax.numpy as jnp
from jax import lax
from jax.experimental import pallas as pl
from jax.experimental.pallas import tpu as pltpu
from jax.sharding import PartitionSpec as P

EPSILON = 1e-06
BF = jnp.bfloat16
F32 = jnp.float32
LANES = 128
VMEM_BYTES = 62 * 1024 * 1024


def dot_nn(left, right):
    return lax.dot_general(left, right, (((1,), (0,)), ((), ())), preferred_element_type=F32)


def dot_nt(left, right):
    return lax.dot_general(left, right, (((1,), (1,)), ((), ())), preferred_element_type=F32)


def dot_tn(left, right):
    return lax.dot_general(left, right, (((0,), (0,)), ((), ())), preferred_element_type=F32)


def iota(shape, axis):
    return lax.broadcasted_iota(jnp.int32, shape, axis)


def whole(shape):
    return pl.BlockSpec(shape, lambda *_: (0,) * len(shape))


def nth_far(i, size):
    return size // 2 + ((i + 1) // 2) * (2 * (i % 2) - 1)


def params(**more):
    return pltpu.CompilerParams(vmem_limit_bytes=VMEM_BYTES, **more)


def forward_kernel(
    head_dim, seq_len, cap, late_rows,
    tokens, ids, table, gain_one, gain_two, wq, wk, wv, wo, wr, ids_row, grad,
    normed_o, q_o, k_o, v_o, att_o, inv_o, soft_o, residual_o, gate_o, slot_col_o, slots_o, raw_o,
    late_o,
    slot_row, grad_slots, table_s, send_sem, recv_sem, own_sem,
):
    step = pl.program_id(0)
    rows, width = tokens.shape
    group = wq.shape[1]
    ranks, local, room = grad_slots.shape[:3]
    experts = ranks * local
    me = lax.axis_index("expert")

    early = room - late_rows

    def raw_span(e):
        return pl.ds(0, early if e else room)

    def raw_copy(e, at, peer):
        return pltpu.make_async_remote_copy(
            src_ref=grad_slots.at[peer, e, raw_span(e)],
            dst_ref=raw_o.at[at, e, raw_span(e)],
            send_sem=send_sem.at[e, peer],
            recv_sem=recv_sem.at[e, at],
            device_id={"expert": peer},
            device_id_type=pl.DeviceIdType.MESH,
        )

    def raw_stay(e):
        return pltpu.make_async_copy(
            grad_slots.at[me, e, raw_span(e)], raw_o.at[me, e, raw_span(e)], own_sem.at[e]
        )

    def late_keep(e):
        return pltpu.make_async_copy(
            grad_slots.at[:, e, pl.ds(early, room - early)], late_o.at[e - 1], own_sem.at[local + e]
        )

    def column(row):
        return jnp.broadcast_to(row, (8, rows)).T[:, :1]

    @pl.when(step == 0)
    def _():
        barrier = pltpu.get_barrier_semaphore()

        def greet(d, carry):
            pl.semaphore_signal(
                barrier, inc=1, device_id={"expert": (me + d) % ranks},
                device_id_type=pl.DeviceIdType.MESH,
            )
            return carry

        lax.fori_loop(1, ranks, greet, 0)
        table_s[...] = jnp.zeros_like(table_s)
        table_s[:, :table.shape[1]] = table[...]
        hot = ids_row[...] == iota((experts, rows), 0)
        earlier = (iota((rows, rows), 0) < iota((rows, rows), 1)).astype(BF)
        counts = dot_nn(hot.astype(BF), earlier)
        place = jnp.sum(jnp.where(hot, counts, 0.0), axis=0, keepdims=True).astype(jnp.int32)
        slot = jnp.where(place < cap, ids_row[...] * room + place, -1)
        slot_row[...] = slot
        pl.semaphore_wait(barrier, ranks - 1)

        def pick_rows(peer):
            each = local * room
            pick = (iota((each, rows), 0) + peer * each == slot).astype(BF)
            grad_slots[peer] = dot_nn(pick, grad[...]).astype(BF).reshape(local, room, width)

        for e in range(local):
            def send(i, carry):
                peer = (me + nth_far(i, ranks)) % ranks
                if e == 0:
                    pick_rows(peer)
                raw_copy(e, me, peer).start()
                return carry

            lax.fori_loop(0, ranks - 1, send, 0)
            if e == 0:
                pick_rows(me)
            raw_stay(e).start()
            if e and early < room:
                late_keep(e).start()
        slot_col_o[...] = column(slot)
        x = tokens[...].astype(F32)
        factor = lax.rsqrt(jnp.mean(x * x, axis=-1, keepdims=True) + EPSILON)
        normed_o[...] = (x * factor * gain_one[...][None, :]).astype(BF)
        residual_o[...] = x

    normed = normed_o[...]
    q_o[...] = dot_nn(normed, wq[...]).astype(BF)
    k_o[...] = dot_nn(normed, wk[...]).astype(BF)
    v_o[...] = dot_nn(normed, wv[...]).astype(BF)
    lane = iota((seq_len, LANES), 1)
    per_tile = LANES // head_dim
    per_group = group // head_dim
    for tile in range(group // LANES):
        cols = slice(tile * LANES, (tile + 1) * LANES)
        gathered = [None] * (rows // seq_len)
        scaled = [None] * (rows // seq_len)
        for part in range(per_tile):
            head = tile * per_tile + part
            mine = (lane >= part * head_dim) & (lane < (part + 1) * head_dim)
            row = jnp.broadcast_to(table_s[pl.ds(step * per_group + head, 1), :], (seq_len, LANES))
            bias = jnp.concatenate(
                [
                    jnp.take_along_axis(
                        row, ids[:, c:c + LANES], axis=1, mode="promise_in_bounds"
                    )
                    for c in range(0, seq_len, LANES)
                ],
                axis=1,
            )
            for seq in range(rows // seq_len):
                span = slice(seq * seq_len, (seq + 1) * seq_len)
                query = jnp.where(mine, q_o[span, cols] * 0.125, 0).astype(BF)
                scores = dot_nt(query, k_o[span, cols]) + bias
                low = jnp.exp(scores - jnp.max(scores, axis=-1, keepdims=True)).astype(BF)
                soft_o[head, seq] = low
                out = dot_nn(low, jnp.where(mine, v_o[span, cols], 1.0).astype(BF))
                inverse = 1.0 / pltpu.roll(out, head_dim, 1)
                out = out * inverse
                if part == 0:
                    gathered[seq], scaled[seq] = out, inverse
                else:
                    gathered[seq] = jnp.where(mine, out, gathered[seq])
                    scaled[seq] = jnp.where(mine, inverse, scaled[seq])
        for seq in range(rows // seq_len):
            span = slice(seq * seq_len, (seq + 1) * seq_len)
            att_o[span, cols] = gathered[seq].astype(BF)
            inv_o[span, cols] = scaled[seq]
    residual_o[...] += dot_nn(att_o[...], wo[...])

    @pl.when(step == pl.num_programs(0) - 1)
    def _():
        residual = residual_o[...]
        factor = lax.rsqrt(jnp.mean(residual * residual, axis=-1, keepdims=True) + EPSILON)
        low = (residual * factor * gain_two[...][None, :]).astype(BF)
        logits = dot_nt(low, wr[...])
        weights = jnp.exp(logits - jnp.max(logits, axis=-1, keepdims=True))
        probs = weights / jnp.sum(weights, axis=-1, keepdims=True)
        hot = column(ids_row[...]) == iota(logits.shape, 1)
        gate_o[...] = jnp.sum(jnp.where(hot, probs, 0.0), axis=1, keepdims=True)
        pick = (iota((slots_o.shape[0], rows), 0) == slot_row[...]).astype(BF)
        slots_o[...] = dot_nn(pick, low).astype(BF)

        for e in range(local):
            def finish(d, carry):
                peer = (me + ranks - d) % ranks
                raw_copy(e, peer, peer).wait_recv()
                raw_copy(e, me, (me + d) % ranks).wait_send()
                return carry

            lax.fori_loop(1, ranks, finish, 0)
            raw_stay(e).wait()
            if e and early < room:
                late_keep(e).wait()


def forward(
    tokens, bucket_ids, table, gains, weights, wr, ids_row, grad, blocks, late, cap, head_dim
):
    rows, width = tokens.shape
    seq_len = bucket_ids.shape[0]
    heads = table.shape[0]
    per_group = 4
    groups = heads // per_group
    group = width // groups
    seqs = rows // seq_len
    ranks, local, room = blocks[:3]
    slots = ranks * local * room
    dma = pltpu.SemaphoreType.DMA
    cols = lambda shape: pl.BlockSpec(shape, lambda g: (0, g))
    wq, wk, wv, wo = weights
    return pl.pallas_call(
        functools.partial(forward_kernel, head_dim, seq_len, cap, late),
        grid=(groups,),
        in_specs=[
            whole((rows, width)),
            whole((seq_len, seq_len)),
            whole(table.shape),
            whole((width,)),
            whole((width,)),
            cols((width, group)),
            cols((width, group)),
            cols((width, group)),
            pl.BlockSpec((group, width), lambda g: (g, 0)),
            whole(wr.shape),
            whole((1, rows)),
            whole((rows, width)),
        ],
        out_specs=(
            whole((rows, width)),
            cols((rows, group)),
            cols((rows, group)),
            cols((rows, group)),
            cols((rows, group)),
            cols((rows, group)),
            pl.BlockSpec((per_group, seqs, seq_len, seq_len), lambda g: (g, 0, 0, 0)),
            whole((rows, width)),
            whole((rows, 1)),
            whole((rows, 1)),
            whole((slots, width)),
            pl.BlockSpec(memory_space=pl.ANY),
            pl.BlockSpec(memory_space=pl.ANY),
        ),
        scratch_shapes=[
            pltpu.VMEM((1, rows), jnp.int32),
            pltpu.VMEM(blocks, BF),
            pltpu.VMEM((heads, LANES), F32),
            dma((local, ranks)),
            dma((local, ranks)),
            dma((2 * local,)),
        ],
        out_shape=(
            jax.ShapeDtypeStruct((rows, width), BF),
            jax.ShapeDtypeStruct((rows, width), BF),
            jax.ShapeDtypeStruct((rows, width), BF),
            jax.ShapeDtypeStruct((rows, width), BF),
            jax.ShapeDtypeStruct((rows, width), BF),
            jax.ShapeDtypeStruct((rows, width), F32),
            jax.ShapeDtypeStruct((heads, seqs, seq_len, seq_len), BF),
            jax.ShapeDtypeStruct((rows, width), F32),
            jax.ShapeDtypeStruct((rows, 1), F32),
            jax.ShapeDtypeStruct((rows, 1), jnp.int32),
            jax.ShapeDtypeStruct((slots, width), BF),
            jax.ShapeDtypeStruct(blocks, BF),
            jax.ShapeDtypeStruct((local - 1, ranks, max(late, 16), width), BF),
        ),
        compiler_params=params(
            dimension_semantics=("arbitrary",), collective_id=2, has_side_effects=True
        ),
        cost_estimate=pl.CostEstimate(
            flops=2 * rows * width * (4 * width + 2 * seq_len * 4),
            bytes_accessed=40 << 20,
            transcendentals=heads * rows * seq_len,
        ),
        name="forward",
    )(tokens, bucket_ids, table, *gains, wq, wk, wv, wo, wr, ids_row, grad)


LATE_TENTHS = 8


def bits_of(size):
    return [1 << i for i in range(size.bit_length() - 1)]


def flip(index, bit):
    return index + bit * (1 - 2 * ((index // bit) % 2))


def flip_all(index, mask, bits):
    for bit in bits:
        index = jnp.where((mask // bit) % 2 == 1, flip(index, bit), index)
    return index


def experts_kernel(
    ranks, copies, late,
    x_send, raw_i, late_i, weight_in, weight_out, wr,
    returned_o, back_o, router_o, next_in_o, keep_in_o, next_out_o, keep_out_o,
    x_recv, raw, back_send, win, wout, grads_in, grads_out, got_in, got_out,
    scaled, probs_s, back_sum, result_sum, result,
    x_ss, x_rs, b_ss, b_rs, l_ss, l_rs, raw_sem, w_sem, first_ss, first_rs, result_sem, out_sem,
):
    local, cap, width = x_send.shape[1:]
    rows = ranks * cap
    chunk = win.shape[2]
    steps = copies
    bits = bits_of(copies)
    orders = (bits, bits[::-1])
    me = lax.axis_index("expert")
    copy = lax.axis_index("dp")
    mesh_id = pl.DeviceIdType.MESH

    barrier = pltpu.get_barrier_semaphore()

    def greet(d, carry):
        pl.semaphore_signal(
            barrier, inc=1, device_id={"expert": (me + d) % ranks}, device_id_type=mesh_id
        )
        return carry

    lax.fori_loop(1, ranks, greet, 0)
    for bit in bits:
        pl.semaphore_signal(
            barrier, inc=1, device_id={"dp": flip(copy, bit)}, device_id_type=mesh_id
        )

    def load(s):
        e, j = s // steps, steps - 1 - s % steps
        at = pl.multiple_of(flip_all(copy, j, bits) * chunk, chunk)
        return (
            pltpu.make_async_copy(
                weight_in.at[e, :, pl.ds(at, chunk)], win.at[s % 2], w_sem.at[0, s % 2]
            ),
            pltpu.make_async_copy(
                weight_out.at[e, pl.ds(at, chunk), :], wout.at[s % 2], w_sem.at[1, s % 2]
            ),
        )

    for one in load(0):
        one.start()
    pl.semaphore_wait(barrier, ranks - 1 + len(bits))


    early = cap - late

    def raw_load(e):
        span = pl.ds(0, early if e else cap)
        return pltpu.make_async_copy(
            raw_i.at[:, e, span], raw.at[e, :, span], raw_sem.at[e]
        )

    def row_copy(out, e, at, peer):
        if out is None:
            source = late_i.at[e - 1, peer]
            target, sends, recvs = raw.at[e, at, pl.ds(early, late)], l_ss, l_rs
        elif out:
            source, target, sends, recvs = x_send.at[peer, e], x_recv.at[e, at], x_ss, x_rs
        else:
            source, target, sends, recvs = back_send.at[e, peer], back_o.at[at, e], b_ss, b_rs
        return pltpu.make_async_remote_copy(
            src_ref=source,
            dst_ref=target,
            send_sem=sends.at[e, peer],
            recv_sem=recvs.at[e, at],
            device_id={"expert": peer},
            device_id_type=mesh_id,
        )

    def stay(out, e):
        if out is None:
            return pltpu.make_async_copy(
                late_i.at[e - 1, me], raw.at[e, me, pl.ds(early, late)], l_rs.at[e, me]
            )
        if out:
            return pltpu.make_async_copy(x_send.at[me, e], x_recv.at[e, me], x_rs.at[e, me])
        return pltpu.make_async_copy(back_send.at[e, me], back_o.at[me, e], b_rs.at[e, me])

    def send(out, e):
        def one(i, carry):
            row_copy(out, e, me, (me + nth_far(i, ranks)) % ranks).start()
            return carry

        lax.fori_loop(0, ranks - 1, one, 0)
        stay(out, e).start()

    def arrive(out, e):
        def one(d, carry):
            peer = (me + ranks - d) % ranks
            row_copy(out, e, peer, peer).wait_recv()
            return carry

        lax.fori_loop(1, ranks, one, 0)
        stay(out, e).wait()

    def leave(out, e):
        def one(d, carry):
            row_copy(out, e, me, (me + d) % ranks).wait_send()
            return carry

        lax.fori_loop(1, ranks, one, 0)

    moves = (
        (grads_in, got_in, bits[0], next_in_o, keep_in_o),
        (grads_out, got_out, bits[1], next_out_o, keep_out_o),
    )
    spare, kept = steps, steps + 1

    def first_copy(k, e, j):
        grads, got, bit = moves[k][:3]
        at = 2 if e else (0 if j == steps - 1 else 1)
        return pltpu.make_async_remote_copy(
            src_ref=grads.at[spare if e else j],
            dst_ref=got.at[at],
            send_sem=first_ss.at[k, at],
            recv_sem=first_rs.at[k, at],
            device_id={"dp": flip(copy, bit)},
            device_id_type=mesh_id,
        )

    def store(k, t):
        grads, _, _, following, keep = moves[k]
        target = keep.at[1] if t == steps - 1 else following.at[2]
        return pltpu.make_async_copy(grads.at[steps - 1], target, out_sem.at[k, 0])

    def out_copy(k, at):
        grads, _, bit, following, keep = moves[k]
        source, target = (
            (grads.at[steps - 1 - bit], following.at[0]),
            (grads.at[0], keep.at[0]),
            (grads.at[kept], following.at[1]),
        )[at]
        return pltpu.make_async_copy(source, target, out_sem.at[k, 1 + at])

    def keep_result(e):
        return pltpu.make_async_copy(result, returned_o.at[e], result_sem)

    send(True, 0)
    for e in range(local):
        raw_load(e).start()
    router_o[...] = jnp.zeros_like(router_o)

    def body(s, carry):
        e, t = s // steps, s % steps
        j = steps - 1 - t

        @pl.when(s + 1 < local * steps)
        def _():
            for one in load(s + 1):
                one.start()

        @pl.when(t == 0)
        def _():
            arrive(True, e)

            @pl.when(e == 0)
            def _():
                raw_load(0).wait()
                for other in range(1, local):
                    if late:
                        send(None, other)
                    send(True, other)

            @pl.when(e > 0)
            def _():
                raw_load(1).wait()
                if late:
                    arrive(None, e)

            logits = dot_nt(x_recv[e].reshape(rows, width), wr[...])
            weights = jnp.exp(logits - jnp.max(logits, axis=-1, keepdims=True))
            probs = weights / jnp.sum(weights, axis=-1, keepdims=True)
            probs_s[...] = probs
            hot = iota(logits.shape, 1) == me * local + e
            gate = jnp.sum(jnp.where(hot, probs, 0.0), axis=1, keepdims=True)

            scaled[...] = (gate * raw[e].reshape(rows, width).astype(F32)).astype(BF)
            back_sum[...] = jnp.zeros_like(back_sum)
            result_sum[...] = jnp.zeros_like(result_sum)

        for one in load(s):
            one.wait()

        late_at = [steps - 1 - moves[k][2] for k in range(2)]
        slots = [
            jnp.where(
                e == 0, j, jnp.where(t == 0, spare, jnp.where(j == late_at[k], kept, steps - 1))
            )
            for k in range(2)
        ]
        for k in range(2):
            bit = moves[k][2]

            @pl.when((e > 0) & (j == bit))
            def _():
                first_copy(k, 0, steps - 1).wait_send()

            @pl.when((e > 0) & (t == steps - 1))
            def _():
                store(k, 0).wait()

        own_in, own_out = win[s % 2], wout[s % 2]
        taken = x_recv[e].reshape(rows, width)
        grads = scaled[...]


        def products(part):
            span = slice(part * (chunk // 3), (part + 1) * (chunk // 3))
            return dot_nn(taken, own_in[:, span]), dot_nt(grads, own_out[span, :])

        def activate(pre, grad_hidden):
            scale = 0.7978845608028654
            square = pre * pre
            bent = jnp.tanh(pre * (scale + (scale * 0.044715) * square))
            half = 0.5 + 0.5 * bent
            slope = half + pre * (half * (1.0 - bent)) * (scale + (scale * 0.134145) * square)
            return (pre * half).astype(BF), (grad_hidden * slope).astype(BF)

        parts = []
        ahead = products(0)
        for part in range(3):
            now, ahead = ahead, products(part + 1) if part < 2 else None
            parts.append(activate(*now))
        hidden, grad_pre = [jnp.concatenate(one, axis=1) for one in zip(*parts)]
        grads_in[slots[0]] = dot_tn(taken, grad_pre).astype(BF)
        grads_out[slots[1]] = dot_tn(hidden, grads).astype(BF)

        for k in range(2):
            bit = moves[k][2]
            for at in (steps - 1, bit):
                @pl.when((e == 0) & (j == at))
                def _():
                    first_copy(k, 0, at).start()

            @pl.when((e > 0) & (t == 0))
            def _():
                first_copy(k, 1, steps - 1).start()

            @pl.when((e > 0) & (j == bit))
            def _():
                store(k, 0).start()

            @pl.when((e > 0) & (t == steps - 1))
            def _():
                store(k, steps - 1).start()

        result_sum[...] += dot_nn(hidden, own_out)
        back_sum[...] += dot_nt(grad_pre, own_in)

        @pl.when(t == steps - 1)
        def _():
            returned = result_sum[...].astype(BF)

            @pl.when(e > 0)
            def _():
                keep_result(e - 1).wait()

            result[...] = returned.reshape(result.shape)
            keep_result(e).start()
            probs = probs_s[...]
            hot = iota(probs.shape, 1) == me * local + e
            gate = jnp.sum(jnp.where(hot, probs, 0.0), axis=1, keepdims=True)

            grad_gate = jnp.sum(
                raw[e].reshape(rows, width).astype(F32) * returned.astype(F32), axis=1, keepdims=True
            )
            slope = jnp.where(hot, 1.0, 0.0) - gate
            grad_logits = (probs * slope * grad_gate).astype(BF)
            router_o[...] += dot_tn(grad_logits, x_recv[e].reshape(rows, width))
            back = (back_sum[...] + dot_nn(grad_logits, wr[...])).astype(BF)
            back_send[e] = back.reshape(ranks, cap, width)
            send(False, e)

        return carry

    lax.fori_loop(0, local * steps, body, 0)

    for at in range(2):
        for k in range(2):
            grads, got, bit = moves[k][:3]
            into = (steps - 1 - bit, 0)[at]
            first_copy(k, 0, (steps - 1, bit)[at]).wait_recv()
            grads[into] = (grads[into].astype(F32) + got[at].astype(F32)).astype(BF)
            out_copy(k, at).start()
    for e in range(local):
        arrive(False, e)
    for k in range(2):
        grads, got = moves[k][:2]
        first_copy(k, 1, steps - 1).wait_recv()
        grads[kept] = (grads[kept].astype(F32) + got[2].astype(F32)).astype(BF)
        out_copy(k, 2).start()
    for k in range(2):
        first_copy(k, 0, moves[k][2]).wait_send()
        first_copy(k, 1, steps - 1).wait_send()
        store(k, steps - 1).wait()
        for at in range(3):
            out_copy(k, at).wait()
    keep_result(local - 1).wait()
    for e in range(local):
        leave(True, e)
        leave(False, e)
        if e and late:
            leave(None, e)


def run_experts(x_send, raw, late_rows, late, weight_in, weight_out, wr, copies):
    ranks, local, cap, width = x_send.shape
    rows = ranks * cap
    hidden = weight_in.shape[2]
    chunk = hidden // copies
    experts = wr.shape[0]
    vmem = pl.BlockSpec(memory_space=pltpu.VMEM)
    hbm = pl.BlockSpec(memory_space=pl.ANY)
    block = (ranks, cap, width)
    dma = pltpu.SemaphoreType.DMA
    return pl.pallas_call(
        functools.partial(experts_kernel, ranks, copies, late),
        in_specs=[hbm, hbm, hbm, hbm, hbm, vmem],
        out_specs=(hbm, hbm, vmem) + (hbm,) * 4,
        out_shape=(
            jax.ShapeDtypeStruct((local,) + block, BF),
            jax.ShapeDtypeStruct(x_send.shape, BF),
            jax.ShapeDtypeStruct((experts, width), F32),
            jax.ShapeDtypeStruct((3, width, chunk), BF),
            jax.ShapeDtypeStruct((2, width, chunk), BF),
            jax.ShapeDtypeStruct((3, chunk, width), BF),
            jax.ShapeDtypeStruct((2, chunk, width), BF),
        ),
        scratch_shapes=[
            pltpu.VMEM((local,) + block, BF),
            pltpu.VMEM((local,) + block, BF),
            pltpu.VMEM((local,) + block, BF),
            pltpu.VMEM((2, width, chunk), BF),
            pltpu.VMEM((2, chunk, width), BF),
            pltpu.VMEM((copies + 2, width, chunk), BF),
            pltpu.VMEM((copies + 2, chunk, width), BF),
            pltpu.VMEM((3, width, chunk), BF),
            pltpu.VMEM((3, chunk, width), BF),
            pltpu.VMEM((rows, width), BF),
            pltpu.VMEM((rows, experts), F32),
            pltpu.VMEM((rows, width), F32),
            pltpu.VMEM((rows, width), F32),
            pltpu.VMEM(block, BF),
            dma((local, ranks)),
            dma((local, ranks)),
            dma((local, ranks)),
            dma((local, ranks)),
            dma((local, ranks)),
            dma((local, ranks)),
            dma((local,)),
            dma((2, 2)),
            dma((2, 3)),
            dma((2, 3)),
            dma,
            dma((2, 4)),
        ],
        compiler_params=params(collective_id=0, has_side_effects=True),
        cost_estimate=pl.CostEstimate(
            flops=12 * local * rows * width * hidden,
            bytes_accessed=8 * local * width * hidden,
            transcendentals=local * rows * hidden,
        ),
        name="experts",
    )(x_send, raw, late_rows, weight_in, weight_out, wr)


PIECES = 4


def sums_inside(width, copies, ranks):
    return ranks == 2 * copies and width % (16 * copies * copies) == 0


def backward_kernel(
    head_dim, seq_len, buckets, copies, ranks,
    tokens_i, gain_one, normed_i, ids_i, q, k, v, att_i, inv, soft, wq, wk, wv,
    back_i, slot_col_i, residual_i, grad_i, gain_two, wo_i, gate_i, router,
    returned, next_in, next_out,
    grad_tokens_o, mixed_o, pieces_o, small_o, got_in_o, got_out_o,
    back, slot_col, residual, grad, wo, att, normed, ids, gate,
    score_sums, normed_sum, low_res, grad_att, grad_gain_two, results, parts, part_got, level_got, level_sum, last_got, last_sum,
    small_s, small_all, small_core, small_line, small_plane, small_half,
    r_ss, r_rs, c_ss, c_rs, l1_ss, l1_rs, l2_ss, l2_rs, g2_ss, g2_rs, g1_ss, g1_rs, h_ss, h_rs,
    own_sem, w_ss, w_rs, m_ss, m_rs, load_sem,
):
    step = pl.program_id(0)
    steps = pl.num_programs(0)
    rows, width = residual.shape
    group = wq.shape[1]
    seqs = rows // seq_len
    local = returned.shape[0]
    bits = bits_of(copies)
    me = lax.axis_index("expert")
    copy = lax.axis_index("dp")
    core = me % 2
    line = me // 2
    mesh_id = pl.DeviceIdType.MESH
    inside = sums_inside(width, copies, ranks)
    count = copies

    def remote(source, target, sends, recvs, device):
        return pltpu.make_async_remote_copy(
            src_ref=source, dst_ref=target, send_sem=sends, recv_sem=recvs,
            device_id=device, device_id_type=mesh_id,
        )


    def result_copy(e, at, peer):
        return remote(
            returned.at[e, peer], results.at[at, e], r_ss.at[e, peer], r_rs.at[e, at],
            {"expert": peer},
        )

    def result_stay(e):
        return pltpu.make_async_copy(returned.at[e, me], results.at[me, e], r_rs.at[e, me])

    def results_start(e):
        def one(d, carry):
            result_copy(e, me, (me + d) % ranks).start()
            return carry

        lax.fori_loop(1, ranks, one, 0)
        result_stay(e).start()

    def results_wait(e):
        def one(d, carry):
            peer = (me + ranks - d) % ranks
            result_copy(e, peer, peer).wait_recv()
            result_copy(e, me, (me + d) % ranks).wait_send()
            return carry

        lax.fori_loop(1, ranks, one, 0)
        result_stay(e).wait()


    moves = (
        (next_in, got_in_o, bits[0], bits[1]),
        (next_out, got_out_o, bits[1], bits[0]),
    )
    shares = 3 * PARTS

    def share_copy(which, n, late):
        source, target, first, second = moves[which]
        at = 2 if late else (n - PARTS) // PARTS
        height = source.shape[1] // PARTS
        span = pl.ds(pl.multiple_of((n % PARTS) * height, 16), height)
        return remote(
            source.at[at, span], target.at[at, span], w_ss.at[which, n], w_rs.at[which, n],
            {"dp": flip(copy, first if late else second)},
        )

    def pump(first, count):
        def one(n, carry):
            @pl.when(n < PARTS)
            def _():
                for which in range(2):
                    share_copy(which, n, True).start()

            @pl.when(n >= PARTS)
            def _():
                for which in (1, 0):
                    share_copy(which, n, False).start()

            return carry

        if count:
            lax.fori_loop(first, jnp.minimum(first + count, shares), one, 0)

    def shares_end():
        def late(n, carry):
            for which in range(2):
                share_copy(which, n, True).wait()
            return carry

        def rest(n, carry):
            for which in range(2):
                share_copy(which, n, False).wait()
            return carry

        lax.fori_loop(0, PARTS, late, 0)
        lax.fori_loop(PARTS, shares, rest, 0)

    def paced(at):
        for p, stage in PLAN.get(at, ()):
            if p == "ret":
                results_start(stage)
            elif inside:
                if p == "small":
                    small_stages[stage]()
                else:
                    stages[stage](p)


    def levels(p):
        along = (line, lambda i: {"expert": 2 * i + core})
        across = (copy, lambda i: {"dp": i})
        return (along, across) if p in ALONG_FIRST else (across, along)

    def core_copy(p):
        return remote(
            parts.at[p, 1 - core], part_got.at[p], c_ss.at[p], c_rs.at[p], {"expert": me + 1 - 2 * core}
        )

    def first_copy(p, peer, at):
        (_, device), _ = levels(p)
        return remote(
            parts.at[p, core, pl.ds(peer * count, count)], level_got.at[p, at],
            l1_ss.at[p, peer], l1_rs.at[p, at], device(peer),
        )

    def second_copy(p, peer, at):
        _, (_, device) = levels(p)
        return remote(
            level_sum.at[p, peer], last_got.at[p, at], l2_ss.at[p, peer], l2_rs.at[p, at],
            device(peer),
        )

    def give_second(p, peer, at):
        (mine, _), (_, device) = levels(p)
        return remote(
            last_sum.at[p], pieces_o.at[p, core, mine * count + at],
            g2_ss.at[p, peer], g2_rs.at[p, at], device(peer),
        )

    def give_own(p):
        (mine, _), (own, _) = levels(p)
        return pltpu.make_async_copy(
            last_sum.at[p], pieces_o.at[p, core, mine * count + own], own_sem.at[p]
        )

    def give_first(p, peer, at):
        (_, device), _ = levels(p)
        block = pieces_o.at[p, core, pl.ds(at * count, count)]
        return remote(block, block, g1_ss.at[p, peer], g1_rs.at[p, at], device(peer))

    def give_core(p, half):
        block = pieces_o.at[p, half]
        return remote(block, block, h_ss.at[p], h_rs.at[p], {"expert": me + 1 - 2 * core})

    def others(own):
        return [(own + d) % count for d in range(1, count)]

    def piece_0(p):
        core_copy(p).start()

    def piece_1(p):
        (own, _), _ = levels(p)
        core_copy(p).wait_recv()
        parts[p, core] = (parts[p, core].astype(F32) + part_got[p].astype(F32)).astype(BF)
        for peer in others(own):
            first_copy(p, peer, own).start()

    def piece_2(p):
        (first, _), (own, _) = levels(p)
        total = parts[p, core, pl.ds(first * count, count)].astype(F32)
        for peer in others(first):
            first_copy(p, peer, peer).wait_recv()
            total += level_got[p, peer].astype(F32)
        level_sum[p] = total.astype(BF)
        for peer in others(own):
            second_copy(p, peer, own).start()

    def piece_3(p):
        _, (own, _) = levels(p)
        total = level_sum[p, own].astype(F32)
        for peer in others(own):
            second_copy(p, peer, peer).wait_recv()
            total += last_got[p, peer].astype(F32)
        last_sum[p] = total.astype(BF)
        for peer in others(own):
            give_second(p, peer, own).start()
        give_own(p).start()

    def piece_4(p):
        (first, _), (own, _) = levels(p)
        for peer in others(own):
            give_second(p, peer, peer).wait_recv()
        give_own(p).wait()
        for peer in others(first):
            give_first(p, peer, first).start()

    def piece_5(p):
        (first, _), _ = levels(p)
        for peer in others(first):
            give_first(p, peer, peer).wait_recv()
        give_core(p, core).start()

    def piece_6(p):
        (first, _), (own, _) = levels(p)
        give_core(p, 1 - core).wait_recv()
        core_copy(p).wait_send()
        give_core(p, core).wait_send()
        for peer in others(first):
            first_copy(p, peer, first).wait_send()
            give_first(p, peer, first).wait_send()
        for peer in others(own):
            second_copy(p, peer, own).wait_send()
            give_second(p, peer, own).wait_send()

    stages = (piece_0, piece_1, piece_2, piece_3, piece_4, piece_5, piece_6)


    half = small_half.shape[0]

    def small_copy(stage, peer, at):
        if stage == 0:
            source, target, device = small_s, small_core, {"expert": me + 1 - 2 * core}
        elif stage == 1:
            source, target, device = small_half, small_line.at[at], {"expert": 2 * peer + core}
        elif stage == 2:
            source, target, device = small_half, small_plane.at[at], {"dp": peer}
        else:
            source = small_all.at[pl.ds(pl.multiple_of(core * half, 8), half)]
            target, device = source, {"expert": me + 1 - 2 * core}
        return remote(source, target, m_ss.at[stage, peer], m_rs.at[stage, at], device)

    def small_0():
        small_copy(0, 0, 0).start()

    def small_1():
        small_copy(0, 0, 0).wait()
        span = pl.ds(pl.multiple_of(core * half, 8), half)
        small_half[...] = small_s[span] + small_core[span]
        for peer in others(line):
            small_copy(1, peer, line).start()

    def small_2():
        total = small_half[...]
        for peer in others(line):
            small_copy(1, peer, peer).wait_recv()
            total += small_line[peer]
        for peer in others(line):
            small_copy(1, peer, line).wait_send()
        small_half[...] = total
        for peer in others(copy):
            small_copy(2, peer, copy).start()

    def small_3():
        total = small_half[...]
        for peer in others(copy):
            small_copy(2, peer, peer).wait_recv()
            total += small_plane[peer]
        small_all[pl.ds(pl.multiple_of(core * half, 8), half)] = total
        small_copy(3, 0, 0).start()

    def small_4():
        for peer in others(copy):
            small_copy(2, peer, copy).wait_send()
        small_copy(3, 0, 0).wait()

    def load_tokens():
        return pltpu.make_async_copy(tokens_i, low_res, load_sem.at[9])

    small_stages = (small_0, small_1, small_2, small_3, small_4)

    @pl.when(step == 0)
    def _():
        barrier = pltpu.get_barrier_semaphore()

        def greet(axis, own, size):
            def one(d, carry):
                pl.semaphore_signal(
                    barrier, inc=1, device_id={axis: (own + d) % size}, device_id_type=mesh_id
                )
                return carry

            lax.fori_loop(1, size, one, 0)

        greet("expert", me, ranks)
        greet("dp", copy, copies)
        pl.semaphore_wait(barrier, ranks + copies - 2)
        pump(0, PUMP_FIRST)
        paced("start")
        loads = [
            pltpu.make_async_copy(source, target, load_sem.at[at])
            for at, (source, target) in enumerate((
                (back_i, back), (slot_col_i, slot_col), (residual_i, residual), (grad_i, grad),
                (wo_i, wo), (att_i, att), (normed_i, normed), (ids_i, ids), (gate_i, gate),
            ))
        ]
        for one in loads:
            one.start()
        for one in loads[:6]:
            one.wait()


        height = rows // 4

        def block(i, gain):
            pump(PUMP_FIRST + PUMP_MIDDLE * i, PUMP_MIDDLE)
            span = pl.ds(pl.multiple_of(i * height, height), height)
            pick = (slot_col[span, :] == iota((height, back.shape[0]), 1)).astype(BF)
            upstream = dot_nn(pick, back[...])
            values = residual[span, :]
            factor = lax.rsqrt(jnp.mean(values * values, axis=-1, keepdims=True) + EPSILON)
            weighted = upstream * gain_two[...][None, :]
            mean = jnp.mean(weighted * values, axis=-1, keepdims=True)
            grad_residual = (
                grad[span, :].astype(F32)
                + factor * weighted
                - values * (factor * factor * factor) * mean
            )
            grad_tokens_o[span, :] = grad_residual
            low = grad_residual.astype(BF)
            low_res[span, :] = low
            grad_att[span, :] = dot_nt(low, wo[...]).astype(BF)
            return gain + jnp.sum(upstream * values * factor, axis=0, keepdims=True)

        grad_gain_two[...] = lax.fori_loop(0, 4, block, jnp.zeros((1, width), F32))
        grad_wo = dot_tn(att[...], low_res[...]).astype(BF)
        for side in range(2):
            across = slice(side * (width // 2), (side + 1) * (width // 2))
            parts[PIECES - 1, side] = grad_wo[:, across].reshape(parts.shape[2:])
        for one in loads[6:]:
            one.wait()
        load_tokens().start()
        paced("middle")


    per_step = group // head_dim
    here = pl.ds(pl.multiple_of(step * group, group), group)
    lane = iota((seq_len, group), 1)
    query_sum = [None] * seqs
    key_rows = [[] for _ in range(seqs)]
    value_rows = [[] for _ in range(seqs)]
    low_grads, inners, grads_t, queries_t = [], [], [], []
    for seq in range(seqs):
        span = slice(seq * seq_len, (seq + 1) * seq_len)
        low_grads.append((grad_att[span, here].astype(F32) * inv[span, :]).astype(BF))
        inners.append(low_grads[seq].astype(F32) * att[span, here].astype(F32))
        grads_t.append(low_grads[seq].T)
        queries_t.append(q[span, :].T)
    for head in range(per_step):
        mine = (lane >= head * head_dim) & (lane < (head + 1) * head_dim)
        own = slice(head * head_dim, (head + 1) * head_dim)
        total = None
        for seq in range(seqs):
            span = slice(seq * seq_len, (seq + 1) * seq_len)
            grad_probs = dot_nt(jnp.where(mine, low_grads[seq], 0).astype(BF), v[span, :])
            row_inner = jnp.sum(jnp.where(mine, inners[seq], 0.0), axis=-1, keepdims=True)
            low_soft = soft[head, seq]
            scores = (low_soft.astype(F32) * (grad_probs - row_inner)).astype(BF)
            total = scores if seq == 0 else total + scores
            value_rows[seq].append(dot_nn(grads_t[seq][own, :], low_soft))
            key_rows[seq].append(dot_nn(queries_t[seq][own, :], scores))
            grad_query = dot_nn(scores, k[span, :])
            query_sum[seq] = grad_query if head == 0 else jnp.where(mine, grad_query, query_sum[seq])
        score_sums[step * per_step + head] = total
        if head < per_step - 1:
            pump(PUMP_FIRST + 4 * PUMP_MIDDLE + 2 * PUMP_STEP * step, PUMP_STEP)
            for after in range(width // group):
                if (after, 0) in PLAN:
                    @pl.when(step == after)
                    def _():
                        paced((after, 0))
    grads = [
        [(one * 0.125).astype(BF) for one in query_sum],
        [(jnp.concatenate(one, axis=0).T * 0.125).astype(BF) for one in key_rows],
        [jnp.concatenate(one, axis=0).T.astype(BF) for one in value_rows],
    ]
    grads = jnp.concatenate([jnp.concatenate(one, axis=0) for one in grads], axis=1)
    weights = jnp.concatenate([wq[...], wk[...], wv[...]], axis=1)
    parts[step // 2, step % 2] = dot_tn(normed[...], grads).astype(BF).reshape(parts.shape[2:])
    part = dot_nt(grads, weights)

    @pl.when(step == 0)
    def _():
        normed_sum[...] = part

    @pl.when(step > 0)
    def _():
        normed_sum[...] += part

    pump(PUMP_FIRST + 4 * PUMP_MIDDLE + 2 * PUMP_STEP * step + PUMP_STEP, PUMP_STEP)
    for after in range(width // group):
        if (after, 1) in PLAN:
            @pl.when(step == after)
            def _():
                paced((after, 1))

    @pl.when(step == steps - 1)
    def _():
        load_tokens().wait()
        upstream = normed_sum[...]
        values = low_res[...].astype(F32)
        factor = lax.rsqrt(jnp.mean(values * values, axis=-1, keepdims=True) + EPSILON)
        weighted = upstream * gain_one[...][None, :]
        mean = jnp.mean(weighted * values, axis=-1, keepdims=True)
        gain = jnp.sum(upstream * values * factor, axis=0, keepdims=True)
        grad_tokens_o[...] = (
            grad_tokens_o[...]
            + factor * weighted
            - values * (factor * factor * factor) * mean
        )
        pump(PUMP_FIRST + 4 * PUMP_MIDDLE + 2 * PUMP_STEP * (width // group), PUMP_LAST)
        paced("norm")
        heads = score_sums.shape[0]
        rows_at = 16

        def add(block, sums):
            at = pl.multiple_of(block * rows_at, rows_at)
            own = ids[pl.ds(at, rows_at), :]
            hot = own[:, None, :] == iota((rows_at, buckets, seq_len), 1)
            hot = hot.astype(BF).reshape(rows_at * buckets, seq_len)
            scores = score_sums[:, pl.ds(at, rows_at), :].reshape(heads * rows_at, seq_len)
            return sums + dot_nt(hot, scores)

        sums = jnp.zeros((rows_at * buckets, heads * rows_at), F32)
        sums = lax.fori_loop(0, seq_len // rows_at, add, sums)
        sums = sums.reshape(rows_at, buckets, heads * rows_at)
        across = iota(sums.shape, 2)
        keep = iota(sums.shape, 0) == across % rows_at
        sums = jnp.sum(jnp.where(keep, sums, 0.0), axis=0)
        into = iota((heads * rows_at, LANES), 0) // rows_at == iota((heads * rows_at, LANES), 1)
        bucket = lax.dot_general(
            sums, into.astype(F32), (((1,), (0,)), ((), ())),
            precision=lax.Precision.HIGHEST, preferred_element_type=F32,
        )
        small_s[...] = jnp.zeros_like(small_s)
        tiles = width // LANES
        experts = router.shape[0]
        for tile in range(tiles):
            cols = slice(tile * LANES, (tile + 1) * LANES)
            small_s[tile:tile + 1, :] = gain[:, cols]
            small_s[8 + tile:9 + tile, :] = grad_gain_two[:, cols]
            at = 16 + buckets + tile * experts
            small_s[at:at + experts, :] = router[:, cols]
        small_s[16:16 + buckets, :] = bucket
        pump(PUMP_FIRST + 4 * PUMP_MIDDLE + 2 * PUMP_STEP * (width // group) + PUMP_LAST, shares)
        paced("bucket")
        small_o[...] = small_all[...] if inside else small_s[...]
        for e in range(local):
            results_wait(e)

        height = rows // 4

        def mix(i, carry):
            span = pl.ds(pl.multiple_of(i * height, height), height)
            pick = (slot_col[span, :] == iota((height, back.shape[0]), 1)).astype(BF)
            combined = dot_nn(pick, results[...].reshape(back.shape))
            grad[span, :] = (residual[span, :] + gate[span, :] * combined).astype(BF)
            return carry

        lax.fori_loop(0, 4, mix, 0)
        out = pltpu.make_async_copy(grad, mixed_o, load_sem.at[0])
        out.start()
        paced("mixed")
        shares_end()
        out.wait()
        if not inside:
            for p in range(PIECES):
                out = pltpu.make_async_copy(parts.at[p], pieces_o.at[p], own_sem.at[p])
                out.start()
                out.wait()


ALONG_FIRST = (0, 1)
PARTS = 12
PUMP_FIRST, PUMP_MIDDLE, PUMP_STEP, PUMP_LAST = 2, 1, 2, 2
PLAN = {
    "start": (("ret", 1),),
    "middle": ((3, 0),),
    (0, 1): ((3, 1),),
    (1, 1): ((0, 0),),
    (2, 0): ((0, 1),),
    (3, 1): ((1, 0), (3, 2)),
    (4, 0): ((1, 1), (0, 2)),
    (4, 1): (("ret", 0),),
    (5, 0): ((0, 3), (3, 3)),
    (5, 1): ((2, 0), (1, 2), (0, 4)),
    "norm": ((2, 1), (1, 3)),
    "bucket": (
        (2, 2), ("small", 0), ("small", 1), (2, 3), (1, 4), ("small", 2), (3, 4), (0, 5),
        ("small", 3), (0, 6), ("small", 4), (2, 4),
    ),
    "mixed": ((3, 5), (1, 5), (2, 5), (3, 6), (1, 6), (2, 6)),
}


def backward(
    tokens, gain_one, normed, bucket_ids, q, k, v, att, inv, soft, weights,
    back, slot_col, residual, grad, gain_two, wo, gate, router, returned, shares,
    head_dim, buckets, copies, ranks,
):
    rows, width = tokens.shape
    seq_len = bucket_ids.shape[0]
    heads, seqs = soft.shape[:2]
    local = returned.shape[0]
    experts = router.shape[0]
    chunk = shares[0].shape[2]
    slots = back.shape[0]
    group = LANES
    steps = width // group
    per_step = heads // steps
    inside = sums_inside(width, copies, ranks)
    chips = copies * copies if inside else 1
    block = (width // chips, width // 2)
    small_rows = -(-(16 + buckets + width // LANES * experts) // 16) * 16
    cols = lambda shape: pl.BlockSpec(shape, lambda g: (0, g))
    once = lambda shape: pl.BlockSpec(
        shape, lambda g: (0,) * len(shape), pipeline_mode=pl.Buffered(1)
    )
    hbm = pl.BlockSpec(memory_space=pl.ANY)
    dma = pltpu.SemaphoreType.DMA
    each = dma((PIECES, copies))
    return pl.pallas_call(
        functools.partial(backward_kernel, head_dim, seq_len, buckets, copies, ranks),
        grid=(steps,),
        in_specs=[
            hbm,
            once((width,)),
            hbm,
            hbm,
            cols((rows, group)),
            cols((rows, group)),
            cols((rows, group)),
            hbm,
            cols((rows, group)),
            pl.BlockSpec((per_step, seqs, seq_len, seq_len), lambda g: (g, 0, 0, 0)),
            cols((width, group)),
            cols((width, group)),
            cols((width, group)),
            hbm,
            hbm,
            hbm,
            hbm,
            once((width,)),
            hbm,
            hbm,
            once((experts, width)),
        ]
        + [hbm] * 3,
        out_specs=(
            once((rows, width)),
            hbm,
            hbm,
            once((small_rows, LANES)),
            hbm,
            hbm,
        ),
        scratch_shapes=[
            pltpu.VMEM((slots, width), BF),
            pltpu.VMEM((rows, 1), jnp.int32),
            pltpu.VMEM((rows, width), F32),
            pltpu.VMEM((rows, width), BF),
            pltpu.VMEM((width, width), BF),
            pltpu.VMEM((rows, width), BF),
            pltpu.VMEM((rows, width), BF),
            pltpu.VMEM((seq_len, seq_len), jnp.int32),
            pltpu.VMEM((rows, 1), F32),
            pltpu.VMEM((heads, seq_len, seq_len), BF),
            pltpu.VMEM((rows, width), F32),
            pltpu.VMEM((rows, width), BF),
            pltpu.VMEM((rows, width), BF),
            pltpu.VMEM((1, width), F32),
            pltpu.VMEM((ranks, local) + returned.shape[2:], BF),
            pltpu.VMEM((PIECES, 2, chips) + block, BF),
            pltpu.VMEM((PIECES, chips) + block, BF),
            pltpu.VMEM((PIECES, copies, copies) + block if inside else (8, LANES), BF),
            pltpu.VMEM((PIECES, copies) + block if inside else (8, LANES), BF),
            pltpu.VMEM((PIECES, copies) + block if inside else (8, LANES), BF),
            pltpu.VMEM((PIECES,) + block, BF),
            pltpu.VMEM((small_rows, LANES), F32),
            pltpu.VMEM((small_rows, LANES), F32),
            pltpu.VMEM((small_rows, LANES), F32),
            pltpu.VMEM((copies, small_rows // 2, LANES), F32),
            pltpu.VMEM((copies, small_rows // 2, LANES), F32),
            pltpu.VMEM((small_rows // 2, LANES), F32),
            dma((local, ranks)),
            dma((local, ranks)),
            dma((PIECES,)),
            dma((PIECES,)),
            each, each, each, each, each, each, each, each,
            dma((PIECES,)),
            dma((PIECES,)),
            dma((PIECES,)),
            dma((2, 3 * PARTS)),
            dma((2, 3 * PARTS)),
            dma((4, copies)),
            dma((4, copies)),
            dma((10,)),
        ],
        out_shape=(
            jax.ShapeDtypeStruct((rows, width), F32),
            jax.ShapeDtypeStruct((rows, width), BF),
            jax.ShapeDtypeStruct((PIECES, 2, chips) + block, BF),
            jax.ShapeDtypeStruct((small_rows, LANES), F32),
            jax.ShapeDtypeStruct((3, width, chunk), BF),
            jax.ShapeDtypeStruct((3, chunk, width), BF),
        ),
        compiler_params=params(
            dimension_semantics=("arbitrary",), collective_id=1, has_side_effects=True
        ),
        cost_estimate=pl.CostEstimate(
            flops=2 * rows * width * (6 * width + 5 * seq_len * 4),
            bytes_accessed=50 << 20,
            transcendentals=0,
        ),
        name="backward",
    )(
        tokens, gain_one, normed, bucket_ids, q, k, v, att, inv, soft, *weights,
        back, slot_col, residual, grad, gain_two, wo, gate, router, returned, *shares,
    )


def finish_kernel(
    pieces, keep_in, got_in, keep_out, got_out, small, wq_o, wk_o, wv_o, wo_o, grad_in_o, grad_out_o,
    gain_one_o, gain_two_o, router_o, bucket_o,
):
    width = wo_o.shape[1]
    half = width // 2
    part = half // 3
    for step in range(width // part):
        block = pieces[step // 2, step % 2].astype(F32)
        for at, out in enumerate((wq_o, wk_o, wv_o)):
            out[:, step * part:(step + 1) * part] = block[:, at * part:(at + 1) * part]
    for side in range(2):
        wo_o[:, side * half:(side + 1) * half] = pieces[PIECES - 1, side].astype(F32)
    for keep, got, out in ((keep_in, got_in, grad_in_o), (keep_out, got_out, grad_out_o)):
        out[0] = keep[0].astype(F32) + got[0].astype(F32)
        out[1] = keep[1].astype(F32) + got[1].astype(F32) + got[2].astype(F32)

    @pl.when(pl.program_id(0) == 0)
    def _():
        heads, buckets = bucket_o.shape
        experts = router_o.shape[0]
        for tile in range(width // LANES):
            cols = slice(tile * LANES, (tile + 1) * LANES)
            gain_one_o[cols] = small[tile, :]
            gain_two_o[cols] = small[8 + tile, :]
            at = 16 + buckets + tile * experts
            router_o[:, cols] = small[at:at + experts, :]
        bucket_o[...] = small[16:16 + buckets, :].T[:heads, :]


def finish(pieces, keep_in, got_in, keep_out, got_out, small, experts, heads, buckets):
    width, chunk = keep_in.shape[1:]
    count = 2
    pieces = pieces.reshape(PIECES, 2, width, width // 2)
    part = width // count
    rows = pl.BlockSpec((part, width), lambda i: (i, 0))
    square = jax.ShapeDtypeStruct((width, width), F32)
    little = ((width,), (width,), (experts, width), (heads, buckets))
    by_in = lambda lead: pl.BlockSpec((lead, part, chunk), lambda i: (0, i, 0))
    by_out = lambda lead: pl.BlockSpec((lead, chunk // count, width), lambda i: (0, i, 0))
    return pl.pallas_call(
        finish_kernel,
        grid=(count,),
        in_specs=[
            pl.BlockSpec((PIECES, 2, part, width // 2), lambda i: (0, 0, i, 0)),
            by_in(2),
            by_in(3),
            by_out(2),
            by_out(3),
            whole(small.shape),
        ],
        out_specs=(rows, rows, rows, rows, by_in(2), by_out(2))
        + tuple(whole(shape) for shape in little),
        out_shape=(
            square,
            square,
            square,
            square,
            jax.ShapeDtypeStruct((2, width, chunk), F32),
            jax.ShapeDtypeStruct((2, chunk, width), F32),
        )
        + tuple(jax.ShapeDtypeStruct(shape, F32) for shape in little),
        compiler_params=params(dimension_semantics=("arbitrary",)),
        cost_estimate=pl.CostEstimate(flops=1 << 20, bytes_accessed=30 << 20, transcendentals=0),
        name="finish",
    )(pieces, keep_in, got_in, keep_out, got_out, small)


def per_device(
    tokens,
    expert_ids,
    bucket_ids,
    attn_gain,
    ffn_gain,
    query_weight,
    key_weight,
    value_weight,
    output_weight,
    router_weight,
    bucket_bias,
    expert_in,
    expert_out,
    grad_output,
):
    tok_rows, width = tokens.shape
    buckets, heads = bucket_bias.shape
    head_dim = width // heads
    local = expert_in.shape[0]
    ranks = lax.axis_size("expert")
    copies = lax.axis_size("dp")
    experts = local * ranks
    cap = (5 * tok_rows + 4 * experts - 1) // (4 * experts)
    room = -(-cap // 16) * 16
    slots = experts * room
    gains = (attn_gain, ffn_gain)

    blocks = (ranks, local, room, width)
    late = (room * LATE_TENTHS // 10) // 16 * 16 if room > 16 else 0
    router_rows = router_weight.T
    (
        normed, q, k, v, att, inv, soft, residual, gate, slot_col, row_slots, grad_slots, late_grads
    ) = forward(
        tokens, bucket_ids, bucket_bias.T, gains,
        (query_weight, key_weight, value_weight, output_weight),
        router_rows, expert_ids.reshape(1, tok_rows), grad_output, blocks, late, cap, head_dim,
    )
    returned, back, router, next_in, keep_in, next_out, keep_out = run_experts(
        row_slots.reshape(blocks), grad_slots, late_grads, late, expert_in, expert_out, router_rows, copies,
    )
    grad_tokens, mixed, pieces, small, got_in, got_out = backward(
        tokens, gains[0], normed, bucket_ids, q, k, v, att, inv, soft,
        (query_weight, key_weight, value_weight), back.reshape(slots, width), slot_col, residual,
        grad_output, gains[1], output_weight, gate, router, returned, (next_in, next_out),
        head_dim, buckets, copies, ranks,
    )
    if not sums_inside(width, copies, ranks):
        pieces = lax.psum(pieces.astype(F32), ("dp", "expert"))
        small = lax.psum(small, ("dp", "expert"))
    (
        grad_wq, grad_wk, grad_wv, grad_wo, grad_expert_in, grad_expert_out,
        grad_attn_gain, grad_ffn_gain, grad_router, grad_bucket,
    ) = finish(pieces, keep_in, got_in, keep_out, got_out, small, experts, heads, buckets)
    return (
        mixed,
        grad_tokens,
        grad_attn_gain,
        grad_ffn_gain,
        grad_wq,
        grad_wk,
        grad_wv,
        grad_wo,
        grad_router.T,
        grad_bucket.T,
        grad_expert_in,
        grad_expert_out,
    )


def solution(mesh):
    shared = P()
    rows = P(("dp", "expert"), None)
    expert = P("expert", None, None)
    return jax.shard_map(
        per_device,
        mesh=mesh,
        in_specs=(rows, rows) + (shared,) * 9 + (expert, expert, rows),
        out_specs=(rows, rows) + (shared,) * 8 + (P("expert", None, "dp"), P("expert", "dp", None)),
        check_vma=False,
    )
```
